32 devices in a mesh: bucket: 8 (over y, x, core), seq: 4 (over z).
Axes of the slice: x: 2, y: 2, z: 4, core: 2. Of those that a mesh axis runs over, the one named last changes fastest.
Arguments:
- tokens: bfloat16 [16384, 1152], P(('bucket', 'seq')), may hold values from -6 to 6
- segment: int32 [16384], P(('bucket', 'seq')), may hold values from 0 to 7, as said below
- keep_route: int32 [16384], P(('bucket', 'seq')), may hold values 0 or 1
- condition: bfloat16 [64, 1152], P('bucket'), may hold values from -6 to 6
- group_bucket: int32 [8], P('bucket'), may hold values from 0 to 9
- head_mask: int32 [10, 16], replicated, may hold values 0 or 1
- channel_mask: int32 [10, 36], replicated, may hold values 0 or 1
- ada_weight: bfloat16 [1152, 6912], replicated, may hold values from -0.1875 to 0.1875
- ada_bias: float32 [6912], replicated, may hold values from -1.2 to 1.2
- qkv_weight: bfloat16 [1152, 3456], replicated, may hold values from -0.1875 to 0.1875
- query_bias: float32 [1152], replicated, may hold values from -1.8 to 1.8
- value_bias: float32 [1152], replicated, may hold values from -1.8 to 1.8
- proj_weight: bfloat16 [1152, 1152], replicated, may hold values from -1.5 to 1.5
- proj_bias: float32 [1152], replicated, may hold values from -1.8 to 1.8
- inner_weight: bfloat16 [1152, 4608], replicated, may hold values from -0.1875 to 0.1875
- inner_bias: float32 [4608], replicated, may hold values from -1.8 to 1.8
- outer_weight: bfloat16 [4608, 1152], replicated, may hold values from -0.1875 to 0.1875
- outer_bias: float32 [1152], replicated, may hold values from -1.8 to 1.8
- cotangent: bfloat16 [16384, 1152], P(('bucket', 'seq')), may hold values from -6 to 6
Outputs:
- block_out: bfloat16 [16384, 1152], P(('bucket', 'seq'))
- grad_tokens: float32 [16384, 1152], P(('bucket', 'seq'))
- grad_ada_weight: float32 [1152, 6912], P(('bucket', 'seq'))
- grad_ada_bias: float32 [6912], P(('bucket', 'seq'))
- grad_qkv_weight: float32 [1152, 3456], P(('bucket', 'seq'))
- grad_query_bias: float32 [1152], P(('bucket', 'seq'))
- grad_value_bias: float32 [1152], P(('bucket', 'seq'))
- grad_proj_weight: float32 [1152, 1152], P(('bucket', 'seq'))
- grad_proj_bias: float32 [1152], P(('bucket', 'seq'))
- grad_inner_weight: float32 [1152, 4608], P(('bucket', 'seq'))
- grad_inner_bias: float32 [4608], P(('bucket', 'seq'))
- grad_outer_weight: float32 [4608, 1152], P(('bucket', 'seq'))
- grad_outer_bias: float32 [1152], P(('bucket', 'seq'))
The draws below stay inside these ranges and needn't reach their ends.
Inputs may be any that keep to these rules, and one draw needn't show every extreme that they name: `segment`: A device's rows hold, in order, an equal share of each item of its group, items of 256 or 1024 tokens; every index of seq in a group holds the same ids; ids never fall along a device's rows, id 0 starts them and id 7 (8 - 1) ends them.
All inputs are finite; a program needn't handle non-finite values. No bound on the sum of `keep_route` on one device may be relied on, other than what follows from the above.
Results may differ from the reference program's by a relative error of at most 0.019.
The reference program's roundings to bfloat16 on the way count: a program that leaves them out, or rounds other values in their place, can miss the bound.
Values may be sent and summed in bfloat16 or wider, within the bound.
No kernel may reach another device: no remote copies, remote signals or barrier semaphores. Data moves between devices by JAX's collectives and lax.ppermute only.
A program may use at most 384 MiB of HBM per device.

```python
import jax
import jax.numpy as jnp
from jax import lax

D = 1152
HEADS = 16
HEAD_DIM = 72
FF = 4608
CGROUPS = 36
TSTEPS = 10
SHORT = 256
LONG = 1024
TOK_DEV = 512
GROUP_TOK = 2048
SLOTS = 8
TOKENS = 16384
N_BUCKET = 8
N_SEQ = 4


def draw_segment(key, part):
    key = jax.random.fold_in(key, 11)
    quarter_short = SHORT // N_SEQ
    quarter_long = LONG // N_SEQ
    ratio = LONG // SHORT
    most_long = GROUP_TOK // LONG

    def one_group(subkey):
        count_key, order_key = jax.random.split(subkey)
        longs = jax.random.randint(count_key, (), 0, most_long + 1)
        items = SLOTS - (ratio - 1) * longs
        position = jnp.arange(SLOTS, dtype=jnp.int32)
        scores = jax.random.permutation(order_key, SLOTS).astype(jnp.int32) + jnp.where(position < items, 0, SLOTS)
        order = jnp.argsort(scores, stable=True)
        ranked = jnp.zeros((SLOTS,), jnp.int32).at[order].set(position)
        quarter = jnp.where(position < items, jnp.where(ranked < longs, quarter_long, quarter_short), 0)
        ends = jnp.cumsum(quarter)
        row_index = jnp.arange(TOK_DEV, dtype=jnp.int32)
        item_index = jnp.sum((ends[None, :] <= row_index[:, None]).astype(jnp.int32), 1)
        slot_index = jnp.where(item_index == items - 1, SLOTS - 1, item_index)
        return jnp.tile(slot_index, N_SEQ)
    groups = jax.vmap(one_group)(jax.random.split(key, N_BUCKET))
    return groups.reshape(TOKENS).astype(jnp.int32)


def with_ends(drawn, key, least, largest):
    index_at = [jax.random.randint(jax.random.fold_in(key, axis), (), 0, length) for axis, length in enumerate(drawn.shape)]
    widest = drawn.shape.index(max(drawn.shape))
    next_to = index_at[:widest] + [(index_at[widest] + 1) % drawn.shape[widest]] + index_at[widest + 1:]
    return drawn.at[tuple(index_at)].set(least).at[tuple(next_to)].set(largest)


def level_of(own_key, extent, cuts, low, largest):
    level, own = 1.0, jax.random.fold_in(own_key, 6)
    for dim, parts in cuts:
        draws = jnp.exp(jax.random.uniform(jax.random.fold_in(own, dim), (parts,), jnp.float32, low / len(cuts), largest / len(cuts)))
        level = level * jnp.repeat(draws, extent[dim] // parts).reshape([-1 if axis == dim else 1 for axis in range(len(extent))])
    return level


def bell_draw(stream_key, extent, scale, reach, cuts=(), held_as=jnp.bfloat16):
    gain = level_of(stream_key, extent, cuts, -0.22, 0.18) if cuts else 1.0
    values = jax.random.normal(stream_key, extent, jnp.float32) * scale * gain
    return jnp.minimum(jnp.maximum(values, -reach), reach).astype(held_as)


def setup_inputs(seed: int = 0) -> dict:
    seeds = jax.random.split(jax.random.key(seed), 20)
    return {
        "tokens": bell_draw(seeds[0], (TOKENS, D), 1.0, 6.0, ((0, 32),)),
        "segment": draw_segment(jax.random.fold_in(seeds[19], 71), 0),
        "keep_route": with_ends((jax.random.randint(seeds[2], (TOKENS,), 0, 4) < 3).astype(jnp.int32), jax.random.fold_in(seeds[2], 1), 0, 1),
        "condition": bell_draw(seeds[3], (N_BUCKET * SLOTS, D), 1.0, 6.0, ((0, 8),)),
        "group_bucket": with_ends(jax.random.randint(seeds[4], (N_BUCKET,), 0, TSTEPS), jax.random.fold_in(seeds[4], 1), 0, TSTEPS - 1).astype(jnp.int32),
        "head_mask": with_ends((jax.random.randint(seeds[5], (TSTEPS, HEADS), 0, 4) < 3).astype(jnp.int32), jax.random.fold_in(seeds[5], 1), 0, 1),
        "channel_mask": with_ends((jax.random.randint(seeds[6], (TSTEPS, CGROUPS), 0, 4) < 3).astype(jnp.int32), jax.random.fold_in(seeds[6], 1), 0, 1),
        "ada_weight": bell_draw(seeds[7], (D, 6 * D), D ** -0.5, 0.1875),
        "ada_bias": bell_draw(seeds[8], (6 * D,), 0.2, 1.2, (), jnp.float32),
        "qkv_weight": bell_draw(seeds[9], (D, 3 * D), D ** -0.5, 0.1875),
        "query_bias": bell_draw(seeds[10], (D,), 0.3, 1.8, (), jnp.float32),
        "value_bias": bell_draw(seeds[11], (D,), 0.3, 1.8, (), jnp.float32),
        "proj_weight": bell_draw(seeds[12], (D, D), (D // 64) ** -0.5, 1.5),
        "proj_bias": bell_draw(seeds[13], (D,), 0.3, 1.8, (), jnp.float32),
        "inner_weight": bell_draw(seeds[14], (D, FF), D ** -0.5, 0.1875),
        "inner_bias": bell_draw(seeds[15], (FF,), 0.3, 1.8, (), jnp.float32),
        "outer_weight": bell_draw(seeds[16], (FF, D), (FF // 4) ** -0.5, 0.1875),
        "outer_bias": bell_draw(seeds[17], (D,), 0.3, 1.8, (), jnp.float32),
        "cotangent": bell_draw(seeds[18], (TOKENS, D), 1.0, 6.0, ((0, 32),)),
    }


EPSILON = 1e-06
NEGATIVE = -1000000000.0

@jax.custom_vjp
def low(v):
    return lax.optimization_barrier(v.astype(jnp.bfloat16)).astype(jnp.float32)

@jax.custom_vjp
def low_back(v):
    return v

def low_keep(v):
    return (low(v), None)

def low_pass(kept, grad):
    return (grad,)

def back_keep(v):
    return (v, None)

def back_low(kept, grad):
    return (low(grad),)
low.defvjp(low_keep, low_pass)
low_back.defvjp(back_keep, back_low)

def matmul(left, right):
    return jnp.dot(left, right, precision=lax.Precision.HIGHEST)

def norm_modulate(value, shift, scale):
    center = value - lax.optimization_barrier(jnp.mean(value, -1, keepdims=True))
    spread = lax.optimization_barrier(jnp.mean(center * center, -1, keepdims=True))
    return center * lax.rsqrt(spread + EPSILON) * (1.0 + scale) + shift

def split_heads(array):
    return array.reshape(GROUP_TOK, HEADS, HEAD_DIM).transpose(1, 0, 2)

def group_forward(params, group):
    ada_weight, ada_bias, qkv_weight, query_bias, value_bias, proj_weight, proj_bias, inner_weight, inner_bias, outer_weight, outer_bias = params
    inputs, segment, keep_route, condition, head_cols, channel_keep = group
    cond_act = low(jax.nn.silu(condition))
    modulation = matmul(cond_act, ada_weight) + ada_bias
    onehot = (segment[:, None] == jnp.arange(SLOTS)[None, :]).astype(jnp.float32)
    token_mod = matmul(onehot, modulation)
    shift_one, scale_one, gate_one, shift_two, scale_two, gate_two = jnp.split(token_mod, 6, axis=1)
    normed_one = low(norm_modulate(inputs, shift_one, scale_one))
    projected = matmul(normed_one, qkv_weight)
    queries = low(low_back(projected[:, :D] + query_bias))
    key_rows = low(low_back(projected[:, D:2 * D]))
    value_rows = low(low_back(projected[:, 2 * D:] + value_bias))
    same_item = segment[:, None] == segment[None, :]

    def head_attend(pieces):
        query_head, key_head, value_head = pieces
        scores = low_back(jnp.where(same_item, matmul(query_head, key_head.T) * HEAD_DIM ** (-0.5), NEGATIVE))
        row_top = lax.optimization_barrier(jnp.max(scores, -1, keepdims=True))
        exponent = jnp.exp(scores - row_top)
        attention = exponent / lax.optimization_barrier(jnp.sum(exponent, -1, keepdims=True))
        return matmul(low(attention), value_head)
    head_out = lax.map(jax.checkpoint(head_attend), (split_heads(queries), split_heads(key_rows), split_heads(value_rows)))
    attended = low(low_back(head_out.transpose(1, 0, 2).reshape(GROUP_TOK, D) * head_cols))
    branch_one = low_back(matmul(attended, proj_weight) + proj_bias)
    middle = inputs + gate_one * branch_one
    normed_two = low(norm_modulate(middle, shift_two, scale_two))
    before = low_back(matmul(normed_two, inner_weight) + inner_bias)
    activated = low(jax.nn.gelu(before, approximate=True) * channel_keep)
    branch_two = low_back(matmul(activated, outer_weight) + outer_bias)
    return middle + keep_route[:, None] * gate_two * branch_two

def reference(tokens, segment, keep_route, condition, group_bucket, head_mask, channel_mask, ada_weight, ada_bias, qkv_weight, query_bias, value_bias, proj_weight, proj_bias, inner_weight, inner_bias, outer_weight, outer_bias, cotangent):
    params = tuple((weight.astype(jnp.float32) for weight in (ada_weight, ada_bias, qkv_weight, query_bias, value_bias, proj_weight, proj_bias, inner_weight, inner_bias, outer_weight, outer_bias)))
    inputs = tokens.astype(jnp.float32).reshape(N_BUCKET, GROUP_TOK, D)
    segments = segment.astype(jnp.int32).reshape(N_BUCKET, GROUP_TOK)
    routes = keep_route.astype(jnp.float32).reshape(N_BUCKET, GROUP_TOK)
    conditions = condition.astype(jnp.float32).reshape(N_BUCKET, SLOTS, D)
    bucket_pick = (group_bucket[:, None] == jnp.arange(TSTEPS)[None, :]).astype(jnp.float32)
    head_cols = jnp.repeat(matmul(bucket_pick, head_mask.astype(jnp.float32)), HEAD_DIM, axis=1)
    channel_keep = jnp.repeat(matmul(bucket_pick, channel_mask.astype(jnp.float32)), FF // CGROUPS, axis=1)

    def forward(weights, block_in):

        def advance(running, group):
            return (running, jax.checkpoint(group_forward)(weights, group))
        running, outputs = lax.scan(advance, jnp.zeros((), jnp.float32), (block_in, segments, routes, conditions, head_cols, channel_keep))
        return outputs
    outputs, pullback = jax.vjp(forward, params, inputs)
    grad_params, grad_inputs = pullback(cotangent.astype(jnp.float32).reshape(N_BUCKET, GROUP_TOK, D))
    return (outputs.reshape(TOKENS, D).astype(jnp.bfloat16), grad_inputs.reshape(TOKENS, D), grad_params[0], grad_params[1], grad_params[2], grad_params[3], grad_params[4], grad_params[5], grad_params[6], grad_params[7], grad_params[8], grad_params[9], grad_params[10])
```

```python
import functools

import jax
import jax.numpy as jnp
from jax import lax
from jax.experimental import pallas as pl
from jax.experimental.pallas import tpu as pltpu
from jax.sharding import PartitionSpec as P

EPSILON = 1e-06
LOG2E = 1.4426950408889634
LANES = 128
GELU_A = 0.7978845608028654
GELU_B = 0.044715
F32 = jnp.float32
BF16 = jnp.bfloat16


def contract(left, right, left_dim, right_dim, out=F32):
    return lax.dot_general(
        left, right, (((left_dim,), (right_dim,)), ((), ())), preferred_element_type=out
    )


def swap(array, axis, bit):
    size = lax.axis_size(axis)
    return lax.ppermute(array, axis, [(i, i ^ bit) for i in range(size)])


def pick_kernel(which_ref, index_ref, own_ref, other_ref, out_ref):
    step = pl.program_id(0)

    @pl.when(which_ref[step] == 0)
    def _():
        out_ref[...] = own_ref[...].astype(out_ref.dtype)

    @pl.when(which_ref[step] != 0)
    def _():
        out_ref[...] = other_ref[...].astype(out_ref.dtype)


def pick_blocks(own, other, which, index, out_dtype):
    _, rows, width = own.shape
    count = index.shape[0]
    return pl.pallas_call(
        pick_kernel,
        grid_spec=pltpu.PrefetchScalarGridSpec(
            num_scalar_prefetch=2,
            grid=(count,),
            in_specs=[
                pl.BlockSpec(
                    (1, rows, width), lambda i, w, x: (jnp.where(w[i] == 0, x[i], 0), 0, 0)
                ),
                pl.BlockSpec(
                    (1, rows, width), lambda i, w, x: (jnp.where(w[i] == 0, 0, x[i]), 0, 0)
                ),
            ],
            out_specs=pl.BlockSpec((1, rows, width), lambda i, w, x: (i, 0, 0)),
        ),
        out_shape=jax.ShapeDtypeStruct((count, rows, width), out_dtype),
        cost_estimate=pl.CostEstimate(
            flops=0, bytes_accessed=count * rows * width * 8, transcendentals=0
        ),
        name="pick_blocks",
    )(which, index, own, other)


def head_columns(ref, start, head_width):
    part = ref[:, start : start + head_width]
    return jnp.concatenate(
        [part, jnp.zeros((part.shape[0], LANES - head_width), part.dtype)], axis=1
    )


def attend_kernel(
    heads, head_width, blocks, long_ref, keep_ref, q_ref, own_ref, other_ref, out_ref, lse_ref,
    qh, kh, vh, oh,
):
    rows, width = q_ref.shape
    block = rows // blocks
    factor = head_width**-0.5 * LOG2E
    is_long = long_ref[0] == 1
    for h in range(heads):
        start = h * head_width
        qh[h] = head_columns(q_ref, start, head_width)
        kh[h, :rows] = head_columns(own_ref, start, head_width)
        vh[h, :rows] = head_columns(own_ref, width + start, head_width)

    @pl.when(is_long)
    def _():
        for h in range(heads):
            start = h * head_width
            kh[h, rows:] = head_columns(other_ref, start, head_width)
            vh[h, rows:] = head_columns(other_ref, width + start, head_width)

    def one(h, first, count, key_first, key_count):
        queries = qh[h, pl.ds(first, count), :]
        keys = kh[h, pl.ds(key_first, key_count), :]
        values = vh[h, pl.ds(key_first, key_count), :]
        scores = contract(keys, queries, 1, 1)
        top = jnp.max(scores, 0, keepdims=True)
        exponent = jnp.exp2((scores - top) * factor)
        total = jnp.sum(exponent, 0, keepdims=True)
        mixed = contract(values, exponent.astype(BF16), 0, 0) * (1.0 / total)
        oh[h, pl.ds(first, count), :] = mixed.T.astype(BF16)
        lse_ref[h, :, pl.ds(first, count)] = top * factor + jnp.log2(total)

    def loop(index, first, count, key_first, key_count):
        def body(h, carry):
            keep = keep_ref[index * heads + h] == 1

            @pl.when(keep)
            def _():
                one(h, first, count, key_first, key_count)

            @pl.when(jnp.logical_not(keep))
            def _():
                oh[h, pl.ds(first, count), :] = jnp.zeros((count, LANES), BF16)

            return carry

        lax.fori_loop(0, heads, body, 0)

    @pl.when(is_long)
    def _():
        loop(0, 0, rows, 0, 2 * rows)

    @pl.when(jnp.logical_not(is_long))
    def _():
        for index in range(blocks):
            loop(index, index * block, block, index * block, block)

    for h in range(heads):
        out_ref[:, h * head_width : (h + 1) * head_width] = oh[h, :, :head_width]


def attend(queries, own, other, long_flag, keep, blocks):
    rows, width = queries.shape
    heads = keep.shape[0] // blocks
    head_width = width // heads
    vmem = pl.BlockSpec(memory_space=pltpu.VMEM)
    smem = pl.BlockSpec(memory_space=pltpu.SMEM)
    return pl.pallas_call(
        functools.partial(attend_kernel, heads, head_width, blocks),
        in_specs=[smem, smem, vmem, vmem, vmem],
        out_specs=[vmem, vmem],
        out_shape=[
            jax.ShapeDtypeStruct((rows, width), BF16),
            jax.ShapeDtypeStruct((heads, 1, rows), F32),
        ],
        scratch_shapes=[
            pltpu.VMEM((heads, rows, LANES), BF16),
            pltpu.VMEM((heads, 2 * rows, LANES), BF16),
            pltpu.VMEM((heads, 2 * rows, LANES), BF16),
            pltpu.VMEM((heads, rows, LANES), BF16),
        ],
        compiler_params=pltpu.CompilerParams(vmem_limit_bytes=56 * 1024 * 1024),
        cost_estimate=pl.CostEstimate(
            flops=8 * rows * rows * width,
            bytes_accessed=12 * rows * width,
            transcendentals=2 * rows * rows * heads,
        ),
        name="attend",
    )(long_flag, keep, queries, own, other)


def attend_back_kernel(
    heads, head_width, blocks, long_ref, keep_ref, q_ref, own_ref, other_ref, go_ref, lse_ref,
    delta_ref, gq_ref, gown_ref, gother_ref, qh, kh, vh, gh, gqh, gkh, gvh,
):
    rows, width = q_ref.shape
    block = rows // blocks
    scale = head_width**-0.5
    factor = scale * LOG2E
    is_long = long_ref[0] == 1
    for h in range(heads):
        start = h * head_width
        qh[h] = head_columns(q_ref, start, head_width)
        gh[h] = head_columns(go_ref, start, head_width)
        kh[h, :rows] = head_columns(own_ref, start, head_width)
        vh[h, :rows] = head_columns(own_ref, width + start, head_width)

    @pl.when(is_long)
    def _():
        for h in range(heads):
            start = h * head_width
            kh[h, rows:] = head_columns(other_ref, start, head_width)
            vh[h, rows:] = head_columns(other_ref, width + start, head_width)

    def one(h, first, count, key_first, key_count):
        queries = qh[h, pl.ds(first, count), :]
        grads = gh[h, pl.ds(first, count), :]
        keys = kh[h, pl.ds(key_first, key_count), :]
        values = vh[h, pl.ds(key_first, key_count), :]
        scores = contract(keys, queries, 1, 1)
        probs = jnp.exp2(scores * factor - lse_ref[h, :, pl.ds(first, count)])
        gvh[h, pl.ds(key_first, key_count), :] = contract(
            probs.astype(BF16), grads, 1, 0
        ).astype(BF16)
        grad_probs = contract(values, grads, 1, 1)
        grad_scores = (probs * (grad_probs - delta_ref[h, :, pl.ds(first, count)])).astype(BF16)
        gkh[h, pl.ds(key_first, key_count), :] = (
            contract(grad_scores, queries, 1, 0) * scale
        ).astype(BF16)
        gqh[h, pl.ds(first, count), :] = (
            (contract(keys, grad_scores, 0, 0) * scale).T
        ).astype(BF16)

    def loop(index, first, count, key_first, key_count):
        def body(h, carry):
            keep = keep_ref[index * heads + h] == 1

            @pl.when(keep)
            def _():
                one(h, first, count, key_first, key_count)

            @pl.when(jnp.logical_not(keep))
            def _():
                gqh[h, pl.ds(first, count), :] = jnp.zeros((count, LANES), BF16)
                gkh[h, pl.ds(key_first, key_count), :] = jnp.zeros((key_count, LANES), BF16)
                gvh[h, pl.ds(key_first, key_count), :] = jnp.zeros((key_count, LANES), BF16)

            return carry

        lax.fori_loop(0, heads, body, 0)

    @pl.when(is_long)
    def _():
        loop(0, 0, rows, 0, 2 * rows)
        for h in range(heads):
            start = h * head_width
            gother_ref[:, start : start + head_width] = gkh[h, rows:, :head_width]
            gother_ref[:, width + start : width + start + head_width] = gvh[h, rows:, :head_width]

    @pl.when(jnp.logical_not(is_long))
    def _():
        for index in range(blocks):
            loop(index, index * block, block, index * block, block)
        gother_ref[...] = jnp.zeros_like(gother_ref)

    for h in range(heads):
        start = h * head_width
        gq_ref[:, start : start + head_width] = gqh[h, :, :head_width]
        gown_ref[:, start : start + head_width] = gkh[h, :rows, :head_width]
        gown_ref[:, width + start : width + start + head_width] = gvh[h, :rows, :head_width]


def attend_back(queries, own, other, grad_out, lse, delta, long_flag, keep, blocks):
    rows, width = queries.shape
    heads = keep.shape[0] // blocks
    head_width = width // heads
    vmem = pl.BlockSpec(memory_space=pltpu.VMEM)
    smem = pl.BlockSpec(memory_space=pltpu.SMEM)
    return pl.pallas_call(
        functools.partial(attend_back_kernel, heads, head_width, blocks),
        in_specs=[smem, smem] + [vmem] * 6,
        out_specs=[vmem] * 3,
        out_shape=[
            jax.ShapeDtypeStruct((rows, width), BF16),
            jax.ShapeDtypeStruct((rows, 2 * width), BF16),
            jax.ShapeDtypeStruct((rows, 2 * width), BF16),
        ],
        scratch_shapes=[
            pltpu.VMEM((heads, rows, LANES), BF16),
            pltpu.VMEM((heads, 2 * rows, LANES), BF16),
            pltpu.VMEM((heads, 2 * rows, LANES), BF16),
            pltpu.VMEM((heads, rows, LANES), BF16),
            pltpu.VMEM((heads, rows, LANES), BF16),
            pltpu.VMEM((heads, 2 * rows, LANES), BF16),
            pltpu.VMEM((heads, 2 * rows, LANES), BF16),
        ],
        compiler_params=pltpu.CompilerParams(vmem_limit_bytes=60 * 1024 * 1024),
        cost_estimate=pl.CostEstimate(
            flops=20 * rows * rows * width,
            bytes_accessed=24 * rows * width,
            transcendentals=2 * rows * rows * heads,
        ),
        name="attend_back",
    )(long_flag, keep, queries, own, other, grad_out, lse, delta)


def feed_kernel(
    blocks, sub, share, core_ref, x_ref, g_ref, xk_ref, xs_ref, keep_ref, bias_ref, wi_ref,
    wo_ref, out_ref, gx_ref, wok_ref, wos_ref, wik_ref, wis_ref, gbias_ref, act, gbefore,
):
    rows, _ = x_ref.shape
    block = rows // blocks
    chunk = wi_ref.shape[1]
    core = core_ref[0]
    first = pl.program_id(0) == 0
    for lo in range(0, chunk, sub):
        cols = slice(lo, lo + sub)
        column_sum = jnp.zeros((1, sub), F32)
        for index in range(blocks):
            part = slice(index * block, (index + 1) * block)
            before = contract(x_ref[part], wi_ref[:, cols], 1, 0) + bias_ref[:, cols]
            grad_act = contract(g_ref[part], wo_ref[cols, :], 1, 1)
            keep = keep_ref[index : index + 1, cols]
            square = before * before
            bend = jnp.tanh(GELU_A * before * (1.0 + GELU_B * square))
            half = 0.5 * (1.0 + bend)
            slope = half + (0.5 * GELU_A) * before * (1.0 - bend * bend) * (
                1.0 + (3.0 * GELU_B) * square
            )
            act[part, cols] = (before * half * keep).astype(BF16)
            grad = (grad_act * keep * slope).astype(BF16)
            gbefore[part, cols] = grad
            column_sum += jnp.sum(grad.astype(F32), 0, keepdims=True)
        gbias_ref[:, cols] = column_sum
    out = contract(act[...], wo_ref[...], 1, 0)
    gx = contract(gbefore[...], wi_ref[...], 1, 1)

    @pl.when(first)
    def _():
        out_ref[...] = out
        gx_ref[...] = gx

    @pl.when(jnp.logical_not(first))
    def _():
        out_ref[...] += out
        gx_ref[...] += gx

    wik_ref[...] = contract(xk_ref[...], gbefore[...], 1, 0).astype(BF16)
    wis_ref[...] = contract(xs_ref[...], gbefore[...], 1, 0).astype(BF16)
    grad_wo = contract(act[...], g_ref[...], 0, 0).astype(BF16)
    for pair in range(chunk // (2 * share)):
        even = grad_wo[2 * pair * share : (2 * pair + 1) * share]
        odd = grad_wo[(2 * pair + 1) * share : (2 * pair + 2) * share]

        @pl.when(core == 0)
        def _():
            wok_ref[pair] = even
            wos_ref[pair] = odd

        @pl.when(core != 0)
        def _():
            wok_ref[pair] = odd
            wos_ref[pair] = even


def feed(core, x, grad, x_keep, x_send, keep, bias, wi, wo, blocks, share, chunk, sub):
    rows, width = x.shape
    hidden = wi.shape[1]
    half = x_keep.shape[0]
    pairs = chunk // (2 * share)
    once = pl.Buffered(1)
    whole = lambda shape: pl.BlockSpec(shape, lambda i: (0, 0), pipeline_mode=once)
    return pl.pallas_call(
        functools.partial(feed_kernel, blocks, sub, share),
        grid=(hidden // chunk,),
        in_specs=[
            pl.BlockSpec(memory_space=pltpu.SMEM),
            whole((rows, width)),
            whole((rows, width)),
            whole((half, rows)),
            whole((half, rows)),
            pl.BlockSpec((blocks, chunk), lambda i: (0, i)),
            pl.BlockSpec((1, chunk), lambda i: (0, i)),
            pl.BlockSpec((width, chunk), lambda i: (0, i)),
            pl.BlockSpec((chunk, width), lambda i: (i, 0)),
        ],
        out_specs=[
            pl.BlockSpec((rows, width), lambda i: (0, 0)),
            pl.BlockSpec((rows, width), lambda i: (0, 0)),
            pl.BlockSpec((pairs, share, width), lambda i: (i, 0, 0)),
            pl.BlockSpec((pairs, share, width), lambda i: (i, 0, 0)),
            pl.BlockSpec((half, chunk), lambda i: (0, i)),
            pl.BlockSpec((half, chunk), lambda i: (0, i)),
            pl.BlockSpec((1, chunk), lambda i: (0, i)),
        ],
        out_shape=[
            jax.ShapeDtypeStruct((rows, width), F32),
            jax.ShapeDtypeStruct((rows, width), F32),
            jax.ShapeDtypeStruct((hidden // (2 * share), share, width), BF16),
            jax.ShapeDtypeStruct((hidden // (2 * share), share, width), BF16),
            jax.ShapeDtypeStruct((half, hidden), BF16),
            jax.ShapeDtypeStruct((half, hidden), BF16),
            jax.ShapeDtypeStruct((1, hidden), F32),
        ],
        scratch_shapes=[pltpu.VMEM((rows, chunk), BF16), pltpu.VMEM((rows, chunk), BF16)],
        compiler_params=pltpu.CompilerParams(vmem_limit_bytes=62 * 1024 * 1024),
        cost_estimate=pl.CostEstimate(
            flops=12 * rows * width * hidden,
            bytes_accessed=8 * width * hidden,
            transcendentals=rows * hidden,
        ),
        name="feed",
    )(core, x, grad, x_keep, x_send, keep, bias, wi, wo)


def norm_parts(value):
    center = value - jnp.mean(value, -1, keepdims=True)
    spread = jnp.mean(center * center, -1, keepdims=True)
    inverse = lax.rsqrt(spread + EPSILON)
    return center * inverse, inverse


def norm_back(grad, normed, inverse, scale):
    scaled = grad * (1.0 + scale)
    mean_one = jnp.mean(scaled, -1, keepdims=True)
    mean_two = jnp.mean(scaled * normed, -1, keepdims=True)
    return inverse * (scaled - mean_one - normed * mean_two)


def add_low(left, right):
    return (left.astype(F32) + right.astype(F32)).astype(BF16)


def split_bit(array, dim, bit):
    keep = lax.dynamic_index_in_dim(array, bit, dim, keepdims=False)
    send = lax.dynamic_index_in_dim(array, 1 - bit, dim, keepdims=False)
    return keep, send


def reduce_rows(keep, send, bucket, seq):
    pairs, rows, columns = keep.shape
    seq_count = lax.axis_size("seq")
    current = add_low(keep, swap(send, "bucket", 1))
    bits = []
    while (1 << len(bits)) < pairs:
        bits.append(len(bits))
    count = len(bits)
    half = rows // 2
    halves = []
    for part in range(2):
        piece = current[:, part * half : (part + 1) * half]
        piece = piece.reshape((2,) * count + (half, columns))
        order = bits if part == 0 else bits[::-1]
        left = list(reversed(bits))
        for bit in order:
            dim = left.index(bit)
            mine, theirs = split_bit(piece, dim, (bucket >> (bit + 1)) & 1)
            left.remove(bit)
            piece = add_low(mine, swap(theirs, "bucket", 2 << bit))
        halves.append(piece)
    zbits = []
    while (1 << len(zbits)) < seq_count:
        zbits.append(len(zbits))
    piece = jnp.stack(halves).reshape((2,) * len(zbits) + (rows // seq_count, columns))
    left = list(reversed(zbits))
    for bit in zbits:
        mine, theirs = split_bit(piece, left.index(bit), (seq >> bit) & 1)
        left.remove(bit)
        got = swap(theirs, "seq", 1 << bit)
        if left:
            piece = add_low(mine, got)
        else:
            piece = mine.astype(F32) + got.astype(F32)
    return piece


def gather_all(array):
    bit = 1
    while bit < lax.axis_size("bucket"):
        array = jnp.concatenate([array, swap(array, "bucket", bit)], 0)
        bit *= 2
    parts = [array] + [swap(array, "seq", k) for k in range(1, lax.axis_size("seq"))]
    return jnp.concatenate(parts, 0)


def on_device(
    tokens,
    segment,
    keep_route,
    condition,
    group_bucket,
    head_mask,
    channel_mask,
    ada_weight,
    ada_bias,
    qkv_weight,
    query_bias,
    value_bias,
    proj_weight,
    proj_bias,
    inner_weight,
    inner_bias,
    outer_weight,
    outer_bias,
    cotangent,
):
    rows, width = tokens.shape
    slots = condition.shape[0]
    heads = head_mask.shape[1]
    head_width = width // heads
    hidden = inner_weight.shape[1]
    channel_groups = channel_mask.shape[1]
    group_count = lax.axis_size("bucket")
    seq_count = lax.axis_size("seq")
    bucket = lax.axis_index("bucket")
    seq = lax.axis_index("seq")
    core = bucket % 2
    piece = rows // slots
    block = piece * seq_count
    blocks = rows // block
    chip_blocks = 2 * blocks

    def pair(own, other):
        first = jnp.where(core == 0, own, other)
        second = jnp.where(core == 0, other, own)
        return jnp.stack([first, second])

    bucket_pick = (jnp.arange(head_mask.shape[0]) == group_bucket[0]).astype(F32)
    own_heads = jnp.sum(bucket_pick[:, None] * head_mask.astype(F32), 0)
    own_channels = jnp.sum(bucket_pick[:, None] * channel_mask.astype(F32), 0)
    ids_own = segment.reshape(slots, piece)[:, 0].astype(F32)
    small = jnp.concatenate([ids_own, own_heads, own_channels, keep_route.astype(F32)])
    small_pair = pair(small, swap(small, "bucket", 1))
    tokens_own = tokens.reshape(slots, piece, width)
    tokens_other = swap(tokens_own, "bucket", 1)
    cond_pair = pair(condition, swap(condition, "bucket", 1))
    grads_own = cotangent.reshape(slots, piece, width)
    grads_other = swap(grads_own, "bucket", 1)
    at = slots
    ids_pair = small_pair[:, :at]
    heads_pair = small_pair[:, at : at + heads]
    at += heads
    channels_pair = small_pair[:, at : at + channel_groups]
    at += channel_groups
    route_pair = small_pair[:, at:]

    total = 2 * slots
    same = ids_pair[:, :, None] == ids_pair[:, None, :]
    long = (jnp.sum(same.astype(jnp.int32), 2) > 1).reshape(total)
    numbers = jnp.arange(total)
    key = jnp.where(long, 0, total) + numbers
    rank = jnp.sum((key[None, :] < key[:, None]).astype(jnp.int32), 1)
    order = jnp.sum(jnp.where(rank[None, :] == numbers[:, None], numbers[None, :], 0), 1)
    ordered = order.reshape(seq_count, 2, blocks)
    core_order = lax.dynamic_index_in_dim(ordered, core, 1, keepdims=False)
    turns = jnp.arange(seq_count) ^ seq
    send_pick = core_order[turns].reshape(-1)
    send_which = (send_pick // slots != core).astype(jnp.int32)
    send_index = send_pick % slots
    mine = core_order[seq]
    mine_hot = (mine[:, None] == numbers[None, :]).astype(F32)
    long_flag = jnp.sum(mine_hot[0] * long.astype(F32)).astype(jnp.int32).reshape(1)
    group_hot = (mine[:, None] // slots == jnp.arange(2)[None, :]).astype(F32)
    own_ranks = lax.dynamic_slice_in_dim(rank, core * slots, slots, 0)
    back_which = ((own_ranks % chip_blocks) // blocks != core).astype(jnp.int32)
    back_index = ((own_ranks // chip_blocks) ^ seq) * blocks + own_ranks % blocks

    def bring(own, other):
        sent = pick_blocks(own, other, send_which, send_index, own.dtype)
        sent = sent.reshape(seq_count, blocks, 1, piece, width)
        parts = [sent[0]] + [swap(sent[k], "seq", k) for k in range(1, seq_count)]
        return jnp.concatenate(parts, 1).reshape(blocks, block, width)

    def take_back(array, out_dtype):
        array = array.reshape(blocks, seq_count, piece, width)
        parts = [array[:, 0]] + [swap(array[:, k], "seq", k) for k in range(1, seq_count)]
        own = jnp.stack(parts).reshape(seq_count * blocks, piece, width)
        other = swap(own, "bucket", 1)
        return pick_blocks(own, other, back_which, back_index, out_dtype).reshape(rows, width)

    x = bring(tokens_own, tokens_other).astype(F32)
    upstream = bring(grads_own, grads_other).astype(F32)
    route_all = jnp.stack([route_pair] + [swap(route_pair, "seq", k) for k in range(1, seq_count)])
    route_all = route_all.reshape(seq_count, total, piece)
    route = jnp.sum(mine_hot[:, None, :, None] * route_all[None], 2).reshape(blocks, block, 1)
    keep_heads = jnp.sum(group_hot[:, :, None] * heads_pair[None], 1)
    keep_channels = jnp.sum(group_hot[:, :, None] * channels_pair[None], 1)
    head_ints = keep_heads.astype(jnp.int32).reshape(-1)
    channel_cols = jnp.repeat(keep_channels, hidden // channel_groups, axis=1)
    head_cols = jnp.repeat(keep_heads, head_width, axis=1)[:, None, :]

    block_ids = jnp.sum(mine_hot * ids_pair.reshape(1, total), 1)
    block_groups = jnp.sum(group_hot * jnp.arange(2, dtype=F32)[None, :], 1)
    slot_hot = (
        (block_groups * slots + block_ids)[:, None] == jnp.arange(total, dtype=F32)[None, :]
    ).astype(F32)
    block_cond = jnp.sum(slot_hot[:, :, None] * cond_pair.reshape(1, total, width).astype(F32), 1)
    cond_act = jax.nn.silu(block_cond).astype(BF16)
    modulation = jnp.dot(cond_act, ada_weight, preferred_element_type=F32) + ada_bias
    shift_one, scale_one, gate_one, shift_two, scale_two, gate_two = (
        m[:, None, :] for m in jnp.split(modulation, 6, axis=1)
    )
    cond_all = gather_all(cond_act)

    def flat(array):
        return array.reshape(rows, width)

    def cube(array):
        return array.reshape(blocks, block, width)

    def row_shares(array):
        turned = array.T.reshape(group_count // 2, 2, width // group_count, rows)
        keep, send = split_bit(turned, 1, core)
        return keep.reshape(width // 2, rows), send.reshape(width // 2, rows)

    normed_x, inverse_x = norm_parts(x)
    normed_one = flat((normed_x * (1.0 + scale_one) + shift_one).astype(BF16))
    pair_bias = jnp.concatenate([jnp.zeros_like(value_bias), value_bias])
    own_kv = (
        jnp.dot(normed_one, qkv_weight[:, width:], preferred_element_type=F32) + pair_bias
    ).astype(BF16)
    other_kv = swap(own_kv, "bucket", 1)
    queries = (
        jnp.dot(normed_one, qkv_weight[:, :width], preferred_element_type=F32) + query_bias
    ).astype(BF16)
    attended, lse = attend(queries, own_kv, other_kv, long_flag, head_ints, blocks)
    branch_one = cube(jnp.dot(attended, proj_weight, preferred_element_type=F32) + proj_bias)
    middle = x + gate_one * branch_one

    normed_mid, inverse_mid = norm_parts(middle)
    normed_two = flat((normed_mid * (1.0 + scale_two) + shift_two).astype(BF16))
    grad_branch_two = flat((route * gate_two * upstream).astype(BF16))
    two_keep, two_send = row_shares(normed_two)
    core_ref = core.astype(jnp.int32).reshape(1)
    share = hidden // group_count
    branch_two, grad_two, wo_keep, wo_send, wi_keep, wi_send, grad_inner_bias = feed(
        core_ref,
        normed_two,
        grad_branch_two,
        two_keep,
        two_send,
        channel_cols,
        inner_bias[None, :],
        inner_weight,
        outer_weight,
        blocks,
        share,
        width,
        width // 3,
    )
    grad_outer_weight = reduce_rows(wo_keep, wo_send, bucket, seq)
    by_rows = (group_count // 2, width // group_count, hidden)
    grad_inner_weight = reduce_rows(
        wi_keep.reshape(by_rows), wi_send.reshape(by_rows), bucket, seq
    )
    branch_two = cube(branch_two) + outer_bias
    block_out = take_back((middle + route * gate_two * branch_two).astype(BF16), BF16)
    grad_outer_bias = jnp.sum(grad_branch_two.astype(F32), 0)
    grad_two = cube(grad_two)
    mod_gate_two = jnp.sum(route * branch_two * upstream, 1)
    mod_shift_two = jnp.sum(grad_two, 1)
    mod_scale_two = jnp.sum(grad_two * normed_mid, 1)
    grad_middle = upstream + norm_back(grad_two, normed_mid, inverse_mid, scale_two)
    mod_gate_one = jnp.sum(grad_middle * branch_one, 1)
    grad_branch_one = flat((gate_one * grad_middle).astype(BF16))
    grad_proj_bias = jnp.sum(grad_branch_one.astype(F32), 0)

    grad_attended = flat(
        (
            cube(contract(grad_branch_one, proj_weight, 1, 1).astype(BF16)).astype(F32) * head_cols
        ).astype(BF16)
    )
    head_hot = (jnp.arange(width)[:, None] // head_width == jnp.arange(heads)[None, :]).astype(F32)
    delta = lax.dot_general(
        head_hot,
        grad_attended.astype(F32) * attended.astype(F32),
        (((0,), (1,)), ((), ())),
        precision=lax.Precision.HIGHEST,
    ).reshape(heads, 1, rows)
    grad_queries, grad_own, grad_other = attend_back(
        queries, own_kv, other_kv, grad_attended, lse, delta, long_flag, head_ints, blocks
    )
    half_shape = (group_count // 2, width // group_count, width)
    att_keep, att_send = row_shares(attended)
    grad_proj_weight = reduce_rows(
        contract(att_keep, grad_branch_one, 1, 0, BF16).reshape(half_shape),
        contract(att_send, grad_branch_one, 1, 0, BF16).reshape(half_shape),
        bucket,
        seq,
    )
    grad_kv = add_low(grad_own, swap(grad_other, "bucket", 1))
    grad_columns = jnp.concatenate([grad_queries, grad_kv], 1)
    one_keep, one_send = row_shares(normed_one)
    qkv_shape = (group_count // 2, width // group_count, 3 * width)
    grad_qkv_weight = reduce_rows(
        contract(one_keep, grad_columns, 1, 0, BF16).reshape(qkv_shape),
        contract(one_send, grad_columns, 1, 0, BF16).reshape(qkv_shape),
        bucket,
        seq,
    )
    column_sums = jnp.sum(grad_columns.astype(F32), 0)
    grad_one = cube(contract(grad_columns, qkv_weight, 1, 1))
    mod_shift_one = jnp.sum(grad_one, 1)
    mod_scale_one = jnp.sum(grad_one * normed_x, 1)
    grad_x = grad_middle + norm_back(grad_one, normed_x, inverse_x, scale_one)
    grad_tokens = take_back(grad_x.astype(BF16), F32)

    early = jnp.concatenate(
        [mod_gate_one, mod_shift_two, mod_scale_two, mod_gate_two], 1
    ).reshape(1, -1)
    early_bias = jnp.concatenate([grad_proj_bias, grad_inner_bias[0], grad_outer_bias])[None, :]
    early_all = gather_all(jnp.concatenate([early, early_bias], 1).astype(BF16))
    late = jnp.concatenate([mod_shift_one, mod_scale_one], 1).reshape(1, -1)
    late_bias = jnp.concatenate([column_sums[:width], column_sums[2 * width :]])[None, :]
    late_all = gather_all(jnp.concatenate([late, late_bias], 1).astype(BF16))
    place = bucket * seq_count + seq
    device_count = group_count * seq_count
    early_mod = early_all[:, : 4 * blocks * width].reshape(-1, 4 * width)
    late_mod = late_all[:, : 2 * blocks * width].reshape(-1, 2 * width)
    cond_mine = lax.dynamic_slice_in_dim(
        cond_all, place * (width // device_count), width // device_count, 1
    )
    all_mod = jnp.concatenate([late_mod, early_mod], 1)
    grad_ada_weight = contract(cond_mine, all_mod, 0, 0)

    def own_sum(array):
        size = array.shape[1] // device_count
        own = lax.dynamic_slice_in_dim(array, place * size, size, 1)
        return jnp.sum(own.astype(F32), 0)

    early_rest = early_all[:, 4 * blocks * width :]
    late_rest = late_all[:, 2 * blocks * width :]
    return (
        block_out,
        grad_tokens,
        grad_ada_weight,
        own_sum(all_mod),
        grad_qkv_weight,
        own_sum(late_rest[:, :width]),
        own_sum(late_rest[:, width:]),
        grad_proj_weight,
        own_sum(early_rest[:, :width]),
        grad_inner_weight,
        own_sum(early_rest[:, width : width + hidden]),
        grad_outer_weight,
        own_sum(early_rest[:, width + hidden :]),
    )


def solution(mesh):
    split = P(("bucket", "seq"))
    split_rows = P(("bucket", "seq"), None)
    return jax.shard_map(
        on_device,
        mesh=mesh,
        in_specs=(split_rows, split, split, P("bucket", None), P("bucket"))
        + (P(),) * 13
        + (split_rows,),
        out_specs=(
            split_rows,
            split_rows,
            split_rows,
            split,
            split_rows,
            split,
            split,
            split_rows,
            split,
            split_rows,
            split,
            split_rows,
            split,
        ),
        check_vma=False,
    )
```

```python
import functools

import jax
import jax.numpy as jnp
from jax import lax
from jax.experimental import pallas as pl
from jax.experimental.pallas import tpu as pltpu
from jax.sharding import PartitionSpec as P

EPSILON = 1e-06
LOG2E = 1.4426950408889634
LANES = 128
NOTES = 16
FEED_VMEM = 60
FEED_SUB = 768
GELU_A = 0.7978845608028654
GELU_B = 0.044715
F32 = jnp.float32
BF16 = jnp.bfloat16


def contract(left, right, left_dim, right_dim, out=F32):
    return lax.dot_general(
        left, right, (((left_dim,), (right_dim,)), ((), ())), preferred_element_type=out
    )


def swap(array, axis, bit):
    size = lax.axis_size(axis)
    return lax.ppermute(array, axis, [(i, i ^ bit) for i in range(size)])


def launch(
    body, out_shape, *, in_specs, out_specs, name, after=(), grid=(), prefetch=0, scratch=(),
    aliases=None, vmem=56, micros=1,
):
    lead = prefetch + len(in_specs)
    waits, outs = len(after), len(out_shape)

    def kernel(*refs):
        rest = refs[lead + waits :]
        body(*refs[:lead], *rest[:outs], *rest[outs + 1 :])
        rest[outs][...] = jnp.zeros(rest[outs].shape, F32)

    token = (8, LANES)
    specs = dict(
        in_specs=list(in_specs) + [pl.BlockSpec(memory_space=pl.ANY)] * waits,
        scratch_shapes=list(scratch),
    )
    if grid:
        specs = dict(
            grid_spec=pltpu.PrefetchScalarGridSpec(
                num_scalar_prefetch=prefetch,
                grid=grid,
                out_specs=list(out_specs) + [pl.BlockSpec(token, lambda *i: (0, 0))],
                **specs,
            )
        )
    else:
        specs["out_specs"] = list(out_specs) + [pl.BlockSpec(memory_space=pltpu.VMEM)]
    call = pl.pallas_call(
        kernel,
        out_shape=list(out_shape) + [jax.ShapeDtypeStruct(token, F32)],
        input_output_aliases=aliases or {},
        compiler_params=pltpu.CompilerParams(vmem_limit_bytes=vmem * 1024 * 1024),
        cost_estimate=pl.CostEstimate(
            flops=int(micros * 1000000000), bytes_accessed=0, transcendentals=0
        ),
        name=name,
        **specs,
    )

    def run(*operands):
        *results, mark = call(*operands, *after)
        return results, mark

    return run


def vmem_specs(count):
    return [pl.BlockSpec(memory_space=pltpu.VMEM)] * count


def smem_specs(count):
    return [pl.BlockSpec(memory_space=pltpu.SMEM)] * count


def like(dtype, *shape):
    return jax.ShapeDtypeStruct(shape, dtype)


def plan_kernel(
    slots, piece, chips, blocks, place_ref, seg_own, seg_other, bucket_own, bucket_other,
    head_mask, channel_mask, send_which, send_index, back_which, back_index, cond_which,
    cond_row, flags, keep_heads, keep_channels, order_ref, rank_ref, id_ref, long_ref,
):
    core = place_ref[0]
    seq = place_ref[1]
    total = 2 * slots
    ids, keys = [], []
    for i in range(total):
        at = (i % slots) * piece
        ids.append(jnp.where(core == i // slots, seg_own[at], seg_other[at]))
    for i in range(total):
        base = (i // slots) * slots
        equal = jnp.int32(0)
        for j in range(slots):
            equal += jnp.where(ids[base + j] == ids[i], 1, 0)
        is_long = jnp.where(equal > 1, 1, 0)
        id_ref[i] = ids[i]
        long_ref[i] = is_long
        keys.append(jnp.where(is_long == 1, i, total + i))
    for i in range(total):
        rank = jnp.int32(0)
        for j in range(total):
            rank += jnp.where(keys[j] < keys[i], 1, 0)
        rank_ref[i] = rank
        order_ref[rank] = jnp.int32(i)
    for k in range(chips):
        for s in range(blocks):
            item = order_ref[((seq ^ k) * 2 + core) * blocks + s]
            send_which[k * blocks + s] = jnp.where(item // slots == core, 0, 1)
            send_index[k * blocks + s] = item % slots
    for j in range(slots):
        rank = rank_ref[core * slots + j]
        back_which[j] = jnp.where((rank // blocks) % 2 == core, 0, 1)
        back_index[j] = ((rank // (2 * blocks)) ^ seq) * blocks + rank % blocks
    flags[0] = long_ref[order_ref[seq * 2 * blocks]]
    flags[1] = core
    heads = head_mask.shape[1]
    groups = channel_mask.shape[1]
    for s in range(blocks):
        item = order_ref[(seq * 2 + core) * blocks + s]
        other = jnp.where(item // slots == core, 0, 1)
        cond_which[s] = other
        cond_row[s] = id_ref[item]
        step = jnp.where(other == 0, bucket_own[0], bucket_other[0])
        for h in range(heads):
            keep_heads[s * heads + h] = head_mask[step, h]
        for f in range(groups):
            keep_channels[s * groups + f] = channel_mask[step, f]


def make_plan(place, segment, seg_other, bucket, bucket_other, head_mask, channel_mask, slots, piece,
              chips, blocks):
    smem = pl.BlockSpec(memory_space=pltpu.SMEM)
    sizes = [chips * blocks] * 2 + [slots] * 2 + [blocks] * 2 + [2]
    sizes += [blocks * head_mask.shape[1], blocks * channel_mask.shape[1]]
    return pl.pallas_call(
        functools.partial(plan_kernel, slots, piece, chips, blocks),
        in_specs=[smem] * 7,
        out_specs=[smem] * 9,
        out_shape=[jax.ShapeDtypeStruct((n,), jnp.int32) for n in sizes],
        scratch_shapes=[pltpu.SMEM((2 * slots,), jnp.int32)] * 4,
        cost_estimate=pl.CostEstimate(flops=0, bytes_accessed=8000000, transcendentals=0),
        name="make_plan",
    )(place, segment, seg_other, bucket, bucket_other, head_mask, channel_mask)


def send_kernel(blocks, which_ref, index_ref, own_ref, other_ref, *outs):
    for m in range(len(outs) * blocks):

        @pl.when(which_ref[m] == 0)
        def _():
            outs[m // blocks][m % blocks] = own_ref[index_ref[m]]

        @pl.when(which_ref[m] != 0)
        def _():
            outs[m // blocks][m % blocks] = other_ref[index_ref[m]]


def send_blocks(own, other, which, index, chips, blocks, after=()):
    _, rows, width = own.shape
    return launch(
        functools.partial(send_kernel, blocks),
        [like(own.dtype, blocks, rows, width)] * chips,
        in_specs=smem_specs(2) + vmem_specs(2),
        out_specs=vmem_specs(chips),
        after=after,
        vmem=16,
        name="send_blocks",
    )(which, index, own, other)


def pick_kernel(which_ref, index_ref, own_ref, other_ref, out_ref):
    for m in range(out_ref.shape[0]):

        @pl.when(which_ref[m] == 0)
        def _():
            out_ref[m] = own_ref[index_ref[m]].astype(out_ref.dtype)

        @pl.when(which_ref[m] != 0)
        def _():
            out_ref[m] = other_ref[index_ref[m]].astype(out_ref.dtype)


def pick_blocks(own, other, which, index, out_dtype, after=()):
    _, rows, width = own.shape
    (out,), mark = launch(
        pick_kernel,
        [like(out_dtype, index.shape[0], rows, width)],
        in_specs=smem_specs(2) + vmem_specs(2),
        out_specs=vmem_specs(1),
        after=after,
        vmem=16,
        micros=3,
        name="pick_blocks",
    )(which, index, own, other)
    return out, mark


def leaving(k, s, value, stay_ref, odd_ref, even_ref):
    rows = value.shape[0]
    if k == 0:
        stay_ref[s] = value
        return
    target = even_ref if k == 2 else odd_ref
    first = ((k // 2 if k % 2 else 0) * stay_ref.shape[0] + s) * rows
    target[first : first + rows] = value


def leaving_shapes(blocks, piece, width):
    count = blocks * piece
    return [
        like(BF16, blocks, piece, width),
        like(BF16, 2 * count + NOTES, width),
        like(BF16, count, width),
    ]


def relay_kernel(even_ref, odd_ref, near_ref, out_ref):
    count = even_ref.shape[0]
    out_ref[:count] = even_ref[...]
    out_ref[count : 2 * count] = near_ref[count : 2 * count]
    out_ref[2 * count : 2 * count + NOTES] = odd_ref[2 * count :]
    out_ref[2 * count + NOTES :] = near_ref[2 * count :]


def relay(even, odd, near, after=()):
    count, width = even.shape
    (out,), mark = launch(
        relay_kernel,
        [like(BF16, 2 * count + 2 * NOTES, width)],
        in_specs=vmem_specs(3),
        out_specs=vmem_specs(1),
        after=after,
        vmem=16,
        name="relay",
    )(even, odd, near)
    return out, mark


def collect_kernel(stay_ref, odd_ref, near_ref, far_ref, out_ref, notes_ref):
    blocks, rows, width = stay_ref.shape
    count = blocks * rows
    out_ref[:blocks] = stay_ref[...]
    for k, part in enumerate((near_ref[:count], far_ref[:count], far_ref[count : 2 * count])):
        out_ref[(k + 1) * blocks : (k + 2) * blocks] = part.reshape(blocks, rows, width)
    notes_ref[:NOTES] = odd_ref[2 * count :]
    notes_ref[NOTES : 2 * NOTES] = near_ref[2 * count :]
    notes_ref[2 * NOTES :] = far_ref[2 * count :]


def collect(stay, odd, near, far, after=()):
    blocks, rows, width = stay.shape
    return launch(
        collect_kernel,
        [like(BF16, 4 * blocks, rows, width), like(BF16, 4 * NOTES, width)],
        in_specs=vmem_specs(4),
        out_specs=vmem_specs(2),
        after=after,
        vmem=16,
        micros=2,
        name="collect",
    )(stay, odd, near, far)


def modulate_kernel(
    blocks, which_ref, row_ref, own_ref, other_ref, weight_ref, bias_ref, out_ref, act_ref, held
):
    @pl.when(pl.program_id(0) == 0)
    def _():
        slots, width = own_ref.shape
        picked = []
        for s in range(blocks):
            hot = lax.broadcasted_iota(jnp.int32, (slots, width), 0) == row_ref[s]
            source = jnp.where(which_ref[s] == 0, own_ref[...].astype(F32), other_ref[...].astype(F32))
            picked.append(jnp.sum(jnp.where(hot, source, 0.0), 0, keepdims=True))
        picked.append(jnp.zeros((16 - blocks, width), F32))
        value = jnp.concatenate(picked, 0)
        held[...] = (value / (1.0 + jnp.exp(-value))).astype(BF16)
        act_ref[...] = held[...]

    out_ref[...] = (contract(held[...], weight_ref[...], 1, 0) + bias_ref[...])[:8]


def modulate(which, row, own, other, weight, bias, blocks, chunk):
    slots, width = own.shape
    columns = weight.shape[1]
    smem = pl.BlockSpec(memory_space=pltpu.SMEM)
    return pl.pallas_call(
        functools.partial(modulate_kernel, blocks),
        grid=(columns // chunk,),
        in_specs=[
            smem,
            smem,
            pl.BlockSpec((slots, width), lambda i: (0, 0)),
            pl.BlockSpec((slots, width), lambda i: (0, 0)),
            pl.BlockSpec((width, chunk), lambda i: (0, i)),
            pl.BlockSpec((1, chunk), lambda i: (0, i)),
        ],
        out_specs=[
            pl.BlockSpec((8, chunk), lambda i: (0, i)),
            pl.BlockSpec((16, width), lambda i: (0, 0)),
        ],
        out_shape=[
            jax.ShapeDtypeStruct((8, columns), F32),
            jax.ShapeDtypeStruct((16, width), BF16),
        ],
        scratch_shapes=[pltpu.VMEM((16, width), BF16)],
        compiler_params=pltpu.CompilerParams(vmem_limit_bytes=32 * 1024 * 1024),
        cost_estimate=pl.CostEstimate(
            flops=0, bytes_accessed=3 * width * columns, transcendentals=0
        ),
        name="modulate",
    )(which, row, own, other, weight, bias[None, :])


def norm_parts(value):
    center = value - jnp.mean(value, -1, keepdims=True)
    spread = jnp.mean(center * center, -1, keepdims=True)
    inverse = lax.rsqrt(spread + EPSILON)
    return center * inverse, inverse


def norm_back(grad, normed, inverse, scale):
    scaled = grad * (1.0 + scale)
    mean_one = jnp.mean(scaled, -1, keepdims=True)
    mean_two = jnp.mean(scaled * normed, -1, keepdims=True)
    return inverse * (scaled - mean_one - normed * mean_two)


def mod_row(mod_ref, index, part, width):
    return mod_ref[index : index + 1, part * width : (part + 1) * width]


def enter_kernel(blocks, *refs):
    parts = refs[:-8]
    mod_ref, weight_ref, bias_ref, x_ref, one_ref, turned_ref, kv_ref, held = refs[-8:]
    _, piece, width = parts[0].shape
    block = held.shape[0] // blocks

    @pl.when(pl.program_id(0) == 0)
    def _():
        for s in range(blocks):
            for k, part in enumerate(parts):
                first = s * block + k * piece
                x = part[s]
                x_ref[first : first + piece] = x
                normed, _ = norm_parts(x.astype(F32))
                one = normed * (1.0 + mod_row(mod_ref, s, 1, width)) + mod_row(mod_ref, s, 0, width)
                held[first : first + piece] = one.astype(BF16)
        one_ref[...] = held[...]
        turned_ref[...] = held[...].T

    kv_ref[...] = (contract(held[...], weight_ref[...], 1, 0) + bias_ref[...]).astype(BF16)


def enter(parts, mod, weight, bias, blocks):
    _, piece, width = parts[0].shape
    rows = piece * blocks * len(parts)
    const = lambda shape: pl.BlockSpec(shape, lambda i: (0,) * len(shape))
    return pl.pallas_call(
        functools.partial(enter_kernel, blocks),
        grid=(2,),
        in_specs=[const(p.shape) for p in parts]
        + [
            const((8, 2 * width)),
            pl.BlockSpec((width, width), lambda i: (0, 1 + i)),
            pl.BlockSpec((1, width), lambda i: (0, i)),
        ],
        out_specs=[
            const((rows, width)),
            const((rows, width)),
            const((width, rows)),
            pl.BlockSpec((rows, width), lambda i: (0, i)),
        ],
        out_shape=[
            jax.ShapeDtypeStruct((rows, width), BF16),
            jax.ShapeDtypeStruct((rows, width), BF16),
            jax.ShapeDtypeStruct((width, rows), BF16),
            jax.ShapeDtypeStruct((rows, 2 * width), BF16),
        ],
        scratch_shapes=[pltpu.VMEM((rows, width), BF16)],
        compiler_params=pltpu.CompilerParams(vmem_limit_bytes=48 * 1024 * 1024),
        cost_estimate=pl.CostEstimate(
            flops=8 * rows * width * width, bytes_accessed=12 * width * width, transcendentals=0
        ),
        name="enter",
    )(*parts, mod, weight, bias)


def linear_kernel(x_ref, weight_ref, bias_ref, out_ref):
    out_ref[...] = (contract(x_ref[...], weight_ref[...], 1, 0) + bias_ref[...]).astype(out_ref.dtype)


def linear(x, weight, bias, columns, chunk):
    rows, width = x.shape
    return pl.pallas_call(
        linear_kernel,
        grid=(columns // chunk,),
        in_specs=[
            pl.BlockSpec((rows, width), lambda i: (0, 0)),
            pl.BlockSpec((width, chunk), lambda i: (0, i)),
            pl.BlockSpec((1, chunk), lambda i: (0, i)),
        ],
        out_specs=pl.BlockSpec((rows, chunk), lambda i: (0, i)),
        out_shape=jax.ShapeDtypeStruct((rows, columns), BF16),
        compiler_params=pltpu.CompilerParams(vmem_limit_bytes=32 * 1024 * 1024),
        cost_estimate=pl.CostEstimate(
            flops=4 * rows * width * columns, bytes_accessed=8 * width * columns, transcendentals=0
        ),
        name="linear",
    )(x, weight, bias[None, :])


def middle_kernel(blocks, *refs):
    parts = refs[:-12]
    (
        att_ref, weight_ref, bias_ref, x_ref, mod_ref,
        branch_ref, middle_ref, two_ref, two_turned, att_turned, grad_ref, bias_grad,
    ) = refs[-12:]
    rows, width = x_ref.shape
    block = rows // blocks
    piece = parts[0].shape[1]
    att_turned[...] = att_ref[...].T
    total = jnp.zeros((1, width), F32)
    for s in range(blocks):
        part = slice(s * block, (s + 1) * block)
        branch = contract(att_ref[part], weight_ref[...], 1, 0) + bias_ref[...]
        branch_ref[part] = branch
        middle = x_ref[part].astype(F32) + mod_row(mod_ref, s, 2, width) * branch
        middle_ref[part] = middle
        normed, _ = norm_parts(middle)
        two_ref[part] = (
            normed * (1.0 + mod_row(mod_ref, s, 4, width)) + mod_row(mod_ref, s, 3, width)
        ).astype(BF16)
        for k, source in enumerate(parts):
            first = s * block + k * piece
            payload = source[s].astype(F32)
            grad = (payload[:, width : width + 1] * mod_row(mod_ref, s, 5, width) * payload[:, :width]).astype(BF16)
            grad_ref[first : first + piece] = grad
            total += jnp.sum(grad.astype(F32), 0, keepdims=True)
    two_turned[...] = two_ref[...].T
    bias_grad[...] = total


def middle_part(parts, attended, weight, bias, x, mod, blocks):
    rows, width = x.shape
    vmem = pl.BlockSpec(memory_space=pltpu.VMEM)
    return pl.pallas_call(
        functools.partial(middle_kernel, blocks),
        in_specs=[vmem] * (len(parts) + 5),
        out_specs=[vmem] * 7,
        out_shape=[
            jax.ShapeDtypeStruct((rows, width), F32),
            jax.ShapeDtypeStruct((rows, width), F32),
            jax.ShapeDtypeStruct((rows, width), BF16),
            jax.ShapeDtypeStruct((width, rows), BF16),
            jax.ShapeDtypeStruct((width, rows), BF16),
            jax.ShapeDtypeStruct((rows, width), BF16),
            jax.ShapeDtypeStruct((1, width), F32),
        ],
        compiler_params=pltpu.CompilerParams(vmem_limit_bytes=48 * 1024 * 1024),
        cost_estimate=pl.CostEstimate(
            flops=8 * rows * width * width, bytes_accessed=24 * rows * width, transcendentals=0
        ),
        name="middle_part",
    )(*parts, attended, weight, bias[None, :], x, mod)


def turn_kernel(blocks, heads, *refs):
    count = 4
    parts = refs[:count]
    (
        keep_ref, out_ref, gx_ref, middle_ref, branch_ref, att_ref, mod_ref, bias_ref, weight_ref,
        act_ref, outer_sum, *hidden_sums,
    ) = refs[count:-7]
    stay_ref, odd_ref, even_ref, grad_middle, grad_one, grad_att, delta_ref = refs[-7:]
    notes = []
    rows, width = middle_ref.shape
    block = rows // blocks
    piece = parts[0].shape[1]
    head_width = width // heads
    column_head = lax.broadcasted_iota(jnp.int32, (heads, width), 1) // head_width
    hot = (column_head == lax.broadcasted_iota(jnp.int32, (heads, width), 0)).astype(F32)
    bias_total = jnp.zeros((1, width), F32)
    for s in range(blocks):
        sums = [jnp.zeros((1, width), F32) for _ in range(4)]
        gate_one = mod_row(mod_ref, s, 2, width)
        scale_two = mod_row(mod_ref, s, 4, width)
        gate_two = mod_row(mod_ref, s, 5, width)
        for k, source in enumerate(parts):
            first = s * block + k * piece
            part = slice(first, first + piece)
            payload = source[s].astype(F32)
            upstream = payload[:, :width]
            route = payload[:, width : width + 1]
            middle = middle_ref[part]
            branch_two = route * (out_ref[part] + bias_ref[...])
            leaving(k, s, (middle + gate_two * branch_two).astype(BF16), stay_ref, odd_ref, even_ref)
            sums[3] += jnp.sum(branch_two * upstream, 0, keepdims=True)
            grad_two = gx_ref[part]
            normed, inverse = norm_parts(middle)
            sums[1] += jnp.sum(grad_two, 0, keepdims=True)
            sums[2] += jnp.sum(grad_two * normed, 0, keepdims=True)
            grad = upstream + norm_back(grad_two, normed, inverse, scale_two)
            grad_middle[part] = grad
            sums[0] += jnp.sum(grad * branch_ref[part], 0, keepdims=True)
            low = (gate_one * grad).astype(BF16)
            grad_one[part] = low
            bias_total += jnp.sum(low.astype(F32), 0, keepdims=True)
        notes += sums
        part = slice(s * block, (s + 1) * block)
        row = jnp.zeros((1, width), F32)
        for h in range(heads):
            row = jnp.where(
                hot[h : h + 1] > 0.5, keep_ref[s * heads + h].astype(F32), row
            )
        low = contract(grad_one[part], weight_ref[...], 1, 1).astype(BF16).astype(F32) * row
        grad_att[part] = low.astype(BF16)
        delta_ref[:, part] = lax.dot_general(
            hot,
            low * att_ref[part].astype(F32),
            (((1,), (1,)), ((), ())),
            precision=lax.Precision.HIGHEST,
            preferred_element_type=F32,
        )
    notes.append(bias_total)
    notes.append(outer_sum[...])
    for ref in hidden_sums:
        notes += [ref[:, lo : lo + width] for lo in range(0, ref.shape[1], width)]
    notes.append(act_ref[:blocks].astype(F32))
    odd_ref[2 * blocks * piece :] = jnp.concatenate(notes, 0).astype(BF16)


def turn_part(
    parts, keep, out, gx, middle, branch, attended, mod, bias, weight, act, sums, blocks, after=()
):
    rows, width = middle.shape
    heads = keep.shape[0] // blocks
    return launch(
        functools.partial(turn_kernel, blocks, heads),
        leaving_shapes(blocks, parts[0].shape[1], width)
        + [
            like(F32, rows, width),
            like(BF16, rows, width),
            like(BF16, rows, width),
            like(F32, heads, rows),
        ],
        in_specs=vmem_specs(len(parts)) + smem_specs(1) + vmem_specs(9 + len(sums)),
        out_specs=vmem_specs(7),
        after=after,
        vmem=48,
        micros=13,
        name="turn_part",
    )(*parts, keep, out, gx, middle, branch, attended, mod, bias[None, :], weight, act, *sums)


def query_back_kernel(
    core_ref, proj_keep, proj_send, one_keep, one_send, grad_one, grad_q, weight_ref, *refs
):
    keep_ref, send_ref, gx_ref, sum_ref = refs[-4:]
    width = grad_q.shape[1]
    half = keep_ref.shape[0]
    rows = grad_q.shape[0]
    turned = lambda ref: ref[...].reshape(half, rows)
    keep_ref[:, :width] = contract(turned(proj_keep), grad_one[...], 1, 0).astype(BF16)
    send_ref[:, :width] = contract(turned(proj_send), grad_one[...], 1, 0).astype(BF16)
    keep_ref[:, width:] = contract(turned(one_keep), grad_q[...], 1, 0).astype(BF16)
    send_ref[:, width:] = contract(turned(one_send), grad_q[...], 1, 0).astype(BF16)
    gx_ref[...] = contract(grad_q[...], weight_ref[...], 1, 1)
    sum_ref[...] = jnp.sum(grad_q[...].astype(F32), 0, keepdims=True)


def turned_specs(array):
    pairs, _, share, rows = array.shape
    keep = pl.BlockSpec((pairs, None, share, rows), lambda i, c: (0, c[0], 0, 0))
    send = pl.BlockSpec((pairs, None, share, rows), lambda i, c: (0, 1 - c[0], 0, 0))
    return [keep, send]


def query_back(core, att_turned, one_turned, grad_one, grad_q, weight, after=()):
    rows, width = grad_q.shape
    half = width // 2
    const = lambda shape: pl.BlockSpec(shape, lambda i, c: (0,) * len(shape))
    return launch(
        query_back_kernel,
        [
            like(BF16, half, 2 * width),
            like(BF16, half, 2 * width),
            like(F32, rows, width),
            like(F32, 1, width),
        ],
        prefetch=1,
        grid=(1,),
        in_specs=turned_specs(att_turned)
        + turned_specs(one_turned)
        + [const((rows, width)), const((rows, width)), const((width, width))],
        out_specs=[
            const((half, 2 * width)),
            const((half, 2 * width)),
            const((rows, width)),
            const((1, width)),
        ],
        after=after,
        micros=10,
        name="query_back",
    )(core, att_turned, att_turned, one_turned, one_turned, grad_one, grad_q, weight)


def leave_kernel(
    blocks, core_ref, one_keep, one_send, own_ref, got_ref, weight_ref, gx_in, x_ref, middle_ref,
    mod_ref, query_sum, keep_ref, send_ref, stay_ref, odd_ref, even_ref, total, grads,
):
    piece = stay_ref.shape[1]
    rows, width = x_ref.shape
    half = keep_ref.shape[0]
    block = rows // blocks
    step = pl.program_id(0)
    turned = lambda ref: ref[...].reshape(half, rows)
    grads[...] = (own_ref[...].astype(F32) + got_ref[...].astype(F32)).astype(BF16)
    keep_ref[...] = contract(turned(one_keep), grads[...], 1, 0).astype(BF16)
    send_ref[...] = contract(turned(one_send), grads[...], 1, 0).astype(BF16)

    @pl.when(step == 0)
    def _():
        total[...] = gx_in[...] + contract(grads[...], weight_ref[...], 1, 1)

    @pl.when(step == 1)
    def _():
        notes = []
        for s in range(blocks):
            part = slice(s * block, (s + 1) * block)
            grad = total[part] + contract(grads[part], weight_ref[...], 1, 1)
            normed, inverse = norm_parts(x_ref[part].astype(F32))
            notes.append(jnp.sum(grad, 0, keepdims=True))
            notes.append(jnp.sum(grad * normed, 0, keepdims=True))
            back = norm_back(grad, normed, inverse, mod_row(mod_ref, s, 1, width))
            low = (middle_ref[part] + back).astype(BF16)
            for k in range(block // piece):
                leaving(k, s, low[k * piece : (k + 1) * piece], stay_ref, odd_ref, even_ref)
        notes.append(query_sum[...])
        notes.append(jnp.sum(grads[...].astype(F32), 0, keepdims=True))
        notes.append(jnp.zeros((NOTES - 2 * blocks - 2, width), F32))
        odd_ref[2 * blocks * piece :] = jnp.concatenate(notes, 0).astype(BF16)


def leave(
    core, one_turned, own, got, weight, gx, x, grad_middle, mod, query_sum, blocks, piece, after=()
):
    rows, width = x.shape
    half = width // 2
    const = lambda shape: pl.BlockSpec(shape, lambda i, c: (0,) * len(shape))
    once = lambda shape: pl.BlockSpec(
        shape, lambda i, c: (0,) * len(shape), pipeline_mode=pl.Buffered(1)
    )
    shapes = leaving_shapes(blocks, piece, width)
    return launch(
        functools.partial(leave_kernel, blocks),
        [like(BF16, half, 2 * width), like(BF16, half, 2 * width)] + shapes,
        prefetch=1,
        grid=(2,),
        in_specs=turned_specs(one_turned)
        + [
            pl.BlockSpec((rows, width), lambda i, c: (0, i)),
            pl.BlockSpec((rows, width), lambda i, c: (0, i)),
            pl.BlockSpec((width, width), lambda i, c: (0, 1 + i)),
            once((rows, width)),
            once((rows, width)),
            once((rows, width)),
            once((8, 2 * width)),
            once((1, width)),
        ],
        out_specs=[
            pl.BlockSpec((half, width), lambda i, c: (0, i)),
            pl.BlockSpec((half, width), lambda i, c: (0, i)),
        ]
        + [const(s.shape) for s in shapes],
        scratch=[pltpu.VMEM((rows, width), F32), pltpu.VMEM((rows, width), BF16)],
        after=after,
        micros=15,
        name="leave",
    )(core, one_turned, one_turned, own, got, weight, gx, x, grad_middle, mod, query_sum)


def head_columns(ref, start, head_width):
    part = ref[:, start : start + head_width]
    return jnp.concatenate(
        [part, jnp.zeros((part.shape[0], LANES - head_width), part.dtype)], axis=1
    )


def attend_kernel(
    heads, head_width, blocks, long_ref, keep_ref, q_ref, own_ref, other_ref, out_ref, lse_ref,
    qh, kh, vh, oh,
):
    rows, width = q_ref.shape
    block = rows // blocks
    factor = head_width**-0.5 * LOG2E
    is_long = long_ref[0] == 1
    for h in range(heads):
        start = h * head_width
        qh[h] = head_columns(q_ref, start, head_width)
        kh[h, :rows] = head_columns(own_ref, start, head_width)
        vh[h, :rows] = head_columns(own_ref, width + start, head_width)

    @pl.when(is_long)
    def _():
        for h in range(heads):
            start = h * head_width
            kh[h, rows:] = head_columns(other_ref, start, head_width)
            vh[h, rows:] = head_columns(other_ref, width + start, head_width)

    def one(h, first, count, key_first, key_count):
        queries = qh[h, pl.ds(first, count), :]
        keys = kh[h, pl.ds(key_first, key_count), :]
        values = vh[h, pl.ds(key_first, key_count), :]
        scores = contract(keys, queries, 1, 1)
        top = jnp.max(scores, 0, keepdims=True)
        exponent = jnp.exp2((scores - top) * factor)
        total = jnp.sum(exponent, 0, keepdims=True)
        mixed = contract(values, exponent.astype(BF16), 0, 0) * (1.0 / total)
        oh[h, pl.ds(first, count), :] = mixed.T.astype(BF16)
        lse_ref[pl.ds(h, 1), pl.ds(first, count)] = top * factor + jnp.log2(total)

    def loop(index, first, count, key_first, key_count):
        def body(h, carry):
            keep = keep_ref[index * heads + h] == 1

            @pl.when(keep)
            def _():
                one(h, first, count, key_first, key_count)

            @pl.when(jnp.logical_not(keep))
            def _():
                oh[h, pl.ds(first, count), :] = jnp.zeros((count, LANES), BF16)

            return carry

        lax.fori_loop(0, heads, body, 0)

    @pl.when(is_long)
    def _():
        loop(0, 0, rows, 0, 2 * rows)

    @pl.when(jnp.logical_not(is_long))
    def _():
        for index in range(blocks):
            loop(index, index * block, block, index * block, block)

    for h in range(heads):
        out_ref[:, h * head_width : (h + 1) * head_width] = oh[h, :, :head_width]


def attend(queries, own, other, long_flag, keep, blocks):
    rows, width = queries.shape
    heads = keep.shape[0] // blocks
    head_width = width // heads
    vmem = pl.BlockSpec(memory_space=pltpu.VMEM)
    smem = pl.BlockSpec(memory_space=pltpu.SMEM)
    return pl.pallas_call(
        functools.partial(attend_kernel, heads, head_width, blocks),
        in_specs=[smem, smem, vmem, vmem, vmem],
        out_specs=[vmem, vmem],
        out_shape=[
            jax.ShapeDtypeStruct((rows, width), BF16),
            jax.ShapeDtypeStruct((heads, rows), F32),
        ],
        scratch_shapes=[
            pltpu.VMEM((heads, rows, LANES), BF16),
            pltpu.VMEM((heads, 2 * rows, LANES), BF16),
            pltpu.VMEM((heads, 2 * rows, LANES), BF16),
            pltpu.VMEM((heads, rows, LANES), BF16),
        ],
        compiler_params=pltpu.CompilerParams(vmem_limit_bytes=56 * 1024 * 1024),
        cost_estimate=pl.CostEstimate(
            flops=100 * rows * rows * width,
            bytes_accessed=12 * rows * width,
            transcendentals=2 * rows * rows * heads,
        ),
        name="attend",
    )(long_flag, keep, queries, own, other)


def attend_back_kernel(
    heads, head_width, blocks, long_ref, keep_ref, q_ref, own_ref, other_ref, go_ref, lse_ref,
    delta_ref, *refs,
):
    gq_ref, gown_ref, gother_ref, qh, kh, vh, gh, gqh, gkh, gvh = refs[-10:]
    rows, width = q_ref.shape
    block = rows // blocks
    scale = head_width**-0.5
    factor = scale * LOG2E
    is_long = long_ref[0] == 1
    for h in range(heads):
        start = h * head_width
        qh[h] = head_columns(q_ref, start, head_width)
        gh[h] = head_columns(go_ref, start, head_width)
        kh[h, :rows] = head_columns(own_ref, start, head_width)
        vh[h, :rows] = head_columns(own_ref, width + start, head_width)

    @pl.when(is_long)
    def _():
        for h in range(heads):
            start = h * head_width
            kh[h, rows:] = head_columns(other_ref, start, head_width)
            vh[h, rows:] = head_columns(other_ref, width + start, head_width)

    def one(h, first, count, key_first, key_count):
        queries = qh[h, pl.ds(first, count), :]
        grads = gh[h, pl.ds(first, count), :]
        keys = kh[h, pl.ds(key_first, key_count), :]
        values = vh[h, pl.ds(key_first, key_count), :]
        scores = contract(keys, queries, 1, 1)
        probs = jnp.exp2(scores * factor - lse_ref[pl.ds(h, 1), pl.ds(first, count)])
        gvh[h, pl.ds(key_first, key_count), :] = contract(
            probs.astype(BF16), grads, 1, 0
        ).astype(BF16)
        grad_probs = contract(values, grads, 1, 1)
        grad_scores = (probs * (grad_probs - delta_ref[pl.ds(h, 1), pl.ds(first, count)])).astype(BF16)
        gkh[h, pl.ds(key_first, key_count), :] = (
            contract(grad_scores, queries, 1, 0) * scale
        ).astype(BF16)
        gqh[h, pl.ds(first, count), :] = (
            (contract(keys, grad_scores, 0, 0) * scale).T
        ).astype(BF16)

    def loop(index, first, count, key_first, key_count):
        def body(h, carry):
            keep = keep_ref[index * heads + h] == 1

            @pl.when(keep)
            def _():
                one(h, first, count, key_first, key_count)

            @pl.when(jnp.logical_not(keep))
            def _():
                gqh[h, pl.ds(first, count), :] = jnp.zeros((count, LANES), BF16)
                gkh[h, pl.ds(key_first, key_count), :] = jnp.zeros((key_count, LANES), BF16)
                gvh[h, pl.ds(key_first, key_count), :] = jnp.zeros((key_count, LANES), BF16)

            return carry

        lax.fori_loop(0, heads, body, 0)

    @pl.when(is_long)
    def _():
        loop(0, 0, rows, 0, 2 * rows)
        for h in range(heads):
            start = h * head_width
            gother_ref[:, start : start + head_width] = gkh[h, rows:, :head_width]
            gother_ref[:, width + start : width + start + head_width] = gvh[h, rows:, :head_width]

    @pl.when(jnp.logical_not(is_long))
    def _():
        for index in range(blocks):
            loop(index, index * block, block, index * block, block)
        gother_ref[...] = jnp.zeros_like(gother_ref)

    for h in range(heads):
        start = h * head_width
        gq_ref[:, start : start + head_width] = gqh[h, :, :head_width]
        gown_ref[:, start : start + head_width] = gkh[h, :rows, :head_width]
        gown_ref[:, width + start : width + start + head_width] = gvh[h, :rows, :head_width]


def attend_back(queries, own, other, grad_out, lse, delta, long_flag, keep, blocks, after=()):
    rows, width = queries.shape
    heads = keep.shape[0] // blocks
    head_width = width // heads
    short = pltpu.VMEM((heads, rows, LANES), BF16)
    full = pltpu.VMEM((heads, 2 * rows, LANES), BF16)
    return launch(
        functools.partial(attend_back_kernel, heads, head_width, blocks),
        [like(BF16, rows, width), like(BF16, rows, 2 * width), like(BF16, rows, 2 * width)],
        in_specs=smem_specs(2) + vmem_specs(6),
        out_specs=vmem_specs(3),
        scratch=[short, full, full, short, short, full, full],
        after=after,
        vmem=60,
        micros=33,
        name="attend_back",
    )(long_flag, keep, queries, own, other, grad_out, lse, delta)


def feed_kernel(
    blocks, sub, group, first, resume, core_ref, keep_ref, x_ref, g_ref, xk_ref, xs_ref, bias_ref,
    wi_ref, wo_ref, *refs,
):
    act, gbefore = refs[-2:]
    out_ref, gx_ref, act_ref, wik_ref, wis_ref, gbias_ref = refs[-8:-2]
    rows, _ = x_ref.shape
    block = rows // blocks
    chunk = wi_ref.shape[1]
    half = wik_ref.shape[0]
    step = pl.program_id(0)
    groups = keep_ref.shape[0] // blocks
    turned = lambda ref: ref[...].reshape(half, rows)
    for lo in range(0, chunk, sub):
        cols = slice(lo, lo + sub)
        column_sum = jnp.zeros((1, sub), F32)
        for index in range(blocks):
            part = slice(index * block, (index + 1) * block)
            before = contract(x_ref[part], wi_ref[:, cols], 1, 0) + bias_ref[:, cols]
            grad_act = contract(g_ref[part], wo_ref[cols, :], 1, 1)
            base = index * groups + ((first + step) * chunk + lo) // group
            keep = jnp.concatenate(
                [
                    jnp.full((1, group), keep_ref[base + m].astype(F32))
                    for m in range(sub // group)
                ],
                axis=1,
            )
            square = before * before
            bend = jnp.tanh(GELU_A * before * (1.0 + GELU_B * square))
            gate = 0.5 * (1.0 + bend)
            slope = gate + (0.5 * GELU_A) * before * (1.0 - bend * bend) * (
                1.0 + (3.0 * GELU_B) * square
            )
            act[part, cols] = (before * gate * keep).astype(BF16)
            grad = (grad_act * keep * slope).astype(BF16)
            gbefore[part, cols] = grad
            column_sum += jnp.sum(grad.astype(F32), 0, keepdims=True)
        gbias_ref[:, cols] = column_sum
    out = contract(act[...], wo_ref[...], 1, 0)
    gx = contract(gbefore[...], wi_ref[...], 1, 1)

    @pl.when(step == 0)
    def _():
        if resume:
            out_ref[...] = refs[0][...] + out
            gx_ref[...] = refs[1][...] + gx
        else:
            out_ref[...] = out
            gx_ref[...] = gx

    @pl.when(step != 0)
    def _():
        out_ref[...] += out
        gx_ref[...] += gx

    act_ref[...] = act[...]
    wik_ref[...] = contract(turned(xk_ref), gbefore[...], 1, 0).astype(BF16)
    wis_ref[...] = contract(turned(xs_ref), gbefore[...], 1, 0).astype(BF16)


def feed(core, keep, x, grad, turned, bias, wi, wo, blocks, chunk, sub, first, count, before=()):
    rows, width = x.shape
    hidden = wi.shape[1]
    half = width // 2
    group = hidden * blocks // keep.shape[0]
    single = pl.Buffered(1)
    once = lambda shape: pl.BlockSpec(shape, lambda i, *c: (0, 0), pipeline_mode=single)
    tpairs, _, tshare, _ = turned.shape
    spec = lambda lead: pl.BlockSpec((tpairs, None, tshare, rows), lead, pipeline_mode=single)
    return launch(
        functools.partial(feed_kernel, blocks, sub, group, first, bool(before)),
        [
            like(F32, rows, width),
            like(F32, rows, width),
            like(BF16, rows, count * chunk),
            like(BF16, half, count * chunk),
            like(BF16, half, count * chunk),
            like(F32, 1, count * chunk),
        ],
        prefetch=2,
        grid=(count,),
        in_specs=[
            once((rows, width)),
            once((rows, width)),
            spec(lambda i, c, k: (0, c[0], 0, 0)),
            spec(lambda i, c, k: (0, 1 - c[0], 0, 0)),
            pl.BlockSpec((1, chunk), lambda i, *c: (0, first + i)),
            pl.BlockSpec((width, chunk), lambda i, *c: (0, first + i)),
            pl.BlockSpec((chunk, width), lambda i, *c: (first + i, 0)),
        ]
        + [once((rows, width))] * len(before),
        out_specs=[
            pl.BlockSpec((rows, width), lambda i, *c: (0, 0)),
            pl.BlockSpec((rows, width), lambda i, *c: (0, 0)),
            pl.BlockSpec((rows, chunk), lambda i, *c: (0, i)),
            pl.BlockSpec((half, chunk), lambda i, *c: (0, i)),
            pl.BlockSpec((half, chunk), lambda i, *c: (0, i)),
            pl.BlockSpec((1, chunk), lambda i, *c: (0, i)),
        ],
        scratch=[pltpu.VMEM((rows, chunk), BF16), pltpu.VMEM((rows, chunk), BF16)],
        vmem=FEED_VMEM,
        micros=25,
        name="feed",
    )(core, keep, x, grad, turned, turned, bias, wi, wo, *before)


def outer_kernel(share, starts, core_ref, *refs):
    acts = refs[: len(starts)]
    g_ref = refs[len(starts)]
    keep_ref, send_ref = refs[-2:]
    core = core_ref[0]
    step = pl.program_id(0)
    for act_ref, (lo, hi) in zip(acts, starts):

        @pl.when((step >= lo) & (step < hi))
        def _():
            grad = contract(act_ref[...], g_ref[...], 0, 0).astype(BF16)
            for pair in range(keep_ref.shape[0]):
                even = grad[2 * pair * share : (2 * pair + 1) * share]
                odd = grad[(2 * pair + 1) * share : (2 * pair + 2) * share]

                @pl.when(core == 0)
                def _():
                    keep_ref[pair] = even
                    send_ref[pair] = odd

                @pl.when(core != 0)
                def _():
                    keep_ref[pair] = odd
                    send_ref[pair] = even


def outer_part(core, acts, grad, share, chunk, after=()):
    rows, width = grad.shape
    pairs = chunk // (2 * share)
    specs, starts, at = [], [], 0
    for act in acts:
        count = act.shape[1] // chunk
        starts.append((at, at + count))
        specs.append(
            pl.BlockSpec(
                (rows, chunk), lambda i, lo=at, n=count: (0, jnp.clip(i - lo, 0, n - 1))
            )
        )
        at += count
    return launch(
        functools.partial(outer_kernel, share, starts),
        [like(BF16, at * pairs, share, width)] * 2,
        grid=(at,),
        in_specs=smem_specs(1) + specs + [pl.BlockSpec((rows, width), lambda i: (0, 0))],
        out_specs=[pl.BlockSpec((pairs, share, width), lambda i: (i, 0, 0))] * 2,
        after=after,
        micros=10,
        name="outer_part",
    )(core, *acts, grad)


def split_bit(array, dim, bit):
    keep = lax.dynamic_index_in_dim(array, bit, dim, keepdims=False)
    send = lax.dynamic_index_in_dim(array, 1 - bit, dim, keepdims=False)
    return keep, send


def split_kernel(units, place_ref, *refs):
    outs = refs[-4:]
    at = 0
    for member, count in enumerate(units):
        ins = refs[8 * member : 8 * member + 8]
        for m, out in enumerate(outs):
            left, right = ins[2 * m], ins[2 * m + 1]
            total = (left[0].astype(F32) + right[0].astype(F32)).astype(BF16)
            if count == 1 and len(total.shape) == 2:
                out[0, at] = total
            else:
                out[0, at : at + count] = total
        at += count


def split_call(place, arrays, blocks, spots, units, tail, count, low_bit, high_bit, after, name):
    low = lambda p: (p[2] >> low_bit) & 1
    high = lambda p: (p[2] >> high_bit) & 1
    leads = [
        lambda j, p: j * 2 + low(p),
        lambda j, p: j * 2 + 1 - low(p),
        lambda j, p: high(p) * count + j,
        lambda j, p: (1 - high(p)) * count + j,
    ]
    specs = []
    for block, spot in zip(blocks, spots):
        for m, lead in enumerate(leads):
            index = lambda j, p, lead=lead, spot=spot[m // 2]: (lead(j, p),) + spot
            specs += [pl.BlockSpec((1,) + block, index)] * 2
    shape = (sum(units),) + tail
    return launch(
        functools.partial(split_kernel, units),
        [like(BF16, count, *shape)] * 4,
        prefetch=1,
        grid=(count,),
        in_specs=specs,
        out_specs=[pl.BlockSpec((1,) + shape, lambda j, p: (j, 0, 0, 0))] * 4,
        after=after,
        micros=3,
        name=name,
    )(place, *arrays)


def cross_kernel(kinds, place_ref, *refs):
    keep_ref, send_ref = refs[-2:]
    share = keep_ref.shape[2]
    bit = place_ref[1] & 1

    def write(out_ref, low):
        tile = 0
        for n, members in enumerate(kinds):
            am, ag, bm, bg = refs[4 * n : 4 * n + 4]
            at = 0
            for by_rows in members:
                if by_rows:
                    for high, (m, g) in enumerate(((am, ag), (bm, bg))):
                        total = m[0, at + low].astype(F32) + g[0, at + low].astype(F32)
                        for q in range(4):
                            out_ref[high, tile + q] = total[q * share : (q + 1) * share].astype(BF16)
                    at += 2
                    tile += 4
                else:
                    for side, (m, g) in enumerate(((am, ag), (bm, bg))):
                        total = m[0, at].astype(F32) + g[0, at].astype(F32)
                        for high in range(2):
                            first = (2 * high + low) * share
                            out_ref[high, tile + side] = total[first : first + share].astype(BF16)
                    at += 1
                    tile += 2

    @pl.when(bit == 0)
    def _():
        write(keep_ref, 0)
        write(send_ref, 1)

    @pl.when(bit == 1)
    def _():
        write(keep_ref, 1)
        write(send_ref, 0)


def last_kernel(place_ref, mine_ref, got_ref, *refs):
    keep_ref, send_ref = refs[-2:]
    bit = place_ref[1] >> 1
    add = lambda i: (mine_ref[i].astype(F32) + got_ref[i].astype(F32)).astype(BF16)
    keep_ref[...] = add(bit)
    send_ref[...] = add(1 - bit)


def small_call(body, place, arrays, shape, after, name):
    return launch(
        body,
        [shape, shape],
        in_specs=smem_specs(1) + vmem_specs(len(arrays)),
        out_specs=vmem_specs(2),
        after=after,
        vmem=24,
        name=name,
    )(place, *arrays)


class Package:
    def __init__(self, place, *members):
        self.place = place
        self.keeps = [keep for keep, _ in members]
        self.flight = [swap(send, "bucket", 1) for _, send in members]
        self.kinds = [keep.ndim == 4 for keep in self.keeps]

    def first(self, *after):
        pairs = self.keeps[0].shape[0]
        self.bits = pairs.bit_length() - 1
        self.count = pairs // 2
        self.turn = 0
        arrays, blocks, spots, units = [], [], [], []
        for keep, got, by_rows in zip(self.keeps, self.flight, self.kinds):
            arrays += [keep, got] * 4
            if by_rows:
                blocks.append((2,) + keep.shape[2:])
                spots.append([(0, 0, 0), (1, 0, 0)])
                units.append(2)
                tail = keep.shape[2:]
            else:
                tail = (keep.shape[1], keep.shape[2] // 2)
                blocks.append(tail)
                spots.append([(0, 0), (0, 1)])
                units.append(1)
        self.unit_count, self.tail = sum(units), tail
        return self.depart(arrays, blocks, spots, units, after, "sum_first")

    def depart(self, arrays, blocks, spots, units, after, name):
        low_bit, high_bit = 1 + self.turn, self.bits - self.turn
        (a_keep, a_send, b_keep, b_send), self.done = split_call(
            self.place, arrays, blocks, spots, units, self.tail, self.count, low_bit, high_bit,
            after, name,
        )
        self.mine = [a_keep, b_keep]
        self.flight = [swap(a_send, "bucket", 1 << low_bit), swap(b_send, "bucket", 1 << high_bit)]
        self.turn += 1
        self.count //= 2
        return self.done

    def second(self, *after):
        while self.turn < self.bits:
            (am, bm), (ag, bg) = self.mine, self.flight
            spots = [[(0, 0, 0), (0, 0, 0)]]
            block = (self.unit_count,) + self.tail
            arrays = [am, ag, am, ag, bm, bg, bm, bg]
            self.depart(arrays, [block], spots, [self.unit_count], after, "sum_second")
        return self.done


class Cross:
    def __init__(self, packages, *after):
        self.place = packages[0].place
        self.kinds = [p.kinds for p in packages]
        unit, width = packages[0].tail
        self.tiles = sum(4 if by_rows else 2 for kinds in self.kinds for by_rows in kinds)
        self.tail = (unit // 4, width)
        arrays = []
        for p in packages:
            arrays += [p.mine[0], p.flight[0], p.mine[1], p.flight[1]]
        shape = jax.ShapeDtypeStruct((2, self.tiles) + self.tail, BF16)
        (self.mine, send), self.done = small_call(
            functools.partial(cross_kernel, self.kinds), self.place, arrays, shape, after, "cross"
        )
        self.flight = swap(send, "seq", 1)

    def last(self, *after):
        shape = jax.ShapeDtypeStruct((self.tiles,) + self.tail, BF16)
        (self.mine, send), self.done = small_call(
            last_kernel, self.place, [self.mine, self.flight], shape, after, "last"
        )
        self.flight = swap(send, "seq", 2)
        return self.done

    def results(self):
        total = self.mine.astype(F32) + self.flight.astype(F32)
        out, tile = [], 0
        for kinds in self.kinds:
            for by_rows in kinds:
                if by_rows:
                    out.append(total[tile : tile + 4].reshape(-1, self.tail[1]))
                    tile += 4
                else:
                    out.append(jnp.concatenate([total[tile], total[tile + 1]], 1))
                    tile += 2
        return out


def notes_kernel(blocks, early_ref, late_ref, early_cond, late_cond, out_ref, early_sum, late_sum):
    width = early_ref.shape[1]
    for part in range(6):
        if part < 2:
            ref, cond, count, which = late_ref, late_cond, 2, part
        else:
            ref, cond, count, which = early_ref, early_cond, 4, part - 2
        inside = lax.broadcasted_iota(jnp.int32, cond.shape, 0) % ref_pitch(ref, early_ref, late_ref)
        mine = (inside % count == which) & (inside < count * blocks)
        picked = jnp.where(mine, cond[...].astype(F32), 0.0).astype(BF16)
        out_ref[:, part * width : (part + 1) * width] = contract(picked, ref[...], 0, 0)
    for ref, total in ((early_ref, early_sum), (late_ref, late_sum)):
        pitch = ref_pitch(ref, early_ref, late_ref)
        shape = (NOTES, ref.shape[0])
        kind = lax.broadcasted_iota(jnp.int32, shape, 0)
        row = lax.broadcasted_iota(jnp.int32, shape, 1) % pitch
        total[...] = contract(jnp.where(kind == row, 1.0, 0.0).astype(BF16), ref[...], 1, 0)


def ref_pitch(ref, early_ref, late_ref):
    return NOTES if ref is early_ref else NOTES * late_ref.shape[0] // early_ref.shape[0]


def notes_part(early, late, early_cond, late_cond, blocks):
    width = early.shape[1]
    return launch(
        functools.partial(notes_kernel, blocks),
        [
            like(F32, early_cond.shape[1], 6 * width),
            like(F32, NOTES, width),
            like(F32, NOTES, width),
        ],
        in_specs=vmem_specs(4),
        out_specs=vmem_specs(3),
        vmem=32,
        micros=3,
        name="notes_part",
    )(early, late, early_cond, late_cond)[0]


def on_device(
    tokens,
    segment,
    keep_route,
    condition,
    group_bucket,
    head_mask,
    channel_mask,
    ada_weight,
    ada_bias,
    qkv_weight,
    query_bias,
    value_bias,
    proj_weight,
    proj_bias,
    inner_weight,
    inner_bias,
    outer_weight,
    outer_bias,
    cotangent,
):
    rows, width = tokens.shape
    slots = condition.shape[0]
    hidden = inner_weight.shape[1]
    group_count = lax.axis_size("bucket")
    seq_count = lax.axis_size("seq")
    bucket = lax.axis_index("bucket")
    seq = lax.axis_index("seq")
    core = bucket % 2
    piece = rows // slots
    block = piece * seq_count
    blocks = rows // block
    place = jnp.stack([core, seq, bucket]).astype(jnp.int32)
    row_share = width // group_count
    aligned = row_share % 16 == 0

    def turned(array):
        split = array.reshape(group_count // 2, 2, row_share, rows)
        if aligned:
            return split
        keep, send = split_bit(split, 1, core)
        return jnp.stack([keep, send]).reshape(1, 2, width // 2, rows)

    turned_core = place[:1] if aligned else jnp.zeros((1,), jnp.int32)

    seg_other = swap(segment, "bucket", 1)
    bucket_other = swap(group_bucket, "bucket", 1)
    tokens_own = tokens.reshape(slots, piece, width)
    tokens_other = swap(tokens_own, "bucket", 1)
    cond_other = swap(condition, "bucket", 1)
    route_columns = jnp.broadcast_to(keep_route.astype(BF16)[:, None], (rows, LANES))
    payload = jnp.concatenate([cotangent, route_columns], 1).reshape(slots, piece, width + LANES)
    payload_other = swap(payload, "bucket", 1)

    (
        send_which, send_index, back_which, back_index, cond_which, cond_row, flags, keep_heads,
        keep_channels,
    ) = make_plan(
        place, segment, seg_other, group_bucket, bucket_other, head_mask, channel_mask, slots,
        piece, seq_count, blocks,
    )

    def bring(pieces):
        return [pieces[0]] + [swap(pieces[k], "seq", k) for k in range(1, seq_count)]

    x_sent, x_mark = send_blocks(tokens_own, tokens_other, send_which, send_index, seq_count, blocks)
    x_parts = bring(x_sent)
    mod, cond_act = modulate(
        cond_which, cond_row, condition, cond_other, ada_weight, ada_bias, blocks, width
    )
    payload_sent, _ = send_blocks(
        payload, payload_other, send_which, send_index, seq_count, blocks, (x_parts[3],)
    )
    payload_parts = bring(payload_sent)
    pair_bias = jnp.concatenate([jnp.zeros_like(value_bias), value_bias])[None, :]
    x, normed_one, one_turned, own_kv = enter(x_parts, mod, qkv_weight, pair_bias, blocks)
    other_kv = swap(own_kv, "bucket", 1)
    queries = linear(normed_one, qkv_weight, query_bias, width, width // 3)
    attended, lse = attend(queries, own_kv, other_kv, flags, keep_heads, blocks)
    branch_one, middle, normed_two, two_turned, att_turned, grad_branch_two, grad_outer_bias = (
        middle_part(payload_parts, attended, proj_weight, proj_bias, x, mod, blocks)
    )

    share = hidden // group_count
    by_rows = (group_count // 2, row_share, -1)
    chunk = 2 * width // 3
    feed_args = (
        turned_core, keep_channels, normed_two, grad_branch_two, turned(two_turned),
        inner_bias[None, :], inner_weight, outer_weight, blocks, chunk, FEED_SUB,
    )
    (branch_two, grad_two, act_a, wi_keep, wi_send, hidden_a), _ = feed(*feed_args, 0, 3)
    inner = Package(place, (wi_keep.reshape(by_rows), wi_send.reshape(by_rows)))
    (branch_two, grad_two, act_b, wi_keep, wi_send, hidden_b), mark = feed(
        *feed_args, 3, 3, (branch_two, grad_two)
    )
    mark = inner.first(mark)
    (wo_keep, wo_send), mark = outer_part(
        place[:1], [act_a, act_b], grad_branch_two, share, width, (mark,)
    )
    by_units = (group_count // 2, 4, share // 4, width)
    rest = Package(
        place,
        (wi_keep.reshape(by_rows), wi_send.reshape(by_rows)),
        (wo_keep.reshape(by_units), wo_send.reshape(by_units)),
    )
    (out_stay, out_odd, out_even, grad_middle, grad_branch_one, grad_attended, delta), mark = (
        turn_part(
            payload_parts, keep_heads, branch_two, grad_two, middle, branch_one, attended, mod,
            outer_bias, proj_weight, cond_act, (grad_outer_bias, hidden_a, hidden_b), blocks,
            (mark,),
        )
    )
    mark = inner.second(mark)
    mark = rest.first(mark)
    out_near = swap(out_odd, "seq", 1)

    (grad_queries, grad_own, grad_other), mark = attend_back(
        queries, own_kv, other_kv, grad_attended, lse, delta, flags, keep_heads, blocks, (mark,)
    )
    grad_got = swap(grad_other, "bucket", 1)
    out_relay, mark = relay(out_even, out_odd, out_near, (mark,))
    out_far = swap(out_relay, "seq", 2)
    inner_cross = Cross([inner], mark)
    (pq_keep, pq_send, grad_one_part, query_sum), mark = query_back(
        turned_core, turned(att_turned), turned(one_turned), grad_branch_one, grad_queries,
        qkv_weight, (inner_cross.done,),
    )
    pq = Package(place, (pq_keep.reshape(by_rows), pq_send.reshape(by_rows)))
    mark = rest.second(mark)
    mark = inner_cross.last(mark)
    (kv_keep, kv_send, x_stay, x_odd, x_even), mark = leave(
        turned_core, turned(one_turned), grad_own, grad_got, qkv_weight, grad_one_part, x,
        grad_middle, mod, query_sum, blocks, piece, (mark,),
    )
    kv = Package(place, (kv_keep.reshape(by_rows), kv_send.reshape(by_rows)))
    x_near = swap(x_odd, "seq", 1)

    mark = pq.first(mark)
    (out_own, early), mark = collect(out_stay, out_odd, out_near, out_far, (mark,))
    out_other = swap(out_own, "bucket", 1)
    early_all = lax.all_gather(early, "bucket", axis=0, tiled=True)
    mark = kv.first(mark)
    x_relay, mark = relay(x_even, x_odd, x_near, (mark,))
    x_far = swap(x_relay, "seq", 2)
    rest_cross = Cross([rest], mark)
    mark = pq.second(rest_cross.done)
    block_out, mark = pick_blocks(out_own, out_other, back_which, back_index, BF16, (mark,))
    mark = kv.second(mark)
    mark = rest_cross.last(mark)
    (x_own, late), mark = collect(x_stay, x_odd, x_near, x_far, (mark,))
    x_other = swap(x_own, "bucket", 1)
    pq_cross = Cross([pq], mark)
    half = NOTES // 2
    late = late.reshape(seq_count, NOTES, width)[:, :half].reshape(seq_count * half, width)
    late_all = lax.all_gather(late, "bucket", axis=0, tiled=True)
    kv_cross = Cross([kv], pq_cross.done)
    grad_tokens, mark = pick_blocks(
        x_own, x_other, back_which, back_index, F32, (kv_cross.done,)
    )
    mark = pq_cross.last(mark)
    mark = kv_cross.last(mark)
    block_out = block_out.reshape(rows, width)
    grad_tokens = grad_tokens.reshape(rows, width)
    (inner_a,) = inner_cross.results()
    inner_b, grad_outer_weight = rest_cross.results()
    grad_inner_weight = jnp.concatenate([inner_a, inner_b], 1)
    (proj_query,) = pq_cross.results()
    grad_proj_weight = proj_query[:, :width]
    grad_qkv_weight = jnp.concatenate([proj_query[:, width:], *kv_cross.results()], 1)

    spot = bucket * seq_count + seq
    device_count = group_count * seq_count
    columns = width // device_count
    cond_mine = lax.dynamic_slice_in_dim(early_all, spot * columns, columns, 1)
    cond_mine = cond_mine.reshape(device_count, NOTES, columns)[:, NOTES - blocks :]

    def at_rows(parts, pitch):
        spread = jnp.broadcast_to(
            cond_mine[:, :, None, :], (device_count, blocks, parts, columns)
        ).reshape(device_count, blocks * parts, columns)
        rest = jnp.zeros((device_count, pitch - blocks * parts, columns), BF16)
        return jnp.concatenate([spread, rest], 1).reshape(device_count * pitch, columns)

    grad_ada_weight, early_sum, late_sum = notes_part(
        early_all, late_all, at_rows(4, NOTES), at_rows(2, half), blocks
    )

    def own_part(array):
        array = array.reshape(-1)
        size = array.shape[0] // device_count
        return lax.dynamic_slice_in_dim(array, spot * size, size, 0)

    ada_rows = jnp.concatenate(
        [
            sum(late_sum[2 * s : 2 * s + 2] for s in range(blocks)),
            sum(early_sum[4 * s : 4 * s + 4] for s in range(blocks)),
        ],
        0,
    )
    at = 4 * blocks
    return (
        block_out,
        grad_tokens,
        grad_ada_weight,
        own_part(ada_rows),
        grad_qkv_weight,
        own_part(late_sum[2 * blocks]),
        own_part(late_sum[2 * blocks + 1]),
        grad_proj_weight,
        own_part(early_sum[at]),
        grad_inner_weight,
        own_part(early_sum[at + 2 : at + 6]),
        grad_outer_weight,
        own_part(early_sum[at + 1]),
    )


def solution(mesh):
    split = P(("bucket", "seq"))
    split_rows = P(("bucket", "seq"), None)
    return jax.shard_map(
        on_device,
        mesh=mesh,
        in_specs=(split_rows, split, split, P("bucket", None), P("bucket"))
        + (P(),) * 13
        + (split_rows,),
        out_specs=(
            split_rows,
            split_rows,
            split_rows,
            split,
            split_rows,
            split,
            split,
            split_rows,
            split,
            split_rows,
            split,
            split_rows,
            split,
        ),
        check_vma=False,
    )
```

```python
import functools

import jax
import jax.numpy as jnp
from jax import lax
from jax.experimental import pallas as pl
from jax.experimental.pallas import tpu as pltpu
from jax.sharding import PartitionSpec as P

EPSILON = 1e-06
LOG2E = 1.4426950408889634
LANES = 128
NOTES = 16
FEED_VMEM = 60
FEED_SUB = 768
GELU_A = 0.7978845608028654
GELU_B = 0.044715
F32 = jnp.float32
BF16 = jnp.bfloat16


def contract(left, right, left_dim, right_dim, out=F32):
    return lax.dot_general(
        left, right, (((left_dim,), (right_dim,)), ((), ())), preferred_element_type=out
    )


def swap(array, axis, bit):
    size = lax.axis_size(axis)
    return lax.ppermute(array, axis, [(i, i ^ bit) for i in range(size)])


def launch(
    body, out_shape, *, in_specs, out_specs, name, after=(), grid=(), prefetch=0, scratch=(),
    aliases=None, vmem=56, micros=0,
):
    lead = prefetch + len(in_specs)
    waits, outs = len(after), len(out_shape)

    def kernel(*refs):
        rest = refs[lead + waits :]
        body(*refs[:lead], *rest[:outs], *rest[outs + 1 :])
        rest[outs][...] = jnp.zeros(rest[outs].shape, F32)

    token = (8, LANES)
    specs = dict(
        in_specs=list(in_specs) + [pl.BlockSpec(memory_space=pl.ANY)] * waits,
        scratch_shapes=list(scratch),
    )
    if grid:
        specs = dict(
            grid_spec=pltpu.PrefetchScalarGridSpec(
                num_scalar_prefetch=prefetch,
                grid=grid,
                out_specs=list(out_specs) + [pl.BlockSpec(token, lambda *i: (0, 0))],
                **specs,
            )
        )
    else:
        specs["out_specs"] = list(out_specs) + [pl.BlockSpec(memory_space=pltpu.VMEM)]
    call = pl.pallas_call(
        kernel,
        out_shape=list(out_shape) + [jax.ShapeDtypeStruct(token, F32)],
        input_output_aliases=aliases or {},
        compiler_params=pltpu.CompilerParams(vmem_limit_bytes=vmem * 1024 * 1024),
        cost_estimate=pl.CostEstimate(
            flops=int(micros * 1000000000), bytes_accessed=0, transcendentals=0
        ),
        name=name,
        **specs,
    )

    def run(*operands):
        *results, mark = call(*operands, *after)
        return results, mark

    return run


def vmem_specs(count):
    return [pl.BlockSpec(memory_space=pltpu.VMEM)] * count


def smem_specs(count):
    return [pl.BlockSpec(memory_space=pltpu.SMEM)] * count


def like(dtype, *shape):
    return jax.ShapeDtypeStruct(shape, dtype)


def hold_kernel(array_ref, *refs):
    pass


def hold(array, *after):
    anywhere = [pl.BlockSpec(memory_space=pl.ANY)]
    return pl.pallas_call(
        hold_kernel,
        in_specs=anywhere * (1 + len(after)),
        out_specs=anywhere[0],
        out_shape=like(array.dtype, *array.shape),
        input_output_aliases={0: 0},
        cost_estimate=pl.CostEstimate(flops=0, bytes_accessed=0, transcendentals=0),
        name="hold",
    )(array, *after)


def plan_kernel(
    slots, piece, chips, blocks, place_ref, seg_own, seg_other, bucket_own, bucket_other,
    head_mask, channel_mask, send_which, send_index, back_which, back_index, cond_which,
    cond_row, flags, keep_heads, keep_channels, order_ref, rank_ref, id_ref, long_ref,
):
    core = place_ref[0]
    seq = place_ref[1]
    total = 2 * slots
    ids, keys = [], []
    for i in range(total):
        at = (i % slots) * piece
        ids.append(jnp.where(core == i // slots, seg_own[at], seg_other[at]))
    for i in range(total):
        base = (i // slots) * slots
        equal = jnp.int32(0)
        for j in range(slots):
            equal += jnp.where(ids[base + j] == ids[i], 1, 0)
        is_long = jnp.where(equal > 1, 1, 0)
        id_ref[i] = ids[i]
        long_ref[i] = is_long
        keys.append(jnp.where(is_long == 1, i, total + i))
    for i in range(total):
        rank = jnp.int32(0)
        for j in range(total):
            rank += jnp.where(keys[j] < keys[i], 1, 0)
        rank_ref[i] = rank
        order_ref[rank] = jnp.int32(i)
    for k in range(chips):
        for s in range(blocks):
            item = order_ref[((seq ^ k) * 2 + core) * blocks + s]
            send_which[k * blocks + s] = jnp.where(item // slots == core, 0, 1)
            send_index[k * blocks + s] = item % slots
    for j in range(slots):
        rank = rank_ref[core * slots + j]
        back_which[j] = jnp.where((rank // blocks) % 2 == core, 0, 1)
        back_index[j] = ((rank // (2 * blocks)) ^ seq) * blocks + rank % blocks
    flags[0] = long_ref[order_ref[seq * 2 * blocks]]
    flags[1] = core
    heads = head_mask.shape[1]
    groups = channel_mask.shape[1]
    for s in range(blocks):
        item = order_ref[(seq * 2 + core) * blocks + s]
        other = jnp.where(item // slots == core, 0, 1)
        cond_which[s] = other
        cond_row[s] = id_ref[item]
        step = jnp.where(other == 0, bucket_own[0], bucket_other[0])
        for h in range(heads):
            keep_heads[s * heads + h] = head_mask[step, h]
        for f in range(groups):
            keep_channels[s * groups + f] = channel_mask[step, f]


def make_plan(place, segment, seg_other, bucket, bucket_other, head_mask, channel_mask, slots, piece,
              chips, blocks):
    smem = pl.BlockSpec(memory_space=pltpu.SMEM)
    sizes = [chips * blocks] * 2 + [slots] * 2 + [blocks] * 2 + [2]
    sizes += [blocks * head_mask.shape[1], blocks * channel_mask.shape[1]]
    return pl.pallas_call(
        functools.partial(plan_kernel, slots, piece, chips, blocks),
        in_specs=[smem] * 7,
        out_specs=[smem] * 9,
        out_shape=[jax.ShapeDtypeStruct((n,), jnp.int32) for n in sizes],
        scratch_shapes=[pltpu.SMEM((2 * slots,), jnp.int32)] * 4,
        cost_estimate=pl.CostEstimate(flops=0, bytes_accessed=8000000, transcendentals=0),
        name="make_plan",
    )(place, segment, seg_other, bucket, bucket_other, head_mask, channel_mask)


def send_kernel(blocks, which_ref, index_ref, own_ref, other_ref, *outs):
    for m in range(len(outs) * blocks):

        @pl.when(which_ref[m] == 0)
        def _():
            outs[m // blocks][m % blocks] = own_ref[index_ref[m]]

        @pl.when(which_ref[m] != 0)
        def _():
            outs[m // blocks][m % blocks] = other_ref[index_ref[m]]


def send_blocks(own, other, which, index, chips, blocks, after=()):
    _, rows, width = own.shape
    return launch(
        functools.partial(send_kernel, blocks),
        [like(own.dtype, blocks, rows, width)] * chips,
        in_specs=smem_specs(2) + vmem_specs(2),
        out_specs=vmem_specs(chips),
        after=after,
        vmem=16,
        name="send_blocks",
    )(which, index, own, other)


def pick_kernel(which_ref, index_ref, own_ref, other_ref, out_ref):
    for m in range(out_ref.shape[0]):

        @pl.when(which_ref[m] == 0)
        def _():
            out_ref[m] = own_ref[index_ref[m]].astype(out_ref.dtype)

        @pl.when(which_ref[m] != 0)
        def _():
            out_ref[m] = other_ref[index_ref[m]].astype(out_ref.dtype)


def pick_blocks(own, other, which, index, out_dtype, after=(), micros=0):
    _, rows, width = own.shape
    (out,), mark = launch(
        pick_kernel,
        [like(out_dtype, index.shape[0], rows, width)],
        in_specs=smem_specs(2) + vmem_specs(2),
        out_specs=vmem_specs(1),
        after=after,
        vmem=16,
        micros=micros,
        name="pick_blocks",
    )(which, index, own, other)
    return out, mark


def leaving(k, s, value, stay_ref, odd_ref, even_ref):
    rows = value.shape[0]
    if k == 0:
        stay_ref[s] = value
        return
    target = even_ref if k == 2 else odd_ref
    first = ((k // 2 if k % 2 else 0) * stay_ref.shape[0] + s) * rows
    target[first : first + rows] = value


def leaving_shapes(blocks, piece, width):
    count = blocks * piece
    return [
        like(BF16, blocks, piece, width),
        like(BF16, 2 * count + NOTES, width),
        like(BF16, count, width),
    ]


def relay_kernel(even_ref, odd_ref, near_ref, out_ref):
    count = even_ref.shape[0]
    out_ref[:count] = even_ref[...]
    out_ref[count : 2 * count] = near_ref[count : 2 * count]
    out_ref[2 * count : 2 * count + NOTES] = odd_ref[2 * count :]
    out_ref[2 * count + NOTES :] = near_ref[2 * count :]


def relay(even, odd, near, after=(), micros=0):
    count, width = even.shape
    (out,), mark = launch(
        relay_kernel,
        [like(BF16, 2 * count + 2 * NOTES, width)],
        in_specs=vmem_specs(3),
        out_specs=vmem_specs(1),
        after=after,
        vmem=16,
        micros=micros,
        name="relay",
    )(even, odd, near)
    return out, mark


def collect_kernel(stay_ref, odd_ref, near_ref, far_ref, out_ref, notes_ref):
    blocks, rows, width = stay_ref.shape
    count = blocks * rows
    out_ref[:blocks] = stay_ref[...]
    for k, part in enumerate((near_ref[:count], far_ref[:count], far_ref[count : 2 * count])):
        out_ref[(k + 1) * blocks : (k + 2) * blocks] = part.reshape(blocks, rows, width)
    notes_ref[:NOTES] = odd_ref[2 * count :]
    notes_ref[NOTES : 2 * NOTES] = near_ref[2 * count :]
    notes_ref[2 * NOTES :] = far_ref[2 * count :]


def collect(stay, odd, near, far, after=(), micros=0):
    blocks, rows, width = stay.shape
    return launch(
        collect_kernel,
        [like(BF16, 4 * blocks, rows, width), like(BF16, 4 * NOTES, width)],
        in_specs=vmem_specs(4),
        out_specs=vmem_specs(2),
        after=after,
        vmem=16,
        micros=micros,
        name="collect",
    )(stay, odd, near, far)


def modulate_kernel(
    blocks, which_ref, row_ref, own_ref, other_ref, weight_ref, bias_ref, out_ref, act_ref, held
):
    @pl.when(pl.program_id(0) == 0)
    def _():
        slots, width = own_ref.shape
        picked = []
        for s in range(blocks):
            hot = lax.broadcasted_iota(jnp.int32, (slots, width), 0) == row_ref[s]
            source = jnp.where(which_ref[s] == 0, own_ref[...].astype(F32), other_ref[...].astype(F32))
            picked.append(jnp.sum(jnp.where(hot, source, 0.0), 0, keepdims=True))
        picked.append(jnp.zeros((16 - blocks, width), F32))
        value = jnp.concatenate(picked, 0)
        held[...] = (value / (1.0 + jnp.exp(-value))).astype(BF16)
        act_ref[...] = held[...]

    out_ref[...] = (contract(held[...], weight_ref[...], 1, 0) + bias_ref[...])[:8]


def modulate(which, row, own, other, weight, bias, blocks, chunk, after=()):
    slots, width = own.shape
    columns = weight.shape[1]
    return launch(
        functools.partial(modulate_kernel, blocks),
        [like(F32, 8, columns), like(BF16, 16, width)],
        grid=(columns // chunk,),
        in_specs=smem_specs(2)
        + [
            pl.BlockSpec((slots, width), lambda i: (0, 0)),
            pl.BlockSpec((slots, width), lambda i: (0, 0)),
            pl.BlockSpec((width, chunk), lambda i: (0, i)),
            pl.BlockSpec((1, chunk), lambda i: (0, i)),
        ],
        out_specs=[
            pl.BlockSpec((8, chunk), lambda i: (0, i)),
            pl.BlockSpec((16, width), lambda i: (0, 0)),
        ],
        scratch=[pltpu.VMEM((16, width), BF16)],
        after=after,
        vmem=32,
        micros=0,
        name="modulate",
    )(which, row, own, other, weight, bias[None, :])[0]


def norm_parts(value):
    center = value - jnp.mean(value, -1, keepdims=True)
    spread = jnp.mean(center * center, -1, keepdims=True)
    inverse = lax.rsqrt(spread + EPSILON)
    return center * inverse, inverse


def norm_back(grad, normed, inverse, scale):
    scaled = grad * (1.0 + scale)
    mean_one = jnp.mean(scaled, -1, keepdims=True)
    mean_two = jnp.mean(scaled * normed, -1, keepdims=True)
    return inverse * (scaled - mean_one - normed * mean_two)


def mod_row(mod_ref, index, part, width):
    return mod_ref[index : index + 1, part * width : (part + 1) * width]


def enter_kernel(blocks, *refs):
    parts = refs[:-8]
    mod_ref, weight_ref, bias_ref, x_ref, one_ref, turned_ref, kv_ref, held = refs[-8:]
    _, piece, width = parts[0].shape
    block = held.shape[0] // blocks

    @pl.when(pl.program_id(0) == 0)
    def _():
        for s in range(blocks):
            for k, part in enumerate(parts):
                first = s * block + k * piece
                x = part[s]
                x_ref[first : first + piece] = x
                normed, _ = norm_parts(x.astype(F32))
                one = normed * (1.0 + mod_row(mod_ref, s, 1, width)) + mod_row(mod_ref, s, 0, width)
                held[first : first + piece] = one.astype(BF16)
        one_ref[...] = held[...]
        turned_ref[...] = held[...].T

    kv_ref[...] = (contract(held[...], weight_ref[...], 1, 0) + bias_ref[...]).astype(BF16)


def enter(parts, mod, weight, bias, blocks):
    _, piece, width = parts[0].shape
    rows = piece * blocks * len(parts)
    const = lambda shape: pl.BlockSpec(shape, lambda i: (0,) * len(shape))
    return pl.pallas_call(
        functools.partial(enter_kernel, blocks),
        grid=(2,),
        in_specs=[const(p.shape) for p in parts]
        + [
            const((8, 2 * width)),
            pl.BlockSpec((width, width), lambda i: (0, 1 + i)),
            pl.BlockSpec((1, width), lambda i: (0, i)),
        ],
        out_specs=[
            const((rows, width)),
            const((rows, width)),
            const((width, rows)),
            pl.BlockSpec((rows, width), lambda i: (0, i)),
        ],
        out_shape=[
            jax.ShapeDtypeStruct((rows, width), BF16),
            jax.ShapeDtypeStruct((rows, width), BF16),
            jax.ShapeDtypeStruct((width, rows), BF16),
            jax.ShapeDtypeStruct((rows, 2 * width), BF16),
        ],
        scratch_shapes=[pltpu.VMEM((rows, width), BF16)],
        compiler_params=pltpu.CompilerParams(vmem_limit_bytes=48 * 1024 * 1024),
        cost_estimate=pl.CostEstimate(
            flops=8 * rows * width * width, bytes_accessed=12 * width * width, transcendentals=0
        ),
        name="enter",
    )(*parts, mod, weight, bias)


def linear_kernel(x_ref, weight_ref, bias_ref, out_ref):
    out_ref[...] = (contract(x_ref[...], weight_ref[...], 1, 0) + bias_ref[...]).astype(out_ref.dtype)


def linear(x, weight, bias, columns, chunk):
    rows, width = x.shape
    return pl.pallas_call(
        linear_kernel,
        grid=(columns // chunk,),
        in_specs=[
            pl.BlockSpec((rows, width), lambda i: (0, 0)),
            pl.BlockSpec((width, chunk), lambda i: (0, i)),
            pl.BlockSpec((1, chunk), lambda i: (0, i)),
        ],
        out_specs=pl.BlockSpec((rows, chunk), lambda i: (0, i)),
        out_shape=jax.ShapeDtypeStruct((rows, columns), BF16),
        compiler_params=pltpu.CompilerParams(vmem_limit_bytes=32 * 1024 * 1024),
        cost_estimate=pl.CostEstimate(
            flops=4 * rows * width * columns, bytes_accessed=8 * width * columns, transcendentals=0
        ),
        name="linear",
    )(x, weight, bias[None, :])


def middle_kernel(blocks, *refs):
    parts = refs[:-12]
    (
        att_ref, weight_ref, bias_ref, x_ref, mod_ref,
        branch_ref, middle_ref, two_ref, two_turned, att_turned, grad_ref, bias_grad,
    ) = refs[-12:]
    rows, width = x_ref.shape
    block = rows // blocks
    piece = parts[0].shape[1]
    att_turned[...] = att_ref[...].T
    total = jnp.zeros((1, width), F32)
    for s in range(blocks):
        part = slice(s * block, (s + 1) * block)
        branch = contract(att_ref[part], weight_ref[...], 1, 0) + bias_ref[...]
        branch_ref[part] = branch
        middle = x_ref[part].astype(F32) + mod_row(mod_ref, s, 2, width) * branch
        middle_ref[part] = middle
        normed, _ = norm_parts(middle)
        two_ref[part] = (
            normed * (1.0 + mod_row(mod_ref, s, 4, width)) + mod_row(mod_ref, s, 3, width)
        ).astype(BF16)
        for k, source in enumerate(parts):
            first = s * block + k * piece
            payload = source[s].astype(F32)
            grad = (payload[:, width : width + 1] * mod_row(mod_ref, s, 5, width) * payload[:, :width]).astype(BF16)
            grad_ref[first : first + piece] = grad
            total += jnp.sum(grad.astype(F32), 0, keepdims=True)
    two_turned[...] = two_ref[...].T
    bias_grad[...] = total


def middle_part(parts, attended, weight, bias, x, mod, blocks):
    rows, width = x.shape
    vmem = pl.BlockSpec(memory_space=pltpu.VMEM)
    return pl.pallas_call(
        functools.partial(middle_kernel, blocks),
        in_specs=[vmem] * (len(parts) + 5),
        out_specs=[vmem] * 7,
        out_shape=[
            jax.ShapeDtypeStruct((rows, width), F32),
            jax.ShapeDtypeStruct((rows, width), F32),
            jax.ShapeDtypeStruct((rows, width), BF16),
            jax.ShapeDtypeStruct((width, rows), BF16),
            jax.ShapeDtypeStruct((width, rows), BF16),
            jax.ShapeDtypeStruct((rows, width), BF16),
            jax.ShapeDtypeStruct((1, width), F32),
        ],
        compiler_params=pltpu.CompilerParams(vmem_limit_bytes=48 * 1024 * 1024),
        cost_estimate=pl.CostEstimate(
            flops=8 * rows * width * width, bytes_accessed=24 * rows * width, transcendentals=0
        ),
        name="middle_part",
    )(*parts, attended, weight, bias[None, :], x, mod)


def turn_kernel(blocks, heads, *refs):
    count = 4
    parts = refs[:count]
    (
        keep_ref, out_ref, gx_ref, middle_ref, branch_ref, att_ref, mod_ref, bias_ref, weight_ref,
        act_ref, outer_sum, *hidden_sums,
    ) = refs[count:-7]
    stay_ref, odd_ref, even_ref, grad_middle, grad_one, grad_att, delta_ref = refs[-7:]
    notes = []
    rows, width = middle_ref.shape
    block = rows // blocks
    piece = parts[0].shape[1]
    head_width = width // heads
    column_head = lax.broadcasted_iota(jnp.int32, (heads, width), 1) // head_width
    hot = (column_head == lax.broadcasted_iota(jnp.int32, (heads, width), 0)).astype(F32)
    bias_total = jnp.zeros((1, width), F32)
    for s in range(blocks):
        sums = [jnp.zeros((1, width), F32) for _ in range(4)]
        gate_one = mod_row(mod_ref, s, 2, width)
        scale_two = mod_row(mod_ref, s, 4, width)
        gate_two = mod_row(mod_ref, s, 5, width)
        for k, source in enumerate(parts):
            first = s * block + k * piece
            part = slice(first, first + piece)
            payload = source[s].astype(F32)
            upstream = payload[:, :width]
            route = payload[:, width : width + 1]
            middle = middle_ref[part]
            branch_two = route * (out_ref[part] + bias_ref[...])
            leaving(k, s, (middle + gate_two * branch_two).astype(BF16), stay_ref, odd_ref, even_ref)
            sums[3] += jnp.sum(branch_two * upstream, 0, keepdims=True)
            grad_two = gx_ref[part]
            normed, inverse = norm_parts(middle)
            sums[1] += jnp.sum(grad_two, 0, keepdims=True)
            sums[2] += jnp.sum(grad_two * normed, 0, keepdims=True)
            grad = upstream + norm_back(grad_two, normed, inverse, scale_two)
            grad_middle[part] = grad
            sums[0] += jnp.sum(grad * branch_ref[part], 0, keepdims=True)
            low = (gate_one * grad).astype(BF16)
            grad_one[part] = low
            bias_total += jnp.sum(low.astype(F32), 0, keepdims=True)
        notes += sums
        part = slice(s * block, (s + 1) * block)
        row = jnp.zeros((1, width), F32)
        for h in range(heads):
            row = jnp.where(
                hot[h : h + 1] > 0.5, keep_ref[s * heads + h].astype(F32), row
            )
        low = contract(grad_one[part], weight_ref[...], 1, 1).astype(BF16).astype(F32) * row
        grad_att[part] = low.astype(BF16)
        delta_ref[:, part] = lax.dot_general(
            hot,
            low * att_ref[part].astype(F32),
            (((1,), (1,)), ((), ())),
            precision=lax.Precision.HIGHEST,
            preferred_element_type=F32,
        )
    notes.append(bias_total)
    notes.append(outer_sum[...])
    for ref in hidden_sums:
        notes += [ref[:, lo : lo + width] for lo in range(0, ref.shape[1], width)]
    notes.append(act_ref[:blocks].astype(F32))
    odd_ref[2 * blocks * piece :] = jnp.concatenate(notes, 0).astype(BF16)


def turn_part(
    parts, keep, out, gx, middle, branch, attended, mod, bias, weight, act, sums, blocks, after=()
):
    rows, width = middle.shape
    heads = keep.shape[0] // blocks
    return launch(
        functools.partial(turn_kernel, blocks, heads),
        leaving_shapes(blocks, parts[0].shape[1], width)
        + [
            like(F32, rows, width),
            like(BF16, rows, width),
            like(BF16, rows, width),
            like(F32, heads, rows),
        ],
        in_specs=vmem_specs(len(parts)) + smem_specs(1) + vmem_specs(9 + len(sums)),
        out_specs=vmem_specs(7),
        after=after,
        vmem=48,
        micros=500,
        name="turn_part",
    )(*parts, keep, out, gx, middle, branch, attended, mod, bias[None, :], weight, act, *sums)


def query_back_kernel(
    core_ref, proj_keep, proj_send, one_keep, one_send, grad_one, grad_q, weight_ref, *refs
):
    keep_ref, send_ref, gx_ref, sum_ref = refs[-4:]
    width = grad_q.shape[1]
    half = keep_ref.shape[0]
    rows = grad_q.shape[0]
    turned = lambda ref: ref[...].reshape(half, rows)
    keep_ref[:, :width] = contract(turned(proj_keep), grad_one[...], 1, 0).astype(BF16)
    send_ref[:, :width] = contract(turned(proj_send), grad_one[...], 1, 0).astype(BF16)
    keep_ref[:, width:] = contract(turned(one_keep), grad_q[...], 1, 0).astype(BF16)
    send_ref[:, width:] = contract(turned(one_send), grad_q[...], 1, 0).astype(BF16)
    gx_ref[...] = contract(grad_q[...], weight_ref[...], 1, 1)
    sum_ref[...] = jnp.sum(grad_q[...].astype(F32), 0, keepdims=True)


def turned_specs(array):
    pairs, _, share, rows = array.shape
    keep = pl.BlockSpec((pairs, None, share, rows), lambda i, c: (0, c[0], 0, 0))
    send = pl.BlockSpec((pairs, None, share, rows), lambda i, c: (0, 1 - c[0], 0, 0))
    return [keep, send]


def query_back(core, att_turned, one_turned, grad_one, grad_q, weight, after=()):
    rows, width = grad_q.shape
    half = width // 2
    const = lambda shape: pl.BlockSpec(shape, lambda i, c: (0,) * len(shape))
    return launch(
        query_back_kernel,
        [
            like(BF16, half, 2 * width),
            like(BF16, half, 2 * width),
            like(F32, rows, width),
            like(F32, 1, width),
        ],
        prefetch=1,
        grid=(1,),
        in_specs=turned_specs(att_turned)
        + turned_specs(one_turned)
        + [const((rows, width)), const((rows, width)), const((width, width))],
        out_specs=[
            const((half, 2 * width)),
            const((half, 2 * width)),
            const((rows, width)),
            const((1, width)),
        ],
        after=after,
        micros=0,
        name="query_back",
    )(core, att_turned, att_turned, one_turned, one_turned, grad_one, grad_q, weight)


def leave_kernel(
    blocks, core_ref, one_keep, one_send, own_ref, got_ref, weight_ref, gx_in, x_ref, middle_ref,
    mod_ref, query_sum, keep_ref, send_ref, stay_ref, odd_ref, even_ref, total, grads,
):
    piece = stay_ref.shape[1]
    rows, width = x_ref.shape
    half = keep_ref.shape[0]
    block = rows // blocks
    step = pl.program_id(0)
    turned = lambda ref: ref[...].reshape(half, rows)
    grads[...] = (own_ref[...].astype(F32) + got_ref[...].astype(F32)).astype(BF16)
    keep_ref[...] = contract(turned(one_keep), grads[...], 1, 0).astype(BF16)
    send_ref[...] = contract(turned(one_send), grads[...], 1, 0).astype(BF16)

    @pl.when(step == 0)
    def _():
        total[...] = gx_in[...] + contract(grads[...], weight_ref[...], 1, 1)

    @pl.when(step == 1)
    def _():
        notes = []
        for s in range(blocks):
            part = slice(s * block, (s + 1) * block)
            grad = total[part] + contract(grads[part], weight_ref[...], 1, 1)
            normed, inverse = norm_parts(x_ref[part].astype(F32))
            notes.append(jnp.sum(grad, 0, keepdims=True))
            notes.append(jnp.sum(grad * normed, 0, keepdims=True))
            back = norm_back(grad, normed, inverse, mod_row(mod_ref, s, 1, width))
            low = (middle_ref[part] + back).astype(BF16)
            for k in range(block // piece):
                leaving(k, s, low[k * piece : (k + 1) * piece], stay_ref, odd_ref, even_ref)
        notes.append(query_sum[...])
        notes.append(jnp.sum(grads[...].astype(F32), 0, keepdims=True))
        notes.append(jnp.zeros((NOTES - 2 * blocks - 2, width), F32))
        odd_ref[2 * blocks * piece :] = jnp.concatenate(notes, 0).astype(BF16)


def leave(
    core, one_turned, own, got, weight, gx, x, grad_middle, mod, query_sum, blocks, piece, after=()
):
    rows, width = x.shape
    half = width // 2
    const = lambda shape: pl.BlockSpec(shape, lambda i, c: (0,) * len(shape))
    once = lambda shape: pl.BlockSpec(
        shape, lambda i, c: (0,) * len(shape), pipeline_mode=pl.Buffered(1)
    )
    shapes = leaving_shapes(blocks, piece, width)
    return launch(
        functools.partial(leave_kernel, blocks),
        [like(BF16, half, 2 * width), like(BF16, half, 2 * width)] + shapes,
        prefetch=1,
        grid=(2,),
        in_specs=turned_specs(one_turned)
        + [
            pl.BlockSpec((rows, width), lambda i, c: (0, i)),
            pl.BlockSpec((rows, width), lambda i, c: (0, i)),
            pl.BlockSpec((width, width), lambda i, c: (0, 1 + i)),
            once((rows, width)),
            once((rows, width)),
            once((rows, width)),
            once((8, 2 * width)),
            once((1, width)),
        ],
        out_specs=[
            pl.BlockSpec((half, width), lambda i, c: (0, i)),
            pl.BlockSpec((half, width), lambda i, c: (0, i)),
        ]
        + [const(s.shape) for s in shapes],
        scratch=[pltpu.VMEM((rows, width), F32), pltpu.VMEM((rows, width), BF16)],
        after=after,
        micros=500,
        name="leave",
    )(core, one_turned, one_turned, own, got, weight, gx, x, grad_middle, mod, query_sum)


def head_columns(ref, start, head_width):
    part = ref[:, start : start + head_width]
    return jnp.concatenate(
        [part, jnp.zeros((part.shape[0], LANES - head_width), part.dtype)], axis=1
    )


def attend_kernel(
    heads, head_width, blocks, long_ref, keep_ref, q_ref, own_ref, other_ref, out_ref, lse_ref,
    qh, kh, vh, oh,
):
    rows, width = q_ref.shape
    block = rows // blocks
    factor = head_width**-0.5 * LOG2E
    is_long = long_ref[0] == 1
    for h in range(heads):
        start = h * head_width
        qh[h] = head_columns(q_ref, start, head_width)
        kh[h, :rows] = head_columns(own_ref, start, head_width)
        vh[h, :rows] = head_columns(own_ref, width + start, head_width)

    @pl.when(is_long)
    def _():
        for h in range(heads):
            start = h * head_width
            kh[h, rows:] = head_columns(other_ref, start, head_width)
            vh[h, rows:] = head_columns(other_ref, width + start, head_width)

    def one(h, first, count, key_first, key_count):
        queries = qh[h, pl.ds(first, count), :]
        keys = kh[h, pl.ds(key_first, key_count), :]
        values = vh[h, pl.ds(key_first, key_count), :]
        scores = contract(keys, queries, 1, 1)
        top = jnp.max(scores, 0, keepdims=True)
        exponent = jnp.exp2((scores - top) * factor)
        total = jnp.sum(exponent, 0, keepdims=True)
        mixed = contract(values, exponent.astype(BF16), 0, 0) * (1.0 / total)
        oh[h, pl.ds(first, count), :] = mixed.T.astype(BF16)
        lse_ref[pl.ds(h, 1), pl.ds(first, count)] = top * factor + jnp.log2(total)

    def loop(index, first, count, key_first, key_count):
        def body(h, carry):
            keep = keep_ref[index * heads + h] == 1

            @pl.when(keep)
            def _():
                one(h, first, count, key_first, key_count)

            @pl.when(jnp.logical_not(keep))
            def _():
                oh[h, pl.ds(first, count), :] = jnp.zeros((count, LANES), BF16)

            return carry

        lax.fori_loop(0, heads, body, 0)

    @pl.when(is_long)
    def _():
        loop(0, 0, rows, 0, 2 * rows)

    @pl.when(jnp.logical_not(is_long))
    def _():
        for index in range(blocks):
            loop(index, index * block, block, index * block, block)

    for h in range(heads):
        out_ref[:, h * head_width : (h + 1) * head_width] = oh[h, :, :head_width]


def attend(queries, own, other, long_flag, keep, blocks):
    rows, width = queries.shape
    heads = keep.shape[0] // blocks
    head_width = width // heads
    vmem = pl.BlockSpec(memory_space=pltpu.VMEM)
    smem = pl.BlockSpec(memory_space=pltpu.SMEM)
    return pl.pallas_call(
        functools.partial(attend_kernel, heads, head_width, blocks),
        in_specs=[smem, smem, vmem, vmem, vmem],
        out_specs=[vmem, vmem],
        out_shape=[
            jax.ShapeDtypeStruct((rows, width), BF16),
            jax.ShapeDtypeStruct((heads, rows), F32),
        ],
        scratch_shapes=[
            pltpu.VMEM((heads, rows, LANES), BF16),
            pltpu.VMEM((heads, 2 * rows, LANES), BF16),
            pltpu.VMEM((heads, 2 * rows, LANES), BF16),
            pltpu.VMEM((heads, rows, LANES), BF16),
        ],
        compiler_params=pltpu.CompilerParams(vmem_limit_bytes=56 * 1024 * 1024),
        cost_estimate=pl.CostEstimate(
            flops=100 * rows * rows * width,
            bytes_accessed=12 * rows * width,
            transcendentals=2 * rows * rows * heads,
        ),
        name="attend",
    )(long_flag, keep, queries, own, other)


def attend_back_kernel(
    heads, head_width, blocks, long_ref, keep_ref, q_ref, own_ref, other_ref, go_ref, lse_ref,
    delta_ref, *refs,
):
    gq_ref, gown_ref, gother_ref, qh, kh, vh, gh, gqh, gkh, gvh = refs[-10:]
    rows, width = q_ref.shape
    block = rows // blocks
    scale = head_width**-0.5
    factor = scale * LOG2E
    is_long = long_ref[0] == 1
    for h in range(heads):
        start = h * head_width
        qh[h] = head_columns(q_ref, start, head_width)
        gh[h] = head_columns(go_ref, start, head_width)
        kh[h, :rows] = head_columns(own_ref, start, head_width)
        vh[h, :rows] = head_columns(own_ref, width + start, head_width)

    @pl.when(is_long)
    def _():
        for h in range(heads):
            start = h * head_width
            kh[h, rows:] = head_columns(other_ref, start, head_width)
            vh[h, rows:] = head_columns(other_ref, width + start, head_width)

    def one(h, first, count, key_first, key_count):
        queries = qh[h, pl.ds(first, count), :]
        grads = gh[h, pl.ds(first, count), :]
        keys = kh[h, pl.ds(key_first, key_count), :]
        values = vh[h, pl.ds(key_first, key_count), :]
        scores = contract(keys, queries, 1, 1)
        probs = jnp.exp2(scores * factor - lse_ref[pl.ds(h, 1), pl.ds(first, count)])
        gvh[h, pl.ds(key_first, key_count), :] = contract(
            probs.astype(BF16), grads, 1, 0
        ).astype(BF16)
        grad_probs = contract(values, grads, 1, 1)
        grad_scores = (probs * (grad_probs - delta_ref[pl.ds(h, 1), pl.ds(first, count)])).astype(BF16)
        gkh[h, pl.ds(key_first, key_count), :] = (
            contract(grad_scores, queries, 1, 0) * scale
        ).astype(BF16)
        gqh[h, pl.ds(first, count), :] = (
            (contract(keys, grad_scores, 0, 0) * scale).T
        ).astype(BF16)

    def loop(index, first, count, key_first, key_count):
        def body(h, carry):
            keep = keep_ref[index * heads + h] == 1

            @pl.when(keep)
            def _():
                one(h, first, count, key_first, key_count)

            @pl.when(jnp.logical_not(keep))
            def _():
                gqh[h, pl.ds(first, count), :] = jnp.zeros((count, LANES), BF16)
                gkh[h, pl.ds(key_first, key_count), :] = jnp.zeros((key_count, LANES), BF16)
                gvh[h, pl.ds(key_first, key_count), :] = jnp.zeros((key_count, LANES), BF16)

            return carry

        lax.fori_loop(0, heads, body, 0)

    @pl.when(is_long)
    def _():
        loop(0, 0, rows, 0, 2 * rows)
        for h in range(heads):
            start = h * head_width
            gother_ref[:, start : start + head_width] = gkh[h, rows:, :head_width]
            gother_ref[:, width + start : width + start + head_width] = gvh[h, rows:, :head_width]

    @pl.when(jnp.logical_not(is_long))
    def _():
        for index in range(blocks):
            loop(index, index * block, block, index * block, block)
        gother_ref[...] = jnp.zeros_like(gother_ref)

    for h in range(heads):
        start = h * head_width
        gq_ref[:, start : start + head_width] = gqh[h, :, :head_width]
        gown_ref[:, start : start + head_width] = gkh[h, :rows, :head_width]
        gown_ref[:, width + start : width + start + head_width] = gvh[h, :rows, :head_width]


def attend_back(queries, own, other, grad_out, lse, delta, long_flag, keep, blocks, after=()):
    rows, width = queries.shape
    heads = keep.shape[0] // blocks
    head_width = width // heads
    short = pltpu.VMEM((heads, rows, LANES), BF16)
    full = pltpu.VMEM((heads, 2 * rows, LANES), BF16)
    return launch(
        functools.partial(attend_back_kernel, heads, head_width, blocks),
        [like(BF16, rows, width), like(BF16, rows, 2 * width), like(BF16, rows, 2 * width)],
        in_specs=smem_specs(2) + vmem_specs(6),
        out_specs=vmem_specs(3),
        scratch=[short, full, full, short, short, full, full],
        after=after,
        vmem=60,
        micros=500,
        name="attend_back",
    )(long_flag, keep, queries, own, other, grad_out, lse, delta)


def feed_kernel(
    blocks, sub, group, first, resume, core_ref, keep_ref, x_ref, g_ref, xk_ref, xs_ref, bias_ref,
    wi_ref, wo_ref, *refs,
):
    act, gbefore = refs[-2:]
    out_ref, gx_ref, act_ref, wik_ref, wis_ref, gbias_ref = refs[-8:-2]
    rows, _ = x_ref.shape
    block = rows // blocks
    chunk = wi_ref.shape[1]
    half = wik_ref.shape[0]
    step = pl.program_id(0)
    groups = keep_ref.shape[0] // blocks
    turned = lambda ref: ref[...].reshape(half, rows)
    for lo in range(0, chunk, sub):
        cols = slice(lo, lo + sub)
        column_sum = jnp.zeros((1, sub), F32)
        for index in range(blocks):
            part = slice(index * block, (index + 1) * block)
            before = contract(x_ref[part], wi_ref[:, cols], 1, 0) + bias_ref[:, cols]
            grad_act = contract(g_ref[part], wo_ref[cols, :], 1, 1)
            base = index * groups + ((first + step) * chunk + lo) // group
            keep = jnp.concatenate(
                [
                    jnp.full((1, group), keep_ref[base + m].astype(F32))
                    for m in range(sub // group)
                ],
                axis=1,
            )
            square = before * before
            bend = jnp.tanh(GELU_A * before * (1.0 + GELU_B * square))
            gate = 0.5 * (1.0 + bend)
            slope = gate + (0.5 * GELU_A) * before * (1.0 - bend * bend) * (
                1.0 + (3.0 * GELU_B) * square
            )
            act[part, cols] = (before * gate * keep).astype(BF16)
            grad = (grad_act * keep * slope).astype(BF16)
            gbefore[part, cols] = grad
            column_sum += jnp.sum(grad.astype(F32), 0, keepdims=True)
        gbias_ref[:, cols] = column_sum
    out = contract(act[...], wo_ref[...], 1, 0)
    gx = contract(gbefore[...], wi_ref[...], 1, 1)

    @pl.when(step == 0)
    def _():
        if resume:
            out_ref[...] = refs[0][...] + out
            gx_ref[...] = refs[1][...] + gx
        else:
            out_ref[...] = out
            gx_ref[...] = gx

    @pl.when(step != 0)
    def _():
        out_ref[...] += out
        gx_ref[...] += gx

    act_ref[...] = act[...]
    wik_ref[...] = contract(turned(xk_ref), gbefore[...], 1, 0).astype(BF16)
    wis_ref[...] = contract(turned(xs_ref), gbefore[...], 1, 0).astype(BF16)


def feed(core, keep, x, grad, turned, bias, wi, wo, blocks, chunk, sub, first, count, before=()):
    rows, width = x.shape
    hidden = wi.shape[1]
    half = width // 2
    group = hidden * blocks // keep.shape[0]
    single = pl.Buffered(1)
    once = lambda shape: pl.BlockSpec(shape, lambda i, *c: (0, 0), pipeline_mode=single)
    tpairs, _, tshare, _ = turned.shape
    spec = lambda lead: pl.BlockSpec((tpairs, None, tshare, rows), lead, pipeline_mode=single)
    return launch(
        functools.partial(feed_kernel, blocks, sub, group, first, bool(before)),
        [
            like(F32, rows, width),
            like(F32, rows, width),
            like(BF16, rows, count * chunk),
            like(BF16, half, count * chunk),
            like(BF16, half, count * chunk),
            like(F32, 1, count * chunk),
        ],
        prefetch=2,
        grid=(count,),
        in_specs=[
            once((rows, width)),
            once((rows, width)),
            spec(lambda i, c, k: (0, c[0], 0, 0)),
            spec(lambda i, c, k: (0, 1 - c[0], 0, 0)),
            pl.BlockSpec((1, chunk), lambda i, *c: (0, first + i)),
            pl.BlockSpec((width, chunk), lambda i, *c: (0, first + i)),
            pl.BlockSpec((chunk, width), lambda i, *c: (first + i, 0)),
        ]
        + [once((rows, width))] * len(before),
        out_specs=[
            pl.BlockSpec((rows, width), lambda i, *c: (0, 0)),
            pl.BlockSpec((rows, width), lambda i, *c: (0, 0)),
            pl.BlockSpec((rows, chunk), lambda i, *c: (0, i)),
            pl.BlockSpec((half, chunk), lambda i, *c: (0, i)),
            pl.BlockSpec((half, chunk), lambda i, *c: (0, i)),
            pl.BlockSpec((1, chunk), lambda i, *c: (0, i)),
        ],
        scratch=[pltpu.VMEM((rows, chunk), BF16), pltpu.VMEM((rows, chunk), BF16)],
        vmem=FEED_VMEM,
        micros=0,
        name="feed",
    )(core, keep, x, grad, turned, turned, bias, wi, wo, *before)


def outer_kernel(share, starts, core_ref, *refs):
    acts = refs[: len(starts)]
    g_ref = refs[len(starts)]
    keep_ref, send_ref = refs[-2:]
    core = core_ref[0]
    step = pl.program_id(0)
    for act_ref, (lo, hi) in zip(acts, starts):

        @pl.when((step >= lo) & (step < hi))
        def _():
            grad = contract(act_ref[...], g_ref[...], 0, 0).astype(BF16)
            for pair in range(keep_ref.shape[0]):
                even = grad[2 * pair * share : (2 * pair + 1) * share]
                odd = grad[(2 * pair + 1) * share : (2 * pair + 2) * share]

                @pl.when(core == 0)
                def _():
                    keep_ref[pair] = even
                    send_ref[pair] = odd

                @pl.when(core != 0)
                def _():
                    keep_ref[pair] = odd
                    send_ref[pair] = even


def outer_part(core, acts, grad, share, chunk, after=()):
    rows, width = grad.shape
    pairs = chunk // (2 * share)
    specs, starts, at = [], [], 0
    for act in acts:
        count = act.shape[1] // chunk
        starts.append((at, at + count))
        specs.append(
            pl.BlockSpec(
                (rows, chunk), lambda i, lo=at, n=count: (0, jnp.clip(i - lo, 0, n - 1))
            )
        )
        at += count
    return launch(
        functools.partial(outer_kernel, share, starts),
        [like(BF16, at * pairs, share, width)] * 2,
        grid=(at,),
        in_specs=smem_specs(1) + specs + [pl.BlockSpec((rows, width), lambda i: (0, 0))],
        out_specs=[pl.BlockSpec((pairs, share, width), lambda i: (i, 0, 0))] * 2,
        after=after,
        micros=0,
        name="outer_part",
    )(core, *acts, grad)


def split_bit(array, dim, bit):
    keep = lax.dynamic_index_in_dim(array, bit, dim, keepdims=False)
    send = lax.dynamic_index_in_dim(array, 1 - bit, dim, keepdims=False)
    return keep, send


def split_kernel(units, place_ref, *refs):
    outs = refs[-4:]
    at = 0
    for member, count in enumerate(units):
        ins = refs[8 * member : 8 * member + 8]
        for m, out in enumerate(outs):
            left, right = ins[2 * m], ins[2 * m + 1]
            total = (left[0].astype(F32) + right[0].astype(F32)).astype(BF16)
            if count == 1 and len(total.shape) == 2:
                out[0, at] = total
            else:
                out[0, at : at + count] = total
        at += count


def split_call(
    place, arrays, blocks, spots, units, tail, count, low_bit, high_bit, after, name, micros=0
):
    low = lambda p: (p[2] >> low_bit) & 1
    high = lambda p: (p[2] >> high_bit) & 1
    leads = [
        lambda j, p: j * 2 + low(p),
        lambda j, p: j * 2 + 1 - low(p),
        lambda j, p: high(p) * count + j,
        lambda j, p: (1 - high(p)) * count + j,
    ]
    specs = []
    for block, spot in zip(blocks, spots):
        for m, lead in enumerate(leads):
            index = lambda j, p, lead=lead, spot=spot[m // 2]: (lead(j, p),) + spot
            specs += [pl.BlockSpec((1,) + block, index)] * 2
    shape = (sum(units),) + tail
    return launch(
        functools.partial(split_kernel, units),
        [like(BF16, count, *shape)] * 4,
        prefetch=1,
        grid=(count,),
        in_specs=specs,
        out_specs=[pl.BlockSpec((1,) + shape, lambda j, p: (j, 0, 0, 0))] * 4,
        after=after,
        micros=micros,
        name=name,
    )(place, *arrays)


def cross_kernel(kinds, share, place_ref, *refs):
    keep_ref, send_ref = refs[-2:]
    bit = place_ref[1] & 1

    def write(out_ref, low):
        rows = [[], []]
        for n, members in enumerate(kinds):
            am, ag, bm, bg = refs[4 * n : 4 * n + 4]
            at = 0
            for by_rows in members:
                if by_rows:
                    for high, (m, g) in enumerate(((am, ag), (bm, bg))):
                        rows[high].append(m[0, at + low].astype(F32) + g[0, at + low].astype(F32))
                    at += 2
                else:
                    for m, g in ((am, ag), (bm, bg)):
                        total = m[0, at].astype(F32) + g[0, at].astype(F32)
                        for high in range(2):
                            first = (2 * high + low) * share
                            rows[high].append(total[first : first + share])
                    at += 1
        for high in range(2):
            count = sum(part.shape[0] for part in rows[high])
            if out_ref.shape[1] > count:
                blank = jnp.zeros((out_ref.shape[1] - count, out_ref.shape[2]), F32)
                rows[high].append(blank)
            out_ref[high] = jnp.concatenate(rows[high], 0).astype(BF16)

    @pl.when(bit == 0)
    def _():
        write(keep_ref, 0)
        write(send_ref, 1)

    @pl.when(bit == 1)
    def _():
        write(keep_ref, 1)
        write(send_ref, 0)


def last_kernel(place_ref, mine_ref, got_ref, *refs):
    keep_ref, send_ref = refs[-2:]
    bit = place_ref[1] >> 1
    add = lambda i: (mine_ref[i].astype(F32) + got_ref[i].astype(F32)).astype(BF16)
    keep_ref[...] = add(bit)
    send_ref[...] = add(1 - bit)


def total_kernel(mine_ref, got_ref, out_ref):
    out_ref[...] = mine_ref[...].astype(F32) + got_ref[...].astype(F32)


def small_call(body, place, arrays, shape, after, name, micros=0):
    return launch(
        body,
        [shape, shape],
        in_specs=smem_specs(1) + vmem_specs(len(arrays)),
        out_specs=vmem_specs(2),
        after=after,
        vmem=24,
        micros=micros,
        name=name,
    )(place, *arrays)


class Package:
    def __init__(self, place, *members):
        self.place = place
        self.keeps = [keep for keep, _ in members]
        self.flight = [swap(send, "bucket", 1) for _, send in members]
        self.kinds = [keep.ndim == 4 for keep in self.keeps]

    def first(self, *after):
        pairs = self.keeps[0].shape[0]
        self.bits = pairs.bit_length() - 1
        self.count = pairs // 2
        self.turn = 0
        arrays, blocks, spots, units = [], [], [], []
        for keep, got, by_rows in zip(self.keeps, self.flight, self.kinds):
            arrays += [keep, got] * 4
            if by_rows:
                blocks.append((2,) + keep.shape[2:])
                spots.append([(0, 0, 0), (1, 0, 0)])
                units.append(2)
                tail = keep.shape[2:]
            else:
                tail = (keep.shape[1], keep.shape[2] // 2)
                blocks.append(tail)
                spots.append([(0, 0), (0, 1)])
                units.append(1)
        self.unit_count, self.tail = sum(units), tail
        return self.depart(arrays, blocks, spots, units, after, "sum_first")

    def depart(self, arrays, blocks, spots, units, after, name, micros=0):
        low_bit, high_bit = 1 + self.turn, self.bits - self.turn
        (a_keep, a_send, b_keep, b_send), self.done = split_call(
            self.place, arrays, blocks, spots, units, self.tail, self.count, low_bit, high_bit,
            after, name, micros,
        )
        self.mine = [a_keep, b_keep]
        self.flight = [swap(a_send, "bucket", 1 << low_bit), swap(b_send, "bucket", 1 << high_bit)]
        self.turn += 1
        self.count //= 2
        return self.done

    def second(self, *after, micros=0):
        while self.turn < self.bits:
            (am, bm), (ag, bg) = self.mine, self.flight
            spots = [[(0, 0, 0), (0, 0, 0)]]
            block = (self.unit_count,) + self.tail
            arrays = [am, ag, am, ag, bm, bg, bm, bg]
            self.depart(
                arrays, [block], spots, [self.unit_count], after, "sum_second", micros
            )
        return self.done


class Cross:
    def __init__(self, packages, *after, micros=0):
        self.place = packages[0].place
        self.kinds = [p.kinds for p in packages]
        unit, width = packages[0].tail
        self.tiles = sum(4 if by_rows else 2 for kinds in self.kinds for by_rows in kinds)
        self.tail = (unit // 4, width)
        arrays = []
        for p in packages:
            arrays += [p.mine[0], p.flight[0], p.mine[1], p.flight[1]]
        self.rows = -(-self.tiles * self.tail[0] // 16) * 16
        shape = like(BF16, 2, self.rows, width)
        (self.mine, send), self.done = small_call(
            functools.partial(cross_kernel, self.kinds, self.tail[0]), self.place, arrays, shape, after, "cross",
            micros,
        )
        self.flight = swap(send, "seq", 1)

    def last(self, *after):
        shape = like(BF16, self.rows, self.tail[1])
        (self.mine, send), self.done = small_call(
            last_kernel, self.place, [self.mine, self.flight], shape, after, "last"
        )
        self.flight = swap(send, "seq", 2)
        return self.done

    def total(self, *after):
        return launch(
            total_kernel,
            [like(F32, *self.mine.shape)],
            in_specs=vmem_specs(2),
            out_specs=vmem_specs(1),
            after=after,
            vmem=24,
            name="total",
        )(self.mine, self.flight)

    def results(self, total):
        out, at = [], 0
        share = self.tail[0]
        for kinds in self.kinds:
            for by_rows in kinds:
                if by_rows:
                    out.append(total[at : at + 4 * share])
                    at += 4 * share
                else:
                    sides = [total[at : at + share], total[at + share : at + 2 * share]]
                    out.append(jnp.concatenate(sides, 1))
                    at += 2 * share
        return out


def notes_kernel(blocks, early_ref, late_ref, early_cond, late_cond, out_ref, early_sum, late_sum):
    width = early_ref.shape[1]
    for part in range(6):
        if part < 2:
            ref, cond, count, which = late_ref, late_cond, 2, part
        else:
            ref, cond, count, which = early_ref, early_cond, 4, part - 2
        inside = lax.broadcasted_iota(jnp.int32, cond.shape, 0) % ref_pitch(ref, early_ref, late_ref)
        mine = (inside % count == which) & (inside < count * blocks)
        picked = jnp.where(mine, cond[...].astype(F32), 0.0).astype(BF16)
        out_ref[:, part * width : (part + 1) * width] = contract(picked, ref[...], 0, 0)
    for ref, total in ((early_ref, early_sum), (late_ref, late_sum)):
        pitch = ref_pitch(ref, early_ref, late_ref)
        shape = (NOTES, ref.shape[0])
        kind = lax.broadcasted_iota(jnp.int32, shape, 0)
        row = lax.broadcasted_iota(jnp.int32, shape, 1) % pitch
        total[...] = contract(jnp.where(kind == row, 1.0, 0.0).astype(BF16), ref[...], 1, 0)


def ref_pitch(ref, early_ref, late_ref):
    return NOTES if ref is early_ref else NOTES * late_ref.shape[0] // early_ref.shape[0]


def notes_part(early, late, early_cond, late_cond, blocks):
    width = early.shape[1]
    return launch(
        functools.partial(notes_kernel, blocks),
        [
            like(F32, early_cond.shape[1], 6 * width),
            like(F32, NOTES, width),
            like(F32, NOTES, width),
        ],
        in_specs=vmem_specs(4),
        out_specs=vmem_specs(3),
        vmem=32,
        name="notes_part",
    )(early, late, early_cond, late_cond)


def on_device(
    tokens,
    segment,
    keep_route,
    condition,
    group_bucket,
    head_mask,
    channel_mask,
    ada_weight,
    ada_bias,
    qkv_weight,
    query_bias,
    value_bias,
    proj_weight,
    proj_bias,
    inner_weight,
    inner_bias,
    outer_weight,
    outer_bias,
    cotangent,
):
    rows, width = tokens.shape
    slots = condition.shape[0]
    hidden = inner_weight.shape[1]
    group_count = lax.axis_size("bucket")
    seq_count = lax.axis_size("seq")
    bucket = lax.axis_index("bucket")
    seq = lax.axis_index("seq")
    core = bucket % 2
    piece = rows // slots
    block = piece * seq_count
    blocks = rows // block
    place = jnp.stack([core, seq, bucket]).astype(jnp.int32)
    row_share = width // group_count
    aligned = row_share % 16 == 0

    def turned(array):
        split = array.reshape(group_count // 2, 2, row_share, rows)
        if aligned:
            return split
        keep, send = split_bit(split, 1, core)
        return jnp.stack([keep, send]).reshape(1, 2, width // 2, rows)

    turned_core = place[:1] if aligned else jnp.zeros((1,), jnp.int32)

    seg_other = swap(segment, "bucket", 1)
    bucket_other = swap(group_bucket, "bucket", 1)
    tokens_own = tokens.reshape(slots, piece, width)
    tokens_other = swap(tokens_own, "bucket", 1)
    cond_other = swap(condition, "bucket", 1)
    route_columns = jnp.broadcast_to(keep_route.astype(BF16)[:, None], (rows, LANES))
    payload = jnp.concatenate([cotangent, route_columns], 1).reshape(slots, piece, width + LANES)

    (
        send_which, send_index, back_which, back_index, cond_which, cond_row, flags, keep_heads,
        keep_channels,
    ) = make_plan(
        place, segment, seg_other, group_bucket, bucket_other, head_mask, channel_mask, slots,
        piece, seq_count, blocks,
    )

    def bring(pieces):
        return [pieces[0]] + [swap(pieces[k], "seq", k) for k in range(1, seq_count)]

    x_sent, x_mark = send_blocks(tokens_own, tokens_other, send_which, send_index, seq_count, blocks)
    x_parts = bring(x_sent)
    payload = hold(payload, x_mark)
    payload_other = swap(payload, "bucket", 1)
    mod, cond_act = modulate(
        cond_which, cond_row, condition, cond_other, ada_weight, ada_bias, blocks, width,
        (payload_other,),
    )
    payload_sent, _ = send_blocks(
        payload, payload_other, send_which, send_index, seq_count, blocks, (x_parts[3],)
    )
    payload_parts = bring(payload_sent)
    pair_bias = jnp.concatenate([jnp.zeros_like(value_bias), value_bias])[None, :]
    x, normed_one, one_turned, own_kv = enter(x_parts, mod, qkv_weight, pair_bias, blocks)
    other_kv = swap(own_kv, "bucket", 1)
    queries = linear(normed_one, qkv_weight, query_bias, width, width // 3)
    attended, lse = attend(queries, own_kv, other_kv, flags, keep_heads, blocks)
    branch_one, middle, normed_two, two_turned, att_turned, grad_branch_two, grad_outer_bias = (
        middle_part(payload_parts, attended, proj_weight, proj_bias, x, mod, blocks)
    )

    share = hidden // group_count
    by_rows = (group_count // 2, row_share, -1)
    chunk = 2 * width // 3
    feed_args = (
        turned_core, keep_channels, normed_two, grad_branch_two, turned(two_turned),
        inner_bias[None, :], inner_weight, outer_weight, blocks, chunk, FEED_SUB,
    )
    (branch_two, grad_two, act_a, wi_keep, wi_send, hidden_a), _ = feed(*feed_args, 0, 3)
    inner = Package(place, (wi_keep.reshape(by_rows), wi_send.reshape(by_rows)))
    (branch_two, grad_two, act_b, wi_keep, wi_send, hidden_b), mark = feed(
        *feed_args, 3, 3, (branch_two, grad_two)
    )
    mark = inner.first(mark)
    (wo_keep, wo_send), mark = outer_part(
        place[:1], [act_a, act_b], grad_branch_two, share, width, (mark,)
    )
    by_units = (group_count // 2, 4, share // 4, width)
    rest = Package(
        place,
        (wi_keep.reshape(by_rows), wi_send.reshape(by_rows)),
        (wo_keep.reshape(by_units), wo_send.reshape(by_units)),
    )
    (out_stay, out_odd, out_even, grad_middle, grad_branch_one, grad_attended, delta), mark = (
        turn_part(
            payload_parts, keep_heads, branch_two, grad_two, middle, branch_one, attended, mod,
            outer_bias, proj_weight, cond_act, (grad_outer_bias, hidden_a, hidden_b), blocks,
            (mark,),
        )
    )
    mark = inner.second(mark)
    mark = rest.first(mark)
    out_near = swap(out_odd, "seq", 1)
    early = out_odd[2 * blocks * piece :]
    early_all = lax.all_gather(early, ("bucket", "seq"), axis=0, tiled=True)

    (grad_queries, grad_own, grad_other), mark = attend_back(
        queries, own_kv, other_kv, grad_attended, lse, delta, flags, keep_heads, blocks, (mark,)
    )
    grad_got = swap(grad_other, "bucket", 1)
    out_relay, mark = relay(out_even, out_odd, out_near, (mark,))
    out_far = swap(out_relay, "seq", 2)
    inner_cross = Cross([inner], mark)
    (pq_keep, pq_send, grad_one_part, query_sum), mark = query_back(
        turned_core, turned(att_turned), turned(one_turned), grad_branch_one, grad_queries,
        qkv_weight, (inner_cross.done,),
    )
    mark = rest.second(mark, micros=500)
    mark = inner_cross.last(mark)
    (kv_keep, kv_send, x_stay, x_odd, x_even), mark = leave(
        turned_core, turned(one_turned), grad_own, grad_got, qkv_weight, grad_one_part, x,
        grad_middle, mod, query_sum, blocks, piece, (mark,),
    )
    projections = Package(
        place,
        (pq_keep.reshape(by_rows), pq_send.reshape(by_rows)),
        (kv_keep.reshape(by_rows), kv_send.reshape(by_rows)),
    )
    x_near = swap(x_odd, "seq", 1)
    late = x_odd[2 * blocks * piece :]
    late_all = lax.all_gather(late, ("bucket", "seq"), axis=0, tiled=True)

    (inner_sum,), mark = inner_cross.total(mark)
    (out_own, _), mark = collect(out_stay, out_odd, out_near, out_far, (mark,))
    out_other = swap(out_own, "bucket", 1)
    rest_cross = Cross([rest], mark, micros=500)
    mark = projections.first(rest_cross.done)
    x_relay, mark = relay(x_even, x_odd, x_near, (mark,), 500)
    x_far = swap(x_relay, "seq", 2)
    mark = rest_cross.last(mark)
    block_out, mark = pick_blocks(
        out_own, out_other, back_which, back_index, BF16, (mark,), 500
    )
    mark = projections.second(mark)
    (x_own, _), mark = collect(x_stay, x_odd, x_near, x_far, (mark,))
    x_other = swap(x_own, "bucket", 1)
    projections_cross = Cross([projections], mark)
    (rest_sum,), mark = rest_cross.total(projections_cross.done)
    grad_tokens, mark = pick_blocks(x_own, x_other, back_which, back_index, F32, (mark,))
    mark = projections_cross.last(mark)
    (projections_sum,), mark = projections_cross.total(mark)
    block_out = block_out.reshape(rows, width)
    grad_tokens = grad_tokens.reshape(rows, width)
    (inner_a,) = inner_cross.results(inner_sum)
    inner_b, grad_outer_weight = rest_cross.results(rest_sum)
    grad_inner_weight = jnp.concatenate([inner_a, inner_b], 1)
    proj_query, key_value = projections_cross.results(projections_sum)
    grad_proj_weight = proj_query[:, :width]
    grad_qkv_weight = jnp.concatenate([proj_query[:, width:], key_value], 1)

    early_all = hold(early_all, projections_cross.done)
    late_all = hold(late_all, projections_cross.done)
    spot = bucket * seq_count + seq
    device_count = group_count * seq_count
    columns = width // device_count
    cond_mine = lax.dynamic_slice_in_dim(early_all, spot * columns, columns, 1)
    cond_mine = cond_mine.reshape(device_count, NOTES, columns)[:, NOTES - blocks :]

    def at_rows(parts, pitch):
        spread = jnp.broadcast_to(
            cond_mine[:, :, None, :], (device_count, blocks, parts, columns)
        ).reshape(device_count, blocks * parts, columns)
        rest = jnp.zeros((device_count, pitch - blocks * parts, columns), BF16)
        return jnp.concatenate([spread, rest], 1).reshape(device_count * pitch, columns)

    (grad_ada_weight, early_sum, late_sum), _ = notes_part(
        early_all, late_all, at_rows(4, NOTES), at_rows(2, NOTES), blocks
    )

    def own_part(array):
        array = array.reshape(-1)
        size = array.shape[0] // device_count
        return lax.dynamic_slice_in_dim(array, spot * size, size, 0)

    ada_rows = jnp.concatenate(
        [
            sum(late_sum[2 * s : 2 * s + 2] for s in range(blocks)),
            sum(early_sum[4 * s : 4 * s + 4] for s in range(blocks)),
        ],
        0,
    )
    at = 4 * blocks
    return (
        block_out,
        grad_tokens,
        grad_ada_weight,
        own_part(ada_rows),
        grad_qkv_weight,
        own_part(late_sum[2 * blocks]),
        own_part(late_sum[2 * blocks + 1]),
        grad_proj_weight,
        own_part(early_sum[at]),
        grad_inner_weight,
        own_part(early_sum[at + 2 : at + 6]),
        grad_outer_weight,
        own_part(early_sum[at + 1]),
    )


def solution(mesh):
    split = P(("bucket", "seq"))
    split_rows = P(("bucket", "seq"), None)
    return jax.shard_map(
        on_device,
        mesh=mesh,
        in_specs=(split_rows, split, split, P("bucket", None), P("bucket"))
        + (P(),) * 13
        + (split_rows,),
        out_specs=(
            split_rows,
            split_rows,
            split_rows,
            split,
            split_rows,
            split,
            split,
            split_rows,
            split,
            split_rows,
            split,
            split_rows,
            split,
        ),
        check_vma=False,
    )
```

```python
import functools

import jax
import jax.numpy as jnp
from jax import lax
from jax.experimental import pallas as pl
from jax.experimental.pallas import tpu as pltpu
from jax.sharding import PartitionSpec as P

EPSILON = 1e-06
LOG2E = 1.4426950408889634
LANES = 128
NOTES = 16
LONG_HEADS = 4
LONG_BACK = 2
SHORT_HEADS = 4
FEED_VMEM = 60
FEED_SUB = 768
GELU_A = 0.7978845608028654
GELU_B = 0.044715
F32 = jnp.float32
BF16 = jnp.bfloat16


def contract(left, right, left_dim, right_dim, out=F32):
    return lax.dot_general(
        left, right, (((left_dim,), (right_dim,)), ((), ())), preferred_element_type=out
    )


def swap(array, axis, bit):
    size = lax.axis_size(axis)
    return lax.ppermute(array, axis, [(i, i ^ bit) for i in range(size)])


def launch(
    body, out_shape, *, in_specs, out_specs, name, after=(), grid=(), prefetch=0, scratch=(),
    aliases=None, vmem=56, micros=0,
):
    lead = prefetch + len(in_specs)
    waits, outs = len(after), len(out_shape)

    def kernel(*refs):
        rest = refs[lead + waits :]
        body(*refs[:lead], *rest[:outs], *rest[outs + 1 :])
        rest[outs][...] = jnp.zeros(rest[outs].shape, F32)

    token = (8, LANES)
    specs = dict(
        in_specs=list(in_specs) + [pl.BlockSpec(memory_space=pl.ANY)] * waits,
        scratch_shapes=list(scratch),
    )
    if grid:
        specs = dict(
            grid_spec=pltpu.PrefetchScalarGridSpec(
                num_scalar_prefetch=prefetch,
                grid=grid,
                out_specs=list(out_specs) + [pl.BlockSpec(token, lambda *i: (0, 0))],
                **specs,
            )
        )
    else:
        specs["out_specs"] = list(out_specs) + [pl.BlockSpec(memory_space=pltpu.VMEM)]
    call = pl.pallas_call(
        kernel,
        out_shape=list(out_shape) + [jax.ShapeDtypeStruct(token, F32)],
        input_output_aliases=aliases or {},
        compiler_params=pltpu.CompilerParams(vmem_limit_bytes=vmem * 1024 * 1024),
        cost_estimate=pl.CostEstimate(
            flops=int(micros * 1000000000), bytes_accessed=0, transcendentals=0
        ),
        name=name,
        **specs,
    )

    def run(*operands):
        *results, mark = call(*operands, *after)
        return results, mark

    return run


def vmem_specs(count):
    return [pl.BlockSpec(memory_space=pltpu.VMEM)] * count


def smem_specs(count):
    return [pl.BlockSpec(memory_space=pltpu.SMEM)] * count


def like(dtype, *shape):
    return jax.ShapeDtypeStruct(shape, dtype)


def hold_kernel(array_ref, *refs):
    pass


def hold(array, *after):
    anywhere = [pl.BlockSpec(memory_space=pl.ANY)]
    return pl.pallas_call(
        hold_kernel,
        in_specs=anywhere * (1 + len(after)),
        out_specs=anywhere[0],
        out_shape=like(array.dtype, *array.shape),
        input_output_aliases={0: 0},
        cost_estimate=pl.CostEstimate(flops=0, bytes_accessed=0, transcendentals=0),
        name="hold",
    )(array, *after)


def plan_kernel(
    slots, piece, chips, blocks, place_ref, seg_own, seg_other, bucket_own, bucket_other,
    head_mask, channel_mask, send_which, send_index, back_which, back_index, cond_which,
    cond_row, flags, keep_heads, keep_channels, kept, order_ref, rank_ref, id_ref, long_ref,
):
    core = place_ref[0]
    seq = place_ref[1]
    total = 2 * slots
    ids, keys = [], []
    for i in range(total):
        at = (i % slots) * piece
        ids.append(jnp.where(core == i // slots, seg_own[at], seg_other[at]))
    for i in range(total):
        base = (i // slots) * slots
        equal = jnp.int32(0)
        for j in range(slots):
            equal += jnp.where(ids[base + j] == ids[i], 1, 0)
        is_long = jnp.where(equal > 1, 1, 0)
        id_ref[i] = ids[i]
        long_ref[i] = is_long
        keys.append(jnp.where(is_long == 1, i, total + i))
    for i in range(total):
        rank = jnp.int32(0)
        for j in range(total):
            rank += jnp.where(keys[j] < keys[i], 1, 0)
        rank_ref[i] = rank
        order_ref[rank] = jnp.int32(i)
    for k in range(chips):
        for s in range(blocks):
            item = order_ref[((seq ^ k) * 2 + core) * blocks + s]
            send_which[k * blocks + s] = jnp.where(item // slots == core, 0, 1)
            send_index[k * blocks + s] = item % slots
    for j in range(slots):
        rank = rank_ref[core * slots + j]
        back_which[j] = jnp.where((rank // blocks) % 2 == core, 0, 1)
        back_index[j] = ((rank // (2 * blocks)) ^ seq) * blocks + rank % blocks
    flags[0] = long_ref[order_ref[seq * 2 * blocks]]
    flags[1] = core
    heads = head_mask.shape[1]
    groups = channel_mask.shape[1]
    for s in range(blocks):
        item = order_ref[(seq * 2 + core) * blocks + s]
        other = jnp.where(item // slots == core, 0, 1)
        cond_which[s] = other
        cond_row[s] = id_ref[item]
        step = jnp.where(other == 0, bucket_own[0], bucket_other[0])
        count = jnp.int32(0)
        for h in range(heads):
            keep = head_mask[step, h]
            keep_heads[s * heads + h] = keep
            kept[s * heads + h] = jnp.int32(0)

            @pl.when(keep == 1)
            def _():
                kept[s * heads + count] = jnp.int32(h)

            count += keep
        kept[blocks * heads + s] = count
        last = kept[s * heads + jnp.maximum(count - 1, 0)]
        for h in range(heads):

            @pl.when(h >= count)
            def _():
                kept[s * heads + h] = last

        for f in range(groups):
            keep_channels[s * groups + f] = channel_mask[step, f]


def make_plan(place, segment, seg_other, bucket, bucket_other, head_mask, channel_mask, slots, piece,
              chips, blocks):
    smem = pl.BlockSpec(memory_space=pltpu.SMEM)
    sizes = [chips * blocks] * 2 + [slots] * 2 + [blocks] * 2 + [2]
    sizes += [blocks * head_mask.shape[1], blocks * channel_mask.shape[1]]
    sizes += [blocks * head_mask.shape[1] + blocks]
    return pl.pallas_call(
        functools.partial(plan_kernel, slots, piece, chips, blocks),
        in_specs=[smem] * 7,
        out_specs=[smem] * 10,
        out_shape=[jax.ShapeDtypeStruct((n,), jnp.int32) for n in sizes],
        scratch_shapes=[pltpu.SMEM((2 * slots,), jnp.int32)] * 4,
        cost_estimate=pl.CostEstimate(flops=0, bytes_accessed=8000000, transcendentals=0),
        name="make_plan",
    )(place, segment, seg_other, bucket, bucket_other, head_mask, channel_mask)


def send_kernel(blocks, which_ref, index_ref, own_ref, other_ref, *outs):
    for m in range(len(outs) * blocks):

        @pl.when(which_ref[m] == 0)
        def _():
            outs[m // blocks][m % blocks] = own_ref[index_ref[m]]

        @pl.when(which_ref[m] != 0)
        def _():
            outs[m // blocks][m % blocks] = other_ref[index_ref[m]]


def send_blocks(own, other, which, index, chips, blocks, after=()):
    _, rows, width = own.shape
    return launch(
        functools.partial(send_kernel, blocks),
        [like(own.dtype, blocks, rows, width)] * chips,
        in_specs=smem_specs(2) + vmem_specs(2),
        out_specs=vmem_specs(chips),
        after=after,
        vmem=16,
        name="send_blocks",
    )(which, index, own, other)


def pick_kernel(which_ref, index_ref, own_ref, other_ref, out_ref):
    for m in range(out_ref.shape[0]):

        @pl.when(which_ref[m] == 0)
        def _():
            out_ref[m] = own_ref[index_ref[m]].astype(out_ref.dtype)

        @pl.when(which_ref[m] != 0)
        def _():
            out_ref[m] = other_ref[index_ref[m]].astype(out_ref.dtype)


def pick_blocks(own, other, which, index, out_dtype, after=(), micros=0):
    _, rows, width = own.shape
    (out,), mark = launch(
        pick_kernel,
        [like(out_dtype, index.shape[0], rows, width)],
        in_specs=smem_specs(2) + vmem_specs(2),
        out_specs=vmem_specs(1),
        after=after,
        vmem=16,
        micros=micros,
        name="pick_blocks",
    )(which, index, own, other)
    return out, mark


def leaving(k, s, value, stay_ref, odd_ref, even_ref):
    rows = value.shape[0]
    if k == 0:
        stay_ref[s] = value
        return
    target = even_ref if k == 2 else odd_ref
    first = ((k // 2 if k % 2 else 0) * stay_ref.shape[0] + s) * rows
    target[first : first + rows] = value


def leaving_shapes(blocks, piece, width):
    count = blocks * piece
    return [
        like(BF16, blocks, piece, width),
        like(BF16, 2 * count, width),
        like(BF16, count, width),
        like(BF16, NOTES, width),
    ]


def relay_kernel(even_ref, near_ref, out_ref):
    count = even_ref.shape[0]
    out_ref[:count] = even_ref[...]
    out_ref[count:] = near_ref[count:]


def relay(even, near, after=(), micros=0):
    count, width = even.shape
    (out,), mark = launch(
        relay_kernel,
        [like(BF16, 2 * count, width)],
        in_specs=vmem_specs(2),
        out_specs=vmem_specs(1),
        after=after,
        vmem=16,
        micros=micros,
        name="relay",
    )(even, near)
    return out, mark


def collect_kernel(stay_ref, near_ref, far_ref, out_ref):
    blocks, rows, width = stay_ref.shape
    count = blocks * rows
    out_ref[:blocks] = stay_ref[...]
    for k, part in enumerate((near_ref[:count], far_ref[:count], far_ref[count:])):
        out_ref[(k + 1) * blocks : (k + 2) * blocks] = part.reshape(blocks, rows, width)


def collect(stay, near, far, after=(), micros=0):
    blocks, rows, width = stay.shape
    (out,), mark = launch(
        collect_kernel,
        [like(BF16, 4 * blocks, rows, width)],
        in_specs=vmem_specs(3),
        out_specs=vmem_specs(1),
        after=after,
        vmem=16,
        micros=micros,
        name="collect",
    )(stay, near, far)
    return out, mark


def modulate_kernel(
    blocks, which_ref, row_ref, own_ref, other_ref, weight_ref, bias_ref, out_ref, act_ref, held
):
    @pl.when(pl.program_id(0) == 0)
    def _():
        slots, width = own_ref.shape
        picked = []
        for s in range(blocks):
            hot = lax.broadcasted_iota(jnp.int32, (slots, width), 0) == row_ref[s]
            source = jnp.where(which_ref[s] == 0, own_ref[...].astype(F32), other_ref[...].astype(F32))
            picked.append(jnp.sum(jnp.where(hot, source, 0.0), 0, keepdims=True))
        picked.append(jnp.zeros((16 - blocks, width), F32))
        value = jnp.concatenate(picked, 0)
        held[...] = (value / (1.0 + jnp.exp(-value))).astype(BF16)
        act_ref[...] = held[...]

    out_ref[...] = (contract(held[...], weight_ref[...], 1, 0) + bias_ref[...])[:8]


def modulate(which, row, own, other, weight, bias, blocks, chunk, after=()):
    slots, width = own.shape
    columns = weight.shape[1]
    return launch(
        functools.partial(modulate_kernel, blocks),
        [like(F32, 8, columns), like(BF16, 16, width)],
        grid=(columns // chunk,),
        in_specs=smem_specs(2)
        + [
            pl.BlockSpec((slots, width), lambda i: (0, 0)),
            pl.BlockSpec((slots, width), lambda i: (0, 0)),
            pl.BlockSpec((width, chunk), lambda i: (0, i)),
            pl.BlockSpec((1, chunk), lambda i: (0, i)),
        ],
        out_specs=[
            pl.BlockSpec((8, chunk), lambda i: (0, i)),
            pl.BlockSpec((16, width), lambda i: (0, 0)),
        ],
        scratch=[pltpu.VMEM((16, width), BF16)],
        after=after,
        vmem=32,
        micros=0,
        name="modulate",
    )(which, row, own, other, weight, bias[None, :])[0]


def norm_parts(value):
    center = value - jnp.mean(value, -1, keepdims=True)
    spread = jnp.mean(center * center, -1, keepdims=True)
    inverse = lax.rsqrt(spread + EPSILON)
    return center * inverse, inverse


def norm_back(grad, normed, inverse, scale):
    scaled = grad * (1.0 + scale)
    mean_one = jnp.mean(scaled, -1, keepdims=True)
    mean_two = jnp.mean(scaled * normed, -1, keepdims=True)
    return inverse * (scaled - mean_one - normed * mean_two)


def mod_row(mod_ref, index, part, width):
    return mod_ref[index : index + 1, part * width : (part + 1) * width]


def enter_kernel(blocks, *refs):
    parts = refs[:-8]
    mod_ref, weight_ref, bias_ref, x_ref, one_ref, turned_ref, kv_ref, held = refs[-8:]
    _, piece, width = parts[0].shape
    block = held.shape[0] // blocks

    @pl.when(pl.program_id(0) == 0)
    def _():
        for s in range(blocks):
            for k, part in enumerate(parts):
                first = s * block + k * piece
                x = part[s]
                x_ref[first : first + piece] = x
                normed, _ = norm_parts(x.astype(F32))
                one = normed * (1.0 + mod_row(mod_ref, s, 1, width)) + mod_row(mod_ref, s, 0, width)
                held[first : first + piece] = one.astype(BF16)
        one_ref[...] = held[...]
        turned_ref[...] = held[...].T

    kv_ref[...] = (contract(held[...], weight_ref[...], 1, 0) + bias_ref[...]).astype(BF16)


def enter(parts, mod, weight, bias, blocks):
    _, piece, width = parts[0].shape
    rows = piece * blocks * len(parts)
    const = lambda shape: pl.BlockSpec(shape, lambda i: (0,) * len(shape))
    return pl.pallas_call(
        functools.partial(enter_kernel, blocks),
        grid=(2,),
        in_specs=[const(p.shape) for p in parts]
        + [
            const((8, 2 * width)),
            pl.BlockSpec((width, width), lambda i: (0, 1 + i)),
            pl.BlockSpec((1, width), lambda i: (0, i)),
        ],
        out_specs=[
            const((rows, width)),
            const((rows, width)),
            const((width, rows)),
            pl.BlockSpec((rows, width), lambda i: (0, i)),
        ],
        out_shape=[
            jax.ShapeDtypeStruct((rows, width), BF16),
            jax.ShapeDtypeStruct((rows, width), BF16),
            jax.ShapeDtypeStruct((width, rows), BF16),
            jax.ShapeDtypeStruct((rows, 2 * width), BF16),
        ],
        scratch_shapes=[pltpu.VMEM((rows, width), BF16)],
        compiler_params=pltpu.CompilerParams(vmem_limit_bytes=48 * 1024 * 1024),
        cost_estimate=pl.CostEstimate(
            flops=8 * rows * width * width, bytes_accessed=12 * width * width, transcendentals=0
        ),
        name="enter",
    )(*parts, mod, weight, bias)


def linear_kernel(x_ref, weight_ref, bias_ref, out_ref):
    out_ref[...] = (contract(x_ref[...], weight_ref[...], 1, 0) + bias_ref[...]).astype(out_ref.dtype)


def linear(x, weight, bias, columns, chunk):
    rows, width = x.shape
    return pl.pallas_call(
        linear_kernel,
        grid=(columns // chunk,),
        in_specs=[
            pl.BlockSpec((rows, width), lambda i: (0, 0)),
            pl.BlockSpec((width, chunk), lambda i: (0, i)),
            pl.BlockSpec((1, chunk), lambda i: (0, i)),
        ],
        out_specs=pl.BlockSpec((rows, chunk), lambda i: (0, i)),
        out_shape=jax.ShapeDtypeStruct((rows, columns), BF16),
        compiler_params=pltpu.CompilerParams(vmem_limit_bytes=32 * 1024 * 1024),
        cost_estimate=pl.CostEstimate(
            flops=4 * rows * width * columns, bytes_accessed=8 * width * columns, transcendentals=0
        ),
        name="linear",
    )(x, weight, bias[None, :])


def middle_kernel(blocks, *refs):
    parts = refs[:-12]
    (
        att_ref, weight_ref, bias_ref, x_ref, mod_ref,
        branch_ref, middle_ref, two_ref, two_turned, att_turned, grad_ref, bias_grad,
    ) = refs[-12:]
    rows, width = x_ref.shape
    block = rows // blocks
    piece = parts[0].shape[1]
    att_turned[...] = att_ref[...].T
    total = jnp.zeros((1, width), F32)
    for s in range(blocks):
        part = slice(s * block, (s + 1) * block)
        branch = contract(att_ref[part], weight_ref[...], 1, 0) + bias_ref[...]
        branch_ref[part] = branch
        middle = x_ref[part].astype(F32) + mod_row(mod_ref, s, 2, width) * branch
        middle_ref[part] = middle
        normed, _ = norm_parts(middle)
        two_ref[part] = (
            normed * (1.0 + mod_row(mod_ref, s, 4, width)) + mod_row(mod_ref, s, 3, width)
        ).astype(BF16)
        for k, source in enumerate(parts):
            first = s * block + k * piece
            payload = source[s].astype(F32)
            grad = (payload[:, width : width + 1] * mod_row(mod_ref, s, 5, width) * payload[:, :width]).astype(BF16)
            grad_ref[first : first + piece] = grad
            total += jnp.sum(grad.astype(F32), 0, keepdims=True)
    two_turned[...] = two_ref[...].T
    bias_grad[...] = total


def middle_part(parts, attended, weight, bias, x, mod, blocks):
    rows, width = x.shape
    vmem = pl.BlockSpec(memory_space=pltpu.VMEM)
    return pl.pallas_call(
        functools.partial(middle_kernel, blocks),
        in_specs=[vmem] * (len(parts) + 5),
        out_specs=[vmem] * 7,
        out_shape=[
            jax.ShapeDtypeStruct((rows, width), F32),
            jax.ShapeDtypeStruct((rows, width), F32),
            jax.ShapeDtypeStruct((rows, width), BF16),
            jax.ShapeDtypeStruct((width, rows), BF16),
            jax.ShapeDtypeStruct((width, rows), BF16),
            jax.ShapeDtypeStruct((rows, width), BF16),
            jax.ShapeDtypeStruct((1, width), F32),
        ],
        compiler_params=pltpu.CompilerParams(vmem_limit_bytes=48 * 1024 * 1024),
        cost_estimate=pl.CostEstimate(
            flops=8 * rows * width * width, bytes_accessed=24 * rows * width, transcendentals=0
        ),
        name="middle_part",
    )(*parts, attended, weight, bias[None, :], x, mod)


def turn_kernel(blocks, heads, *refs):
    count = 4
    parts = refs[:count]
    (
        keep_ref, out_ref, gx_ref, middle_ref, branch_ref, att_ref, mod_ref, bias_ref, weight_ref,
        act_ref, outer_sum, *hidden_sums,
    ) = refs[count:-8]
    stay_ref, odd_ref, even_ref, notes_ref, grad_middle, grad_one, grad_att, delta_ref = refs[-8:]
    notes = []
    rows, width = middle_ref.shape
    block = rows // blocks
    piece = parts[0].shape[1]
    head_width = width // heads
    column_head = lax.broadcasted_iota(jnp.int32, (heads, width), 1) // head_width
    hot = (column_head == lax.broadcasted_iota(jnp.int32, (heads, width), 0)).astype(F32)
    bias_total = jnp.zeros((1, width), F32)
    for s in range(blocks):
        sums = [jnp.zeros((1, width), F32) for _ in range(4)]
        gate_one = mod_row(mod_ref, s, 2, width)
        scale_two = mod_row(mod_ref, s, 4, width)
        gate_two = mod_row(mod_ref, s, 5, width)
        for k, source in enumerate(parts):
            first = s * block + k * piece
            part = slice(first, first + piece)
            payload = source[s].astype(F32)
            upstream = payload[:, :width]
            route = payload[:, width : width + 1]
            middle = middle_ref[part]
            branch_two = route * (out_ref[part] + bias_ref[...])
            leaving(k, s, (middle + gate_two * branch_two).astype(BF16), stay_ref, odd_ref, even_ref)
            sums[3] += jnp.sum(branch_two * upstream, 0, keepdims=True)
            grad_two = gx_ref[part]
            normed, inverse = norm_parts(middle)
            sums[1] += jnp.sum(grad_two, 0, keepdims=True)
            sums[2] += jnp.sum(grad_two * normed, 0, keepdims=True)
            grad = upstream + norm_back(grad_two, normed, inverse, scale_two)
            grad_middle[part] = grad
            sums[0] += jnp.sum(grad * branch_ref[part], 0, keepdims=True)
            low = (gate_one * grad).astype(BF16)
            grad_one[part] = low
            bias_total += jnp.sum(low.astype(F32), 0, keepdims=True)
        notes += sums
        part = slice(s * block, (s + 1) * block)
        row = jnp.zeros((1, width), F32)
        for h in range(heads):
            row = jnp.where(
                hot[h : h + 1] > 0.5, keep_ref[s * heads + h].astype(F32), row
            )
        low = contract(grad_one[part], weight_ref[...], 1, 1).astype(BF16).astype(F32) * row
        grad_att[part] = low.astype(BF16)
        delta_ref[:, part] = lax.dot_general(
            hot,
            low * att_ref[part].astype(F32),
            (((1,), (1,)), ((), ())),
            precision=lax.Precision.HIGHEST,
            preferred_element_type=F32,
        )
    notes.append(bias_total)
    notes.append(outer_sum[...])
    for ref in hidden_sums:
        notes += [ref[:, lo : lo + width] for lo in range(0, ref.shape[1], width)]
    notes.append(act_ref[:blocks].astype(F32))
    notes_ref[...] = jnp.concatenate(notes, 0).astype(BF16)


def turn_part(
    parts, keep, out, gx, middle, branch, attended, mod, bias, weight, act, sums, blocks, after=()
):
    rows, width = middle.shape
    heads = keep.shape[0] // blocks
    return launch(
        functools.partial(turn_kernel, blocks, heads),
        leaving_shapes(blocks, parts[0].shape[1], width)
        + [
            like(F32, rows, width),
            like(BF16, rows, width),
            like(BF16, rows, width),
            like(F32, heads, rows),
        ],
        in_specs=vmem_specs(len(parts)) + smem_specs(1) + vmem_specs(9 + len(sums)),
        out_specs=vmem_specs(8),
        after=after,
        vmem=48,
        micros=500,
        name="turn_part",
    )(*parts, keep, out, gx, middle, branch, attended, mod, bias[None, :], weight, act, *sums)


def query_back_kernel(
    core_ref, proj_keep, proj_send, one_keep, one_send, grad_one, grad_q, weight_ref, *refs
):
    keep_ref, send_ref, gx_ref, sum_ref = refs[-4:]
    width = grad_q.shape[1]
    half = keep_ref.shape[0]
    rows = grad_q.shape[0]
    turned = lambda ref: ref[...].reshape(half, rows)
    keep_ref[:, :width] = contract(turned(proj_keep), grad_one[...], 1, 0).astype(BF16)
    send_ref[:, :width] = contract(turned(proj_send), grad_one[...], 1, 0).astype(BF16)
    keep_ref[:, width:] = contract(turned(one_keep), grad_q[...], 1, 0).astype(BF16)
    send_ref[:, width:] = contract(turned(one_send), grad_q[...], 1, 0).astype(BF16)
    gx_ref[...] = contract(grad_q[...], weight_ref[...], 1, 1)
    sum_ref[...] = jnp.sum(grad_q[...].astype(F32), 0, keepdims=True)


def turned_specs(array):
    pairs, _, share, rows = array.shape
    keep = pl.BlockSpec((pairs, None, share, rows), lambda i, c: (0, c[0], 0, 0))
    send = pl.BlockSpec((pairs, None, share, rows), lambda i, c: (0, 1 - c[0], 0, 0))
    return [keep, send]


def query_back(core, att_turned, one_turned, grad_one, grad_q, weight, after=()):
    rows, width = grad_q.shape
    half = width // 2
    const = lambda shape: pl.BlockSpec(shape, lambda i, c: (0,) * len(shape))
    return launch(
        query_back_kernel,
        [
            like(BF16, half, 2 * width),
            like(BF16, half, 2 * width),
            like(F32, rows, width),
            like(F32, 1, width),
        ],
        prefetch=1,
        grid=(1,),
        in_specs=turned_specs(att_turned)
        + turned_specs(one_turned)
        + [const((rows, width)), const((rows, width)), const((width, width))],
        out_specs=[
            const((half, 2 * width)),
            const((half, 2 * width)),
            const((rows, width)),
            const((1, width)),
        ],
        after=after,
        micros=0,
        name="query_back",
    )(core, att_turned, att_turned, one_turned, one_turned, grad_one, grad_q, weight)


def leave_kernel(
    blocks, core_ref, one_keep, one_send, own_ref, got_ref, weight_ref, gx_in, x_ref, middle_ref,
    mod_ref, query_sum, keep_ref, send_ref, stay_ref, odd_ref, even_ref, notes_ref, total,
    grads,
):
    piece = stay_ref.shape[1]
    rows, width = x_ref.shape
    half = keep_ref.shape[0]
    block = rows // blocks
    step = pl.program_id(0)
    turned = lambda ref: ref[...].reshape(half, rows)
    grads[...] = (own_ref[...].astype(F32) + got_ref[...].astype(F32)).astype(BF16)
    keep_ref[...] = contract(turned(one_keep), grads[...], 1, 0).astype(BF16)
    send_ref[...] = contract(turned(one_send), grads[...], 1, 0).astype(BF16)

    @pl.when(step == 0)
    def _():
        total[...] = gx_in[...] + contract(grads[...], weight_ref[...], 1, 1)

    @pl.when(step == 1)
    def _():
        notes = []
        for s in range(blocks):
            part = slice(s * block, (s + 1) * block)
            grad = total[part] + contract(grads[part], weight_ref[...], 1, 1)
            normed, inverse = norm_parts(x_ref[part].astype(F32))
            notes.append(jnp.sum(grad, 0, keepdims=True))
            notes.append(jnp.sum(grad * normed, 0, keepdims=True))
            back = norm_back(grad, normed, inverse, mod_row(mod_ref, s, 1, width))
            low = (middle_ref[part] + back).astype(BF16)
            for k in range(block // piece):
                leaving(k, s, low[k * piece : (k + 1) * piece], stay_ref, odd_ref, even_ref)
        notes.append(query_sum[...])
        notes.append(jnp.sum(grads[...].astype(F32), 0, keepdims=True))
        notes.append(jnp.zeros((NOTES - 2 * blocks - 2, width), F32))
        notes_ref[...] = jnp.concatenate(notes, 0).astype(BF16)


def leave(
    core, one_turned, own, got, weight, gx, x, grad_middle, mod, query_sum, blocks, piece, after=()
):
    rows, width = x.shape
    half = width // 2
    const = lambda shape: pl.BlockSpec(shape, lambda i, c: (0,) * len(shape))
    once = lambda shape: pl.BlockSpec(
        shape, lambda i, c: (0,) * len(shape), pipeline_mode=pl.Buffered(1)
    )
    shapes = leaving_shapes(blocks, piece, width)
    return launch(
        functools.partial(leave_kernel, blocks),
        [like(BF16, half, 2 * width), like(BF16, half, 2 * width)] + shapes,
        prefetch=1,
        grid=(2,),
        in_specs=turned_specs(one_turned)
        + [
            pl.BlockSpec((rows, width), lambda i, c: (0, i)),
            pl.BlockSpec((rows, width), lambda i, c: (0, i)),
            pl.BlockSpec((width, width), lambda i, c: (0, 1 + i)),
            once((rows, width)),
            once((rows, width)),
            once((rows, width)),
            once((8, 2 * width)),
            once((1, width)),
        ],
        out_specs=[
            pl.BlockSpec((half, width), lambda i, c: (0, i)),
            pl.BlockSpec((half, width), lambda i, c: (0, i)),
        ]
        + [const(s.shape) for s in shapes],
        scratch=[pltpu.VMEM((rows, width), F32), pltpu.VMEM((rows, width), BF16)],
        after=after,
        micros=500,
        name="leave",
    )(core, one_turned, one_turned, own, got, weight, gx, x, grad_middle, mod, query_sum)


def head_columns(ref, start, head_width):
    part = ref[:, start : start + head_width]
    return jnp.concatenate(
        [part, jnp.zeros((part.shape[0], LANES - head_width), part.dtype)], axis=1
    )


def kept_heads(list_ref, blocks, heads, index, one, together):
    count = list_ref[blocks * heads + index]

    def body(i, carry):
        one([list_ref[index * heads + i * together + u] for u in range(together)])
        return carry

    lax.fori_loop(0, (count + together - 1) // together, body, 0)


def masked_heads(keep_ref, blocks, heads, block, blank):
    for index in range(blocks):

        def body(h, carry):
            @pl.when(keep_ref[index * heads + h] == 0)
            def _():
                blank(h, pl.ds(index * block, block))

            return carry

        lax.fori_loop(0, heads, body, 0)


def attend_kernel(
    heads, head_width, blocks, long_ref, keep_ref, list_ref, q_ref, own_ref, other_ref, out_ref,
    lse_ref, qh, kh, vh, oh,
):
    rows, width = q_ref.shape
    block = rows // blocks
    factor = head_width**-0.5 * LOG2E
    is_long = long_ref[0] == 1
    for h in range(heads):
        start = h * head_width
        qh[h] = head_columns(q_ref, start, head_width)
        kh[h, :rows] = head_columns(own_ref, start, head_width)
        vh[h, :rows] = head_columns(own_ref, width + start, head_width)

    @pl.when(is_long)
    def _():
        for h in range(heads):
            start = h * head_width
            kh[h, rows:] = head_columns(other_ref, start, head_width)
            vh[h, rows:] = head_columns(other_ref, width + start, head_width)

    def blank(h, part):
        oh[h, part, :] = jnp.zeros((block, LANES), BF16)

    masked_heads(keep_ref, blocks, heads, block, blank)

    def loop(index, together, first, count, key_first, key_count):
        def one(group):
            part, keys_part = pl.ds(first, count), pl.ds(key_first, key_count)
            scores = [contract(kh[h, keys_part, :], qh[h, part, :], 1, 1) for h in group]
            tops = [jnp.max(x, 0, keepdims=True) for x in scores]
            exponents = [jnp.exp2((x - top) * factor) for x, top in zip(scores, tops)]
            totals = [jnp.sum(x, 0, keepdims=True) for x in exponents]
            for h, exponent, top, total in zip(group, exponents, tops, totals):
                mixed = contract(vh[h, keys_part, :], exponent.astype(BF16), 0, 0) * (1.0 / total)
                oh[h, part, :] = mixed.T.astype(BF16)
                lse_ref[pl.ds(h, 1), part] = top * factor + jnp.log2(total)

        kept_heads(list_ref, blocks, heads, index, one, together)

    @pl.when(is_long)
    def _():
        loop(0, LONG_HEADS, 0, rows, 0, 2 * rows)

    @pl.when(jnp.logical_not(is_long))
    def _():
        for index in range(blocks):
            loop(index, SHORT_HEADS, index * block, block, index * block, block)

    for h in range(heads):
        out_ref[:, h * head_width : (h + 1) * head_width] = oh[h, :, :head_width]


def attend(queries, own, other, long_flag, keep, kept, blocks):
    rows, width = queries.shape
    heads = keep.shape[0] // blocks
    head_width = width // heads
    vmem = pl.BlockSpec(memory_space=pltpu.VMEM)
    smem = pl.BlockSpec(memory_space=pltpu.SMEM)
    return pl.pallas_call(
        functools.partial(attend_kernel, heads, head_width, blocks),
        in_specs=[smem, smem, smem, vmem, vmem, vmem],
        out_specs=[vmem, vmem],
        out_shape=[
            jax.ShapeDtypeStruct((rows, width), BF16),
            jax.ShapeDtypeStruct((heads, rows), F32),
        ],
        scratch_shapes=[
            pltpu.VMEM((heads, rows, LANES), BF16),
            pltpu.VMEM((heads, 2 * rows, LANES), BF16),
            pltpu.VMEM((heads, 2 * rows, LANES), BF16),
            pltpu.VMEM((heads, rows, LANES), BF16),
        ],
        compiler_params=pltpu.CompilerParams(vmem_limit_bytes=56 * 1024 * 1024),
        cost_estimate=pl.CostEstimate(
            flops=100 * rows * rows * width,
            bytes_accessed=12 * rows * width,
            transcendentals=2 * rows * rows * heads,
        ),
        name="attend",
    )(long_flag, keep, kept, queries, own, other)


def attend_back_kernel(
    heads, head_width, blocks, long_ref, keep_ref, list_ref, q_ref, own_ref, other_ref, go_ref,
    lse_ref, delta_ref, gq_ref, gown_ref, gother_ref, qh, kh, vh, gh, gqh, gkh, gvh,
):
    rows, width = q_ref.shape
    block = rows // blocks
    scale = head_width**-0.5
    factor = scale * LOG2E
    is_long = long_ref[0] == 1
    for h in range(heads):
        start = h * head_width
        qh[h] = head_columns(q_ref, start, head_width)
        gh[h] = head_columns(go_ref, start, head_width)
        kh[h, :rows] = head_columns(own_ref, start, head_width)
        vh[h, :rows] = head_columns(own_ref, width + start, head_width)

    @pl.when(is_long)
    def _():
        for h in range(heads):
            start = h * head_width
            kh[h, rows:] = head_columns(other_ref, start, head_width)
            vh[h, rows:] = head_columns(other_ref, width + start, head_width)

    def blank(h, part):
        for ref in (gqh, gkh, gvh):
            ref[h, part, :] = jnp.zeros((block, LANES), BF16)

    masked_heads(keep_ref, blocks, heads, block, blank)

    def loop(index, together, first, count, key_first, key_count):
        def one(group):
            part, keys_part = pl.ds(first, count), pl.ds(key_first, key_count)
            scores = [contract(kh[h, keys_part, :], qh[h, part, :], 1, 1) for h in group]
            grads = [contract(vh[h, keys_part, :], gh[h, part, :], 1, 1) for h in group]
            probs = [
                jnp.exp2(x * factor - lse_ref[pl.ds(h, 1), part]) for h, x in zip(group, scores)
            ]
            slopes = [
                (p * (g - delta_ref[pl.ds(h, 1), part])).astype(BF16)
                for h, p, g in zip(group, probs, grads)
            ]
            for h, p, slope in zip(group, probs, slopes):
                gvh[h, keys_part, :] = contract(p.astype(BF16), gh[h, part, :], 1, 0).astype(BF16)
                gkh[h, keys_part, :] = (contract(slope, qh[h, part, :], 1, 0) * scale).astype(BF16)
                gqh[h, part, :] = ((contract(kh[h, keys_part, :], slope, 0, 0) * scale).T).astype(BF16)

        kept_heads(list_ref, blocks, heads, index, one, together)

    @pl.when(is_long)
    def _():
        def blank_other(h, part):
            for ref in (gkh, gvh):
                ref[h, pl.ds(rows + part.start, block), :] = jnp.zeros((block, LANES), BF16)

        masked_heads(keep_ref, blocks, heads, block, blank_other)
        loop(0, LONG_BACK, 0, rows, 0, 2 * rows)

    @pl.when(jnp.logical_not(is_long))
    def _():
        for index in range(blocks):
            loop(index, SHORT_HEADS, index * block, block, index * block, block)
        gother_ref[...] = jnp.zeros_like(gother_ref)

    for h in range(heads):
        start = h * head_width
        gq_ref[:, start : start + head_width] = gqh[h, :, :head_width]
        gown_ref[:, start : start + head_width] = gkh[h, :rows, :head_width]
        gown_ref[:, width + start : width + start + head_width] = gvh[h, :rows, :head_width]

    @pl.when(is_long)
    def _():
        for h in range(heads):
            start = h * head_width
            gother_ref[:, start : start + head_width] = gkh[h, rows:, :head_width]
            gother_ref[:, width + start : width + start + head_width] = gvh[h, rows:, :head_width]


def attend_back(
    queries, own, other, grad_out, lse, delta, long_flag, keep, kept, blocks, after=()
):
    rows, width = queries.shape
    heads = keep.shape[0] // blocks
    head_width = width // heads
    short = pltpu.VMEM((heads, rows, LANES), BF16)
    full = pltpu.VMEM((heads, 2 * rows, LANES), BF16)
    return launch(
        functools.partial(attend_back_kernel, heads, head_width, blocks),
        [like(BF16, rows, width), like(BF16, rows, 2 * width), like(BF16, rows, 2 * width)],
        in_specs=smem_specs(3) + vmem_specs(6),
        out_specs=vmem_specs(3),
        scratch=[short, full, full, short, short, full, full],
        after=after,
        vmem=60,
        micros=500,
        name="attend_back",
    )(long_flag, keep, kept, queries, own, other, grad_out, lse, delta)


def feed_kernel(
    blocks, sub, group, first, resume, core_ref, keep_ref, x_ref, g_ref, xk_ref, xs_ref, bias_ref,
    wi_ref, wo_ref, *refs,
):
    act, gbefore = refs[-2:]
    out_ref, gx_ref, act_ref, wik_ref, wis_ref, gbias_ref = refs[-8:-2]
    rows, _ = x_ref.shape
    block = rows // blocks
    chunk = wi_ref.shape[1]
    half = wik_ref.shape[0]
    step = pl.program_id(0)
    groups = keep_ref.shape[0] // blocks
    turned = lambda ref: ref[...].reshape(half, rows)
    for lo in range(0, chunk, sub):
        cols = slice(lo, lo + sub)
        column_sum = jnp.zeros((1, sub), F32)
        for index in range(blocks):
            part = slice(index * block, (index + 1) * block)
            before = contract(x_ref[part], wi_ref[:, cols], 1, 0) + bias_ref[:, cols]
            grad_act = contract(g_ref[part], wo_ref[cols, :], 1, 1)
            base = index * groups + ((first + step) * chunk + lo) // group
            keep = jnp.concatenate(
                [
                    jnp.full((1, group), keep_ref[base + m].astype(F32))
                    for m in range(sub // group)
                ],
                axis=1,
            )
            square = before * before
            bend = jnp.tanh(GELU_A * before * (1.0 + GELU_B * square))
            gate = 0.5 * (1.0 + bend)
            slope = gate + (0.5 * GELU_A) * before * (1.0 - bend * bend) * (
                1.0 + (3.0 * GELU_B) * square
            )
            act[part, cols] = (before * gate * keep).astype(BF16)
            grad = (grad_act * keep * slope).astype(BF16)
            gbefore[part, cols] = grad
            column_sum += jnp.sum(grad.astype(F32), 0, keepdims=True)
        gbias_ref[:, cols] = column_sum
    out = contract(act[...], wo_ref[...], 1, 0)
    gx = contract(gbefore[...], wi_ref[...], 1, 1)

    @pl.when(step == 0)
    def _():
        if resume:
            out_ref[...] = refs[0][...] + out
            gx_ref[...] = refs[1][...] + gx
        else:
            out_ref[...] = out
            gx_ref[...] = gx

    @pl.when(step != 0)
    def _():
        out_ref[...] += out
        gx_ref[...] += gx

    act_ref[...] = act[...]
    wik_ref[...] = contract(turned(xk_ref), gbefore[...], 1, 0).astype(BF16)
    wis_ref[...] = contract(turned(xs_ref), gbefore[...], 1, 0).astype(BF16)


def feed(core, keep, x, grad, turned, bias, wi, wo, blocks, chunk, sub, first, count, before=()):
    rows, width = x.shape
    hidden = wi.shape[1]
    half = width // 2
    group = hidden * blocks // keep.shape[0]
    single = pl.Buffered(1)
    once = lambda shape: pl.BlockSpec(shape, lambda i, *c: (0, 0), pipeline_mode=single)
    tpairs, _, tshare, _ = turned.shape
    spec = lambda lead: pl.BlockSpec((tpairs, None, tshare, rows), lead, pipeline_mode=single)
    return launch(
        functools.partial(feed_kernel, blocks, sub, group, first, bool(before)),
        [
            like(F32, rows, width),
            like(F32, rows, width),
            like(BF16, rows, count * chunk),
            like(BF16, half, count * chunk),
            like(BF16, half, count * chunk),
            like(F32, 1, count * chunk),
        ],
        prefetch=2,
        grid=(count,),
        in_specs=[
            once((rows, width)),
            once((rows, width)),
            spec(lambda i, c, k: (0, c[0], 0, 0)),
            spec(lambda i, c, k: (0, 1 - c[0], 0, 0)),
            pl.BlockSpec((1, chunk), lambda i, *c: (0, first + i)),
            pl.BlockSpec((width, chunk), lambda i, *c: (0, first + i)),
            pl.BlockSpec((chunk, width), lambda i, *c: (first + i, 0)),
        ]
        + [once((rows, width))] * len(before),
        out_specs=[
            pl.BlockSpec((rows, width), lambda i, *c: (0, 0)),
            pl.BlockSpec((rows, width), lambda i, *c: (0, 0)),
            pl.BlockSpec((rows, chunk), lambda i, *c: (0, i)),
            pl.BlockSpec((half, chunk), lambda i, *c: (0, i)),
            pl.BlockSpec((half, chunk), lambda i, *c: (0, i)),
            pl.BlockSpec((1, chunk), lambda i, *c: (0, i)),
        ],
        scratch=[pltpu.VMEM((rows, chunk), BF16), pltpu.VMEM((rows, chunk), BF16)],
        vmem=FEED_VMEM,
        micros=0,
        name="feed",
    )(core, keep, x, grad, turned, turned, bias, wi, wo, *before)


def outer_kernel(share, starts, core_ref, *refs):
    acts = refs[: len(starts)]
    g_ref = refs[len(starts)]
    keep_ref, send_ref = refs[-2:]
    core = core_ref[0]
    step = pl.program_id(0)
    for act_ref, (lo, hi) in zip(acts, starts):

        @pl.when((step >= lo) & (step < hi))
        def _():
            grad = contract(act_ref[...], g_ref[...], 0, 0).astype(BF16)
            for pair in range(keep_ref.shape[0]):
                even = grad[2 * pair * share : (2 * pair + 1) * share]
                odd = grad[(2 * pair + 1) * share : (2 * pair + 2) * share]

                @pl.when(core == 0)
                def _():
                    keep_ref[pair] = even
                    send_ref[pair] = odd

                @pl.when(core != 0)
                def _():
                    keep_ref[pair] = odd
                    send_ref[pair] = even


def outer_part(core, acts, grad, share, chunk, after=()):
    rows, width = grad.shape
    pairs = chunk // (2 * share)
    specs, starts, at = [], [], 0
    for act in acts:
        count = act.shape[1] // chunk
        starts.append((at, at + count))
        specs.append(
            pl.BlockSpec(
                (rows, chunk), lambda i, lo=at, n=count: (0, jnp.clip(i - lo, 0, n - 1))
            )
        )
        at += count
    return launch(
        functools.partial(outer_kernel, share, starts),
        [like(BF16, at * pairs, share, width)] * 2,
        grid=(at,),
        in_specs=smem_specs(1) + specs + [pl.BlockSpec((rows, width), lambda i: (0, 0))],
        out_specs=[pl.BlockSpec((pairs, share, width), lambda i: (i, 0, 0))] * 2,
        after=after,
        micros=0,
        name="outer_part",
    )(core, *acts, grad)


def split_bit(array, dim, bit):
    keep = lax.dynamic_index_in_dim(array, bit, dim, keepdims=False)
    send = lax.dynamic_index_in_dim(array, 1 - bit, dim, keepdims=False)
    return keep, send


def split_kernel(units, place_ref, *refs):
    outs = refs[-4:]
    at = 0
    for member, count in enumerate(units):
        ins = refs[8 * member : 8 * member + 8]
        for m, out in enumerate(outs):
            left, right = ins[2 * m], ins[2 * m + 1]
            total = (left[0].astype(F32) + right[0].astype(F32)).astype(BF16)
            if count == 1 and len(total.shape) == 2:
                out[0, at] = total
            else:
                out[0, at : at + count] = total
        at += count


def split_call(
    place, arrays, blocks, spots, units, tail, count, low_bit, high_bit, after, name, micros=0
):
    low = lambda p: (p[2] >> low_bit) & 1
    high = lambda p: (p[2] >> high_bit) & 1
    leads = [
        lambda j, p: j * 2 + low(p),
        lambda j, p: j * 2 + 1 - low(p),
        lambda j, p: high(p) * count + j,
        lambda j, p: (1 - high(p)) * count + j,
    ]
    specs = []
    for block, spot in zip(blocks, spots):
        for m, lead in enumerate(leads):
            index = lambda j, p, lead=lead, spot=spot[m // 2]: (lead(j, p),) + spot
            specs += [pl.BlockSpec((1,) + block, index)] * 2
    shape = (sum(units),) + tail
    return launch(
        functools.partial(split_kernel, units),
        [like(BF16, count, *shape)] * 4,
        prefetch=1,
        grid=(count,),
        in_specs=specs,
        out_specs=[pl.BlockSpec((1,) + shape, lambda j, p: (j, 0, 0, 0))] * 4,
        after=after,
        micros=micros,
        name=name,
    )(place, *arrays)


def cross_kernel(kinds, share, place_ref, *refs):
    keep_ref, send_ref = refs[-2:]
    bit = place_ref[1] & 1

    def write(out_ref, low):
        rows = [[], []]
        for n, members in enumerate(kinds):
            am, ag, bm, bg = refs[4 * n : 4 * n + 4]
            at = 0
            for by_rows in members:
                if by_rows:
                    for high, (m, g) in enumerate(((am, ag), (bm, bg))):
                        rows[high].append(m[0, at + low].astype(F32) + g[0, at + low].astype(F32))
                    at += 2
                else:
                    for m, g in ((am, ag), (bm, bg)):
                        total = m[0, at].astype(F32) + g[0, at].astype(F32)
                        for high in range(2):
                            first = (2 * high + low) * share
                            rows[high].append(total[first : first + share])
                    at += 1
        for high in range(2):
            count = sum(part.shape[0] for part in rows[high])
            if out_ref.shape[1] > count:
                blank = jnp.zeros((out_ref.shape[1] - count, out_ref.shape[2]), F32)
                rows[high].append(blank)
            out_ref[high] = jnp.concatenate(rows[high], 0).astype(BF16)

    @pl.when(bit == 0)
    def _():
        write(keep_ref, 0)
        write(send_ref, 1)

    @pl.when(bit == 1)
    def _():
        write(keep_ref, 1)
        write(send_ref, 0)


def last_kernel(place_ref, mine_ref, got_ref, *refs):
    keep_ref, send_ref = refs[-2:]
    bit = place_ref[1] >> 1
    add = lambda i: (mine_ref[i].astype(F32) + got_ref[i].astype(F32)).astype(BF16)
    keep_ref[...] = add(bit)
    send_ref[...] = add(1 - bit)


def total_kernel(mine_ref, got_ref, out_ref):
    out_ref[...] = mine_ref[...].astype(F32) + got_ref[...].astype(F32)


def small_call(body, place, arrays, shape, after, name, micros=0):
    return launch(
        body,
        [shape, shape],
        in_specs=smem_specs(1) + vmem_specs(len(arrays)),
        out_specs=vmem_specs(2),
        after=after,
        vmem=24,
        micros=micros,
        name=name,
    )(place, *arrays)


class Package:
    def __init__(self, place, *members):
        self.place = place
        self.keeps = [keep for keep, _ in members]
        self.flight = [swap(send, "bucket", 1) for _, send in members]
        self.kinds = [keep.ndim == 4 for keep in self.keeps]

    def first(self, *after):
        pairs = self.keeps[0].shape[0]
        self.bits = pairs.bit_length() - 1
        self.count = pairs // 2
        self.turn = 0
        arrays, blocks, spots, units = [], [], [], []
        for keep, got, by_rows in zip(self.keeps, self.flight, self.kinds):
            arrays += [keep, got] * 4
            if by_rows:
                blocks.append((2,) + keep.shape[2:])
                spots.append([(0, 0, 0), (1, 0, 0)])
                units.append(2)
                tail = keep.shape[2:]
            else:
                tail = (keep.shape[1], keep.shape[2] // 2)
                blocks.append(tail)
                spots.append([(0, 0), (0, 1)])
                units.append(1)
        self.unit_count, self.tail = sum(units), tail
        return self.depart(arrays, blocks, spots, units, after, "sum_first")

    def depart(self, arrays, blocks, spots, units, after, name, micros=0):
        low_bit, high_bit = 1 + self.turn, self.bits - self.turn
        (a_keep, a_send, b_keep, b_send), self.done = split_call(
            self.place, arrays, blocks, spots, units, self.tail, self.count, low_bit, high_bit,
            after, name, micros,
        )
        self.mine = [a_keep, b_keep]
        self.flight = [swap(a_send, "bucket", 1 << low_bit), swap(b_send, "bucket", 1 << high_bit)]
        self.turn += 1
        self.count //= 2
        return self.done

    def second(self, *after, micros=0):
        while self.turn < self.bits:
            (am, bm), (ag, bg) = self.mine, self.flight
            spots = [[(0, 0, 0), (0, 0, 0)]]
            block = (self.unit_count,) + self.tail
            arrays = [am, ag, am, ag, bm, bg, bm, bg]
            self.depart(
                arrays, [block], spots, [self.unit_count], after, "sum_second", micros
            )
        return self.done


class Cross:
    def __init__(self, packages, *after, micros=0):
        self.place = packages[0].place
        self.kinds = [p.kinds for p in packages]
        unit, width = packages[0].tail
        self.tiles = sum(4 if by_rows else 2 for kinds in self.kinds for by_rows in kinds)
        self.tail = (unit // 4, width)
        arrays = []
        for p in packages:
            arrays += [p.mine[0], p.flight[0], p.mine[1], p.flight[1]]
        self.rows = -(-self.tiles * self.tail[0] // 16) * 16
        shape = like(BF16, 2, self.rows, width)
        (self.mine, send), self.done = small_call(
            functools.partial(cross_kernel, self.kinds, self.tail[0]), self.place, arrays, shape, after, "cross",
            micros,
        )
        self.flight = swap(send, "seq", 1)

    def last(self, *after):
        shape = like(BF16, self.rows, self.tail[1])
        (self.mine, send), self.done = small_call(
            last_kernel, self.place, [self.mine, self.flight], shape, after, "last"
        )
        self.flight = swap(send, "seq", 2)
        return self.done

    def total(self, *after):
        return launch(
            total_kernel,
            [like(F32, *self.mine.shape)],
            in_specs=vmem_specs(2),
            out_specs=vmem_specs(1),
            after=after,
            vmem=24,
            name="total",
        )(self.mine, self.flight)

    def results(self, total):
        out, at = [], 0
        share = self.tail[0]
        for kinds in self.kinds:
            for by_rows in kinds:
                if by_rows:
                    out.append(total[at : at + 4 * share])
                    at += 4 * share
                else:
                    sides = [total[at : at + share], total[at + share : at + 2 * share]]
                    out.append(jnp.concatenate(sides, 1))
                    at += 2 * share
        return out


def notes_kernel(blocks, early_ref, late_ref, early_cond, late_cond, out_ref, early_sum, late_sum):
    width = early_ref.shape[1]
    for part in range(6):
        if part < 2:
            ref, cond, count, which = late_ref, late_cond, 2, part
        else:
            ref, cond, count, which = early_ref, early_cond, 4, part - 2
        inside = lax.broadcasted_iota(jnp.int32, cond.shape, 0) % ref_pitch(ref, early_ref, late_ref)
        mine = (inside % count == which) & (inside < count * blocks)
        picked = jnp.where(mine, cond[...].astype(F32), 0.0).astype(BF16)
        out_ref[:, part * width : (part + 1) * width] = contract(picked, ref[...], 0, 0)
    for ref, total in ((early_ref, early_sum), (late_ref, late_sum)):
        pitch = ref_pitch(ref, early_ref, late_ref)
        shape = (NOTES, ref.shape[0])
        kind = lax.broadcasted_iota(jnp.int32, shape, 0)
        row = lax.broadcasted_iota(jnp.int32, shape, 1) % pitch
        total[...] = contract(jnp.where(kind == row, 1.0, 0.0).astype(BF16), ref[...], 1, 0)


def ref_pitch(ref, early_ref, late_ref):
    return NOTES if ref is early_ref else NOTES * late_ref.shape[0] // early_ref.shape[0]


def notes_part(early, late, early_cond, late_cond, blocks):
    width = early.shape[1]
    return launch(
        functools.partial(notes_kernel, blocks),
        [
            like(F32, early_cond.shape[1], 6 * width),
            like(F32, NOTES, width),
            like(F32, NOTES, width),
        ],
        in_specs=vmem_specs(4),
        out_specs=vmem_specs(3),
        vmem=32,
        name="notes_part",
    )(early, late, early_cond, late_cond)


def on_device(
    tokens,
    segment,
    keep_route,
    condition,
    group_bucket,
    head_mask,
    channel_mask,
    ada_weight,
    ada_bias,
    qkv_weight,
    query_bias,
    value_bias,
    proj_weight,
    proj_bias,
    inner_weight,
    inner_bias,
    outer_weight,
    outer_bias,
    cotangent,
):
    rows, width = tokens.shape
    slots = condition.shape[0]
    hidden = inner_weight.shape[1]
    group_count = lax.axis_size("bucket")
    seq_count = lax.axis_size("seq")
    bucket = lax.axis_index("bucket")
    seq = lax.axis_index("seq")
    core = bucket % 2
    piece = rows // slots
    block = piece * seq_count
    blocks = rows // block
    place = jnp.stack([core, seq, bucket]).astype(jnp.int32)
    row_share = width // group_count
    aligned = row_share % 16 == 0

    def turned(array):
        split = array.reshape(group_count // 2, 2, row_share, rows)
        if aligned:
            return split
        keep, send = split_bit(split, 1, core)
        return jnp.stack([keep, send]).reshape(1, 2, width // 2, rows)

    turned_core = place[:1] if aligned else jnp.zeros((1,), jnp.int32)

    seg_other = swap(segment, "bucket", 1)
    bucket_other = swap(group_bucket, "bucket", 1)
    tokens_own = tokens.reshape(slots, piece, width)
    tokens_other = swap(tokens_own, "bucket", 1)
    cond_other = swap(condition, "bucket", 1)
    route_columns = jnp.broadcast_to(keep_route.astype(BF16)[:, None], (rows, LANES))
    payload = jnp.concatenate([cotangent, route_columns], 1).reshape(slots, piece, width + LANES)

    (
        send_which, send_index, back_which, back_index, cond_which, cond_row, flags, keep_heads,
        keep_channels, kept,
    ) = make_plan(
        place, segment, seg_other, group_bucket, bucket_other, head_mask, channel_mask, slots,
        piece, seq_count, blocks,
    )

    def bring(pieces):
        return [pieces[0]] + [swap(pieces[k], "seq", k) for k in range(1, seq_count)]

    x_sent, x_mark = send_blocks(tokens_own, tokens_other, send_which, send_index, seq_count, blocks)
    x_parts = bring(x_sent)
    payload = hold(payload, x_mark)
    payload_other = swap(payload, "bucket", 1)
    mod, cond_act = modulate(
        cond_which, cond_row, condition, cond_other, ada_weight, ada_bias, blocks, width,
        (payload_other,),
    )
    payload_sent, _ = send_blocks(
        payload, payload_other, send_which, send_index, seq_count, blocks, (x_parts[3],)
    )
    payload_parts = bring(payload_sent)
    pair_bias = jnp.concatenate([jnp.zeros_like(value_bias), value_bias])[None, :]
    x, normed_one, one_turned, own_kv = enter(x_parts, mod, qkv_weight, pair_bias, blocks)
    other_kv = swap(own_kv, "bucket", 1)
    queries = linear(normed_one, qkv_weight, query_bias, width, width // 3)
    attended, lse = attend(queries, own_kv, other_kv, flags, keep_heads, kept, blocks)
    branch_one, middle, normed_two, two_turned, att_turned, grad_branch_two, grad_outer_bias = (
        middle_part(payload_parts, attended, proj_weight, proj_bias, x, mod, blocks)
    )

    share = hidden // group_count
    by_rows = (group_count // 2, row_share, -1)
    chunk = 2 * width // 3
    feed_args = (
        turned_core, keep_channels, normed_two, grad_branch_two, turned(two_turned),
        inner_bias[None, :], inner_weight, outer_weight, blocks, chunk, FEED_SUB,
    )
    (branch_two, grad_two, act_a, wi_keep, wi_send, hidden_a), _ = feed(*feed_args, 0, 3)
    inner = Package(place, (wi_keep.reshape(by_rows), wi_send.reshape(by_rows)))
    (branch_two, grad_two, act_b, wi_keep, wi_send, hidden_b), mark = feed(
        *feed_args, 3, 3, (branch_two, grad_two)
    )
    mark = inner.first(mark)
    (wo_keep, wo_send), mark = outer_part(
        place[:1], [act_a, act_b], grad_branch_two, share, width, (mark,)
    )
    by_units = (group_count // 2, 4, share // 4, width)
    rest = Package(
        place,
        (wi_keep.reshape(by_rows), wi_send.reshape(by_rows)),
        (wo_keep.reshape(by_units), wo_send.reshape(by_units)),
    )
    (out_stay, out_odd, out_even, early, grad_middle, grad_branch_one, grad_attended, delta), mark = (
        turn_part(
            payload_parts, keep_heads, branch_two, grad_two, middle, branch_one, attended, mod,
            outer_bias, proj_weight, cond_act, (grad_outer_bias, hidden_a, hidden_b), blocks,
            (mark,),
        )
    )
    mark = inner.second(mark)
    mark = rest.first(mark)
    out_near = swap(out_odd, "seq", 1)
    early_all = lax.all_gather(early, ("bucket", "seq"), axis=0, tiled=True)

    (grad_queries, grad_own, grad_other), mark = attend_back(
        queries, own_kv, other_kv, grad_attended, lse, delta, flags, keep_heads, kept, blocks,
        (mark,),
    )
    grad_got = swap(grad_other, "bucket", 1)
    out_relay, mark = relay(out_even, out_near, (mark,))
    out_far = swap(out_relay, "seq", 2)
    inner_cross = Cross([inner], mark)
    (pq_keep, pq_send, grad_one_part, query_sum), mark = query_back(
        turned_core, turned(att_turned), turned(one_turned), grad_branch_one, grad_queries,
        qkv_weight, (inner_cross.done,),
    )
    mark = rest.second(mark, micros=500)
    mark = inner_cross.last(mark)
    (kv_keep, kv_send, x_stay, x_odd, x_even, late), mark = leave(
        turned_core, turned(one_turned), grad_own, grad_got, qkv_weight, grad_one_part, x,
        grad_middle, mod, query_sum, blocks, piece, (mark,),
    )
    projections = Package(
        place,
        (pq_keep.reshape(by_rows), pq_send.reshape(by_rows)),
        (kv_keep.reshape(by_rows), kv_send.reshape(by_rows)),
    )
    x_near = swap(x_odd, "seq", 1)
    late_all = lax.all_gather(late, ("bucket", "seq"), axis=0, tiled=True)

    (inner_sum,), mark = inner_cross.total(mark)
    out_own, mark = collect(out_stay, out_near, out_far, (mark,))
    out_other = swap(out_own, "bucket", 1)
    rest_cross = Cross([rest], mark, micros=500)
    mark = projections.first(rest_cross.done)
    x_relay, mark = relay(x_even, x_near, (mark,), 500)
    x_far = swap(x_relay, "seq", 2)
    mark = rest_cross.last(mark)
    block_out, mark = pick_blocks(
        out_own, out_other, back_which, back_index, BF16, (mark,), 500
    )
    mark = projections.second(mark)
    x_own, mark = collect(x_stay, x_near, x_far, (mark,))
    x_other = swap(x_own, "bucket", 1)
    projections_cross = Cross([projections], mark)
    (rest_sum,), mark = rest_cross.total(projections_cross.done)
    grad_tokens, mark = pick_blocks(x_own, x_other, back_which, back_index, F32, (mark,))
    mark = projections_cross.last(mark)
    (projections_sum,), mark = projections_cross.total(mark)
    block_out = block_out.reshape(rows, width)
    grad_tokens = grad_tokens.reshape(rows, width)
    (inner_a,) = inner_cross.results(inner_sum)
    inner_b, grad_outer_weight = rest_cross.results(rest_sum)
    grad_inner_weight = jnp.concatenate([inner_a, inner_b], 1)
    proj_query, key_value = projections_cross.results(projections_sum)
    grad_proj_weight = proj_query[:, :width]
    grad_qkv_weight = jnp.concatenate([proj_query[:, width:], key_value], 1)

    early_all = hold(early_all, projections_cross.done)
    late_all = hold(late_all, projections_cross.done)
    spot = bucket * seq_count + seq
    device_count = group_count * seq_count
    columns = width // device_count
    cond_mine = lax.dynamic_slice_in_dim(early_all, spot * columns, columns, 1)
    cond_mine = cond_mine.reshape(device_count, NOTES, columns)[:, NOTES - blocks :]

    def at_rows(parts, pitch):
        spread = jnp.broadcast_to(
            cond_mine[:, :, None, :], (device_count, blocks, parts, columns)
        ).reshape(device_count, blocks * parts, columns)
        rest = jnp.zeros((device_count, pitch - blocks * parts, columns), BF16)
        return jnp.concatenate([spread, rest], 1).reshape(device_count * pitch, columns)

    (grad_ada_weight, early_sum, late_sum), _ = notes_part(
        early_all, late_all, at_rows(4, NOTES), at_rows(2, NOTES), blocks
    )

    def own_part(array):
        array = array.reshape(-1)
        size = array.shape[0] // device_count
        return lax.dynamic_slice_in_dim(array, spot * size, size, 0)

    ada_rows = jnp.concatenate(
        [
            sum(late_sum[2 * s : 2 * s + 2] for s in range(blocks)),
            sum(early_sum[4 * s : 4 * s + 4] for s in range(blocks)),
        ],
        0,
    )
    at = 4 * blocks
    return (
        block_out,
        grad_tokens,
        grad_ada_weight,
        own_part(ada_rows),
        grad_qkv_weight,
        own_part(late_sum[2 * blocks]),
        own_part(late_sum[2 * blocks + 1]),
        grad_proj_weight,
        own_part(early_sum[at]),
        grad_inner_weight,
        own_part(early_sum[at + 2 : at + 6]),
        grad_outer_weight,
        own_part(early_sum[at + 1]),
    )


def solution(mesh):
    split = P(("bucket", "seq"))
    split_rows = P(("bucket", "seq"), None)
    return jax.shard_map(
        on_device,
        mesh=mesh,
        in_specs=(split_rows, split, split, P("bucket", None), P("bucket"))
        + (P(),) * 13
        + (split_rows,),
        out_specs=(
            split_rows,
            split_rows,
            split_rows,
            split,
            split_rows,
            split,
            split,
            split_rows,
            split,
            split_rows,
            split,
            split_rows,
            split,
        ),
        check_vma=False,
    )
```

```python
import functools

import jax
import jax.numpy as jnp
from jax import lax
from jax.experimental import pallas as pl
from jax.experimental.pallas import tpu as pltpu
from jax.sharding import PartitionSpec as P

EPSILON = 1e-06
LOG2E = 1.4426950408889634
LANES = 128
NOTES = 16
LONG_HEADS = 4
LONG_BACK = 2
SHORT_HEADS = 4
FEED_VMEM = 60
FEED_SUB = 768
GELU_A = 0.7978845608028654
GELU_B = 0.044715
F32 = jnp.float32
BF16 = jnp.bfloat16


def contract(left, right, left_dim, right_dim, out=F32):
    return lax.dot_general(
        left, right, (((left_dim,), (right_dim,)), ((), ())), preferred_element_type=out
    )


def swap(array, axis, bit):
    size = lax.axis_size(axis)
    return lax.ppermute(array, axis, [(i, i ^ bit) for i in range(size)])


def launch(
    body, out_shape, *, in_specs, out_specs, name, after=(), grid=(), prefetch=0, scratch=(),
    aliases=None, vmem=56, micros=0,
):
    lead = prefetch + len(in_specs)
    waits, outs = len(after), len(out_shape)

    def kernel(*refs):
        rest = refs[lead + waits :]
        body(*refs[:lead], *rest[:outs], *rest[outs + 1 :])
        rest[outs][...] = jnp.zeros(rest[outs].shape, F32)

    token = (8, LANES)
    specs = dict(
        in_specs=list(in_specs) + [pl.BlockSpec(memory_space=pl.ANY)] * waits,
        scratch_shapes=list(scratch),
    )
    if grid:
        specs = dict(
            grid_spec=pltpu.PrefetchScalarGridSpec(
                num_scalar_prefetch=prefetch,
                grid=grid,
                out_specs=list(out_specs) + [pl.BlockSpec(token, lambda *i: (0, 0))],
                **specs,
            )
        )
    else:
        specs["out_specs"] = list(out_specs) + [pl.BlockSpec(memory_space=pltpu.VMEM)]
    call = pl.pallas_call(
        kernel,
        out_shape=list(out_shape) + [jax.ShapeDtypeStruct(token, F32)],
        input_output_aliases=aliases or {},
        compiler_params=pltpu.CompilerParams(vmem_limit_bytes=vmem * 1024 * 1024),
        cost_estimate=pl.CostEstimate(
            flops=int(micros * 1000000000), bytes_accessed=0, transcendentals=0
        ),
        name=name,
        **specs,
    )

    def run(*operands):
        *results, mark = call(*operands, *after)
        return results, mark

    return run


def vmem_specs(count):
    return [pl.BlockSpec(memory_space=pltpu.VMEM)] * count


def smem_specs(count):
    return [pl.BlockSpec(memory_space=pltpu.SMEM)] * count


def like(dtype, *shape):
    return jax.ShapeDtypeStruct(shape, dtype)


def hold_kernel(array_ref, *refs):
    pass


def hold(array, *after):
    anywhere = [pl.BlockSpec(memory_space=pl.ANY)]
    return pl.pallas_call(
        hold_kernel,
        in_specs=anywhere * (1 + len(after)),
        out_specs=anywhere[0],
        out_shape=like(array.dtype, *array.shape),
        input_output_aliases={0: 0},
        cost_estimate=pl.CostEstimate(flops=0, bytes_accessed=0, transcendentals=0),
        name="hold",
    )(array, *after)


def plan_kernel(
    slots, piece, chips, blocks, place_ref, seg_own, seg_other, bucket_own, bucket_other,
    head_mask, channel_mask, send_which, send_index, back_which, back_index, cond_which,
    cond_row, flags, keep_heads, keep_channels, kept, order_ref, rank_ref, id_ref, long_ref,
):
    core = place_ref[0]
    seq = place_ref[1]
    total = 2 * slots
    ids, keys = [], []
    for i in range(total):
        at = (i % slots) * piece
        ids.append(jnp.where(core == i // slots, seg_own[at], seg_other[at]))
    for i in range(total):
        base = (i // slots) * slots
        equal = jnp.int32(0)
        for j in range(slots):
            equal += jnp.where(ids[base + j] == ids[i], 1, 0)
        is_long = jnp.where(equal > 1, 1, 0)
        id_ref[i] = ids[i]
        long_ref[i] = is_long
        keys.append(jnp.where(is_long == 1, i, total + i))
    for i in range(total):
        rank = jnp.int32(0)
        for j in range(total):
            rank += jnp.where(keys[j] < keys[i], 1, 0)
        rank_ref[i] = rank
        order_ref[rank] = jnp.int32(i)
    for k in range(chips):
        for s in range(blocks):
            item = order_ref[((seq ^ k) * 2 + core) * blocks + s]
            send_which[k * blocks + s] = jnp.where(item // slots == core, 0, 1)
            send_index[k * blocks + s] = item % slots
    for j in range(slots):
        rank = rank_ref[core * slots + j]
        back_which[j] = jnp.where((rank // blocks) % 2 == core, 0, 1)
        back_index[j] = ((rank // (2 * blocks)) ^ seq) * blocks + rank % blocks
    flags[0] = long_ref[order_ref[seq * 2 * blocks]]
    flags[1] = core
    heads = head_mask.shape[1]
    groups = channel_mask.shape[1]
    for s in range(blocks):
        item = order_ref[(seq * 2 + core) * blocks + s]
        other = jnp.where(item // slots == core, 0, 1)
        cond_which[s] = other
        cond_row[s] = id_ref[item]
        step = jnp.where(other == 0, bucket_own[0], bucket_other[0])
        count = jnp.int32(0)
        for h in range(heads):
            keep = head_mask[step, h]
            keep_heads[s * heads + h] = keep
            kept[s * heads + h] = jnp.int32(0)

            @pl.when(keep == 1)
            def _():
                kept[s * heads + count] = jnp.int32(h)

            count += keep
        kept[blocks * heads + s] = count
        last = kept[s * heads + jnp.maximum(count - 1, 0)]
        for h in range(heads):

            @pl.when(h >= count)
            def _():
                kept[s * heads + h] = last

        for f in range(groups):
            keep_channels[s * groups + f] = channel_mask[step, f]


def make_plan(place, segment, seg_other, bucket, bucket_other, head_mask, channel_mask, slots, piece,
              chips, blocks):
    smem = pl.BlockSpec(memory_space=pltpu.SMEM)
    sizes = [chips * blocks] * 2 + [slots] * 2 + [blocks] * 2 + [2]
    sizes += [blocks * head_mask.shape[1], blocks * channel_mask.shape[1]]
    sizes += [blocks * head_mask.shape[1] + blocks]
    return pl.pallas_call(
        functools.partial(plan_kernel, slots, piece, chips, blocks),
        in_specs=[smem] * 7,
        out_specs=[smem] * 10,
        out_shape=[jax.ShapeDtypeStruct((n,), jnp.int32) for n in sizes],
        scratch_shapes=[pltpu.SMEM((2 * slots,), jnp.int32)] * 4,
        cost_estimate=pl.CostEstimate(flops=0, bytes_accessed=8000000, transcendentals=0),
        name="make_plan",
    )(place, segment, seg_other, bucket, bucket_other, head_mask, channel_mask)


def send_kernel(blocks, which_ref, index_ref, own_ref, other_ref, *outs):
    for m in range(len(outs) * blocks):

        @pl.when(which_ref[m] == 0)
        def _():
            outs[m // blocks][m % blocks] = own_ref[index_ref[m]]

        @pl.when(which_ref[m] != 0)
        def _():
            outs[m // blocks][m % blocks] = other_ref[index_ref[m]]


def send_blocks(own, other, which, index, chips, blocks, after=()):
    _, rows, width = own.shape
    return launch(
        functools.partial(send_kernel, blocks),
        [like(own.dtype, blocks, rows, width)] * chips,
        in_specs=smem_specs(2) + vmem_specs(2),
        out_specs=vmem_specs(chips),
        after=after,
        vmem=16,
        name="send_blocks",
    )(which, index, own, other)


def pick_kernel(which_ref, index_ref, own_ref, other_ref, out_ref):
    for m in range(out_ref.shape[0]):

        @pl.when(which_ref[m] == 0)
        def _():
            out_ref[m] = own_ref[index_ref[m]].astype(out_ref.dtype)

        @pl.when(which_ref[m] != 0)
        def _():
            out_ref[m] = other_ref[index_ref[m]].astype(out_ref.dtype)


def pick_blocks(own, other, which, index, out_dtype, after=(), micros=0):
    _, rows, width = own.shape
    (out,), mark = launch(
        pick_kernel,
        [like(out_dtype, index.shape[0], rows, width)],
        in_specs=smem_specs(2) + vmem_specs(2),
        out_specs=vmem_specs(1),
        after=after,
        vmem=16,
        micros=micros,
        name="pick_blocks",
    )(which, index, own, other)
    return out, mark


def leaving(k, s, value, stay_ref, odd_ref, even_ref):
    rows = value.shape[0]
    if k == 0:
        stay_ref[s] = value
        return
    target = even_ref if k == 2 else odd_ref
    first = ((k // 2 if k % 2 else 0) * stay_ref.shape[0] + s) * rows
    target[first : first + rows] = value


def leaving_shapes(blocks, piece, width):
    count = blocks * piece
    return [
        like(BF16, blocks, piece, width),
        like(BF16, 2 * count, width),
        like(BF16, count, width),
        like(BF16, NOTES, width),
    ]


def relay_kernel(even_ref, near_ref, out_ref):
    count = even_ref.shape[0]
    out_ref[:count] = even_ref[...]
    out_ref[count:] = near_ref[count:]


def relay(even, near, after=(), micros=0):
    count, width = even.shape
    (out,), mark = launch(
        relay_kernel,
        [like(BF16, 2 * count, width)],
        in_specs=vmem_specs(2),
        out_specs=vmem_specs(1),
        after=after,
        vmem=16,
        micros=micros,
        name="relay",
    )(even, near)
    return out, mark


def collect_kernel(stay_ref, near_ref, far_ref, out_ref):
    blocks, rows, width = stay_ref.shape
    count = blocks * rows
    out_ref[:blocks] = stay_ref[...]
    for k, part in enumerate((near_ref[:count], far_ref[:count], far_ref[count:])):
        out_ref[(k + 1) * blocks : (k + 2) * blocks] = part.reshape(blocks, rows, width)


def collect(stay, near, far, after=(), micros=0):
    blocks, rows, width = stay.shape
    (out,), mark = launch(
        collect_kernel,
        [like(BF16, 4 * blocks, rows, width)],
        in_specs=vmem_specs(3),
        out_specs=vmem_specs(1),
        after=after,
        vmem=16,
        micros=micros,
        name="collect",
    )(stay, near, far)
    return out, mark


def modulate_kernel(
    blocks, which_ref, row_ref, own_ref, other_ref, weight_ref, bias_ref, out_ref, act_ref, held
):
    @pl.when(pl.program_id(0) == 0)
    def _():
        slots, width = own_ref.shape
        picked = []
        for s in range(blocks):
            hot = lax.broadcasted_iota(jnp.int32, (slots, width), 0) == row_ref[s]
            source = jnp.where(which_ref[s] == 0, own_ref[...].astype(F32), other_ref[...].astype(F32))
            picked.append(jnp.sum(jnp.where(hot, source, 0.0), 0, keepdims=True))
        picked.append(jnp.zeros((16 - blocks, width), F32))
        value = jnp.concatenate(picked, 0)
        held[...] = (value / (1.0 + jnp.exp(-value))).astype(BF16)
        act_ref[...] = held[...]

    out_ref[...] = (contract(held[...], weight_ref[...], 1, 0) + bias_ref[...])[:8]


def modulate(which, row, own, other, weight, bias, blocks, chunk, after=()):
    slots, width = own.shape
    columns = weight.shape[1]
    return launch(
        functools.partial(modulate_kernel, blocks),
        [like(F32, 8, columns), like(BF16, 16, width)],
        grid=(columns // chunk,),
        in_specs=smem_specs(2)
        + [
            pl.BlockSpec((slots, width), lambda i: (0, 0)),
            pl.BlockSpec((slots, width), lambda i: (0, 0)),
            pl.BlockSpec((width, chunk), lambda i: (0, i)),
            pl.BlockSpec((1, chunk), lambda i: (0, i)),
        ],
        out_specs=[
            pl.BlockSpec((8, chunk), lambda i: (0, i)),
            pl.BlockSpec((16, width), lambda i: (0, 0)),
        ],
        scratch=[pltpu.VMEM((16, width), BF16)],
        after=after,
        vmem=32,
        micros=0,
        name="modulate",
    )(which, row, own, other, weight, bias[None, :])[0]


def norm_parts(value):
    center = value - jnp.mean(value, -1, keepdims=True)
    spread = jnp.mean(center * center, -1, keepdims=True)
    inverse = lax.rsqrt(spread + EPSILON)
    return center * inverse, inverse


def norm_back(grad, normed, inverse, scale):
    scaled = grad * (1.0 + scale)
    mean_one = jnp.mean(scaled, -1, keepdims=True)
    mean_two = jnp.mean(scaled * normed, -1, keepdims=True)
    return inverse * (scaled - mean_one - normed * mean_two)


def mod_row(mod_ref, index, part, width):
    return mod_ref[index : index + 1, part * width : (part + 1) * width]


def enter_kernel(blocks, *refs):
    parts = refs[:-8]
    mod_ref, weight_ref, bias_ref, x_ref, one_ref, turned_ref, kv_ref, held = refs[-8:]
    _, piece, width = parts[0].shape
    block = held.shape[0] // blocks

    @pl.when(pl.program_id(0) == 0)
    def _():
        for s in range(blocks):
            for k, part in enumerate(parts):
                first = s * block + k * piece
                x = part[s]
                x_ref[first : first + piece] = x
                normed, _ = norm_parts(x.astype(F32))
                one = normed * (1.0 + mod_row(mod_ref, s, 1, width)) + mod_row(mod_ref, s, 0, width)
                held[first : first + piece] = one.astype(BF16)
        one_ref[...] = held[...]
        turned_ref[...] = held[...].T

    kv_ref[...] = (contract(held[...], weight_ref[...], 1, 0) + bias_ref[...]).astype(BF16)


def enter(parts, mod, weight, bias, blocks):
    _, piece, width = parts[0].shape
    rows = piece * blocks * len(parts)
    const = lambda shape: pl.BlockSpec(shape, lambda i: (0,) * len(shape))
    return pl.pallas_call(
        functools.partial(enter_kernel, blocks),
        grid=(2,),
        in_specs=[const(p.shape) for p in parts]
        + [
            const((8, 2 * width)),
            pl.BlockSpec((width, width), lambda i: (0, 1 + i)),
            pl.BlockSpec((1, width), lambda i: (0, i)),
        ],
        out_specs=[
            const((rows, width)),
            const((rows, width)),
            const((width, rows)),
            pl.BlockSpec((rows, width), lambda i: (0, i)),
        ],
        out_shape=[
            jax.ShapeDtypeStruct((rows, width), BF16),
            jax.ShapeDtypeStruct((rows, width), BF16),
            jax.ShapeDtypeStruct((width, rows), BF16),
            jax.ShapeDtypeStruct((rows, 2 * width), BF16),
        ],
        scratch_shapes=[pltpu.VMEM((rows, width), BF16)],
        compiler_params=pltpu.CompilerParams(vmem_limit_bytes=48 * 1024 * 1024),
        cost_estimate=pl.CostEstimate(
            flops=8 * rows * width * width, bytes_accessed=12 * width * width, transcendentals=0
        ),
        name="enter",
    )(*parts, mod, weight, bias)


def linear_kernel(x_ref, weight_ref, bias_ref, out_ref):
    out_ref[...] = (contract(x_ref[...], weight_ref[...], 1, 0) + bias_ref[...]).astype(out_ref.dtype)


def linear(x, weight, bias, columns, chunk):
    rows, width = x.shape
    return pl.pallas_call(
        linear_kernel,
        grid=(columns // chunk,),
        in_specs=[
            pl.BlockSpec((rows, width), lambda i: (0, 0)),
            pl.BlockSpec((width, chunk), lambda i: (0, i)),
            pl.BlockSpec((1, chunk), lambda i: (0, i)),
        ],
        out_specs=pl.BlockSpec((rows, chunk), lambda i: (0, i)),
        out_shape=jax.ShapeDtypeStruct((rows, columns), BF16),
        compiler_params=pltpu.CompilerParams(vmem_limit_bytes=32 * 1024 * 1024),
        cost_estimate=pl.CostEstimate(
            flops=4 * rows * width * columns, bytes_accessed=8 * width * columns, transcendentals=0
        ),
        name="linear",
    )(x, weight, bias[None, :])


def middle_kernel(blocks, *refs):
    parts = refs[:-12]
    (
        att_ref, weight_ref, bias_ref, x_ref, mod_ref,
        branch_ref, middle_ref, two_ref, two_turned, att_turned, grad_ref, bias_grad,
    ) = refs[-12:]
    rows, width = x_ref.shape
    block = rows // blocks
    piece = parts[0].shape[1]
    att_turned[...] = att_ref[...].T
    total = jnp.zeros((1, width), F32)
    for s in range(blocks):
        part = slice(s * block, (s + 1) * block)
        branch = contract(att_ref[part], weight_ref[...], 1, 0) + bias_ref[...]
        branch_ref[part] = branch
        middle = x_ref[part].astype(F32) + mod_row(mod_ref, s, 2, width) * branch
        middle_ref[part] = middle
        normed, _ = norm_parts(middle)
        two_ref[part] = (
            normed * (1.0 + mod_row(mod_ref, s, 4, width)) + mod_row(mod_ref, s, 3, width)
        ).astype(BF16)
        for k, source in enumerate(parts):
            first = s * block + k * piece
            payload = source[s].astype(F32)
            grad = (payload[:, width : width + 1] * mod_row(mod_ref, s, 5, width) * payload[:, :width]).astype(BF16)
            grad_ref[first : first + piece] = grad
            total += jnp.sum(grad.astype(F32), 0, keepdims=True)
    two_turned[...] = two_ref[...].T
    bias_grad[...] = total


def middle_part(parts, attended, weight, bias, x, mod, blocks):
    rows, width = x.shape
    vmem = pl.BlockSpec(memory_space=pltpu.VMEM)
    return pl.pallas_call(
        functools.partial(middle_kernel, blocks),
        in_specs=[vmem] * (len(parts) + 5),
        out_specs=[vmem] * 7,
        out_shape=[
            jax.ShapeDtypeStruct((rows, width), F32),
            jax.ShapeDtypeStruct((rows, width), F32),
            jax.ShapeDtypeStruct((rows, width), BF16),
            jax.ShapeDtypeStruct((width, rows), BF16),
            jax.ShapeDtypeStruct((width, rows), BF16),
            jax.ShapeDtypeStruct((rows, width), BF16),
            jax.ShapeDtypeStruct((1, width), F32),
        ],
        compiler_params=pltpu.CompilerParams(vmem_limit_bytes=48 * 1024 * 1024),
        cost_estimate=pl.CostEstimate(
            flops=8 * rows * width * width, bytes_accessed=24 * rows * width, transcendentals=0
        ),
        name="middle_part",
    )(*parts, attended, weight, bias[None, :], x, mod)


def turn_kernel(blocks, heads, *refs):
    count = 4
    parts = refs[:count]
    (
        keep_ref, out_ref, gx_ref, middle_ref, branch_ref, att_ref, mod_ref, bias_ref, weight_ref,
        act_ref, outer_sum, *hidden_sums,
    ) = refs[count:-8]
    stay_ref, odd_ref, even_ref, notes_ref, grad_middle, grad_one, grad_att, delta_ref = refs[-8:]
    notes = []
    rows, width = middle_ref.shape
    block = rows // blocks
    piece = parts[0].shape[1]
    head_width = width // heads
    column_head = lax.broadcasted_iota(jnp.int32, (heads, width), 1) // head_width
    hot = (column_head == lax.broadcasted_iota(jnp.int32, (heads, width), 0)).astype(F32)
    bias_total = jnp.zeros((1, width), F32)
    for s in range(blocks):
        sums = [jnp.zeros((1, width), F32) for _ in range(4)]
        gate_one = mod_row(mod_ref, s, 2, width)
        scale_two = mod_row(mod_ref, s, 4, width)
        gate_two = mod_row(mod_ref, s, 5, width)
        for k, source in enumerate(parts):
            first = s * block + k * piece
            part = slice(first, first + piece)
            payload = source[s].astype(F32)
            upstream = payload[:, :width]
            route = payload[:, width : width + 1]
            middle = middle_ref[part]
            branch_two = route * (out_ref[part] + bias_ref[...])
            leaving(k, s, (middle + gate_two * branch_two).astype(BF16), stay_ref, odd_ref, even_ref)
            sums[3] += jnp.sum(branch_two * upstream, 0, keepdims=True)
            grad_two = gx_ref[part]
            normed, inverse = norm_parts(middle)
            sums[1] += jnp.sum(grad_two, 0, keepdims=True)
            sums[2] += jnp.sum(grad_two * normed, 0, keepdims=True)
            grad = upstream + norm_back(grad_two, normed, inverse, scale_two)
            grad_middle[part] = grad
            sums[0] += jnp.sum(grad * branch_ref[part], 0, keepdims=True)
            low = (gate_one * grad).astype(BF16)
            grad_one[part] = low
            bias_total += jnp.sum(low.astype(F32), 0, keepdims=True)
        notes += sums
        part = slice(s * block, (s + 1) * block)
        row = jnp.zeros((1, width), F32)
        for h in range(heads):
            row = jnp.where(
                hot[h : h + 1] > 0.5, keep_ref[s * heads + h].astype(F32), row
            )
        low = contract(grad_one[part], weight_ref[...], 1, 1).astype(BF16).astype(F32) * row
        grad_att[part] = low.astype(BF16)
        delta_ref[:, part] = lax.dot_general(
            hot,
            low * att_ref[part].astype(F32),
            (((1,), (1,)), ((), ())),
            precision=lax.Precision.HIGHEST,
            preferred_element_type=F32,
        )
    notes.append(bias_total)
    notes.append(outer_sum[...])
    for ref in hidden_sums:
        notes += [ref[:, lo : lo + width] for lo in range(0, ref.shape[1], width)]
    notes.append(act_ref[:blocks].astype(F32))
    notes_ref[...] = jnp.concatenate(notes, 0).astype(BF16)


def turn_part(
    parts, keep, out, gx, middle, branch, attended, mod, bias, weight, act, sums, blocks, after=()
):
    rows, width = middle.shape
    heads = keep.shape[0] // blocks
    return launch(
        functools.partial(turn_kernel, blocks, heads),
        leaving_shapes(blocks, parts[0].shape[1], width)
        + [
            like(F32, rows, width),
            like(BF16, rows, width),
            like(BF16, rows, width),
            like(F32, heads, rows),
        ],
        in_specs=vmem_specs(len(parts)) + smem_specs(1) + vmem_specs(9 + len(sums)),
        out_specs=vmem_specs(8),
        after=after,
        vmem=48,
        micros=500,
        name="turn_part",
    )(*parts, keep, out, gx, middle, branch, attended, mod, bias[None, :], weight, act, *sums)


def query_back_kernel(
    core_ref, proj_keep, proj_send, one_keep, one_send, grad_one, grad_q, weight_ref, *refs
):
    keep_ref, send_ref, gx_ref, sum_ref = refs[-4:]
    width = grad_q.shape[1]
    half = keep_ref.shape[0]
    rows = grad_q.shape[0]
    turned = lambda ref: ref[...].reshape(half, rows)
    keep_ref[:, :width] = contract(turned(proj_keep), grad_one[...], 1, 0).astype(BF16)
    send_ref[:, :width] = contract(turned(proj_send), grad_one[...], 1, 0).astype(BF16)
    keep_ref[:, width:] = contract(turned(one_keep), grad_q[...], 1, 0).astype(BF16)
    send_ref[:, width:] = contract(turned(one_send), grad_q[...], 1, 0).astype(BF16)
    gx_ref[...] = contract(grad_q[...], weight_ref[...], 1, 1)
    sum_ref[...] = jnp.sum(grad_q[...].astype(F32), 0, keepdims=True)


def turned_specs(array):
    pairs, _, share, rows = array.shape
    keep = pl.BlockSpec((pairs, None, share, rows), lambda i, c: (0, c[0], 0, 0))
    send = pl.BlockSpec((pairs, None, share, rows), lambda i, c: (0, 1 - c[0], 0, 0))
    return [keep, send]


def query_back(core, att_turned, one_turned, grad_one, grad_q, weight, after=()):
    rows, width = grad_q.shape
    half = width // 2
    const = lambda shape: pl.BlockSpec(shape, lambda i, c: (0,) * len(shape))
    return launch(
        query_back_kernel,
        [
            like(BF16, half, 2 * width),
            like(BF16, half, 2 * width),
            like(F32, rows, width),
            like(F32, 1, width),
        ],
        prefetch=1,
        grid=(1,),
        in_specs=turned_specs(att_turned)
        + turned_specs(one_turned)
        + [const((rows, width)), const((rows, width)), const((width, width))],
        out_specs=[
            const((half, 2 * width)),
            const((half, 2 * width)),
            const((rows, width)),
            const((1, width)),
        ],
        after=after,
        micros=0,
        name="query_back",
    )(core, att_turned, att_turned, one_turned, one_turned, grad_one, grad_q, weight)


def leave_kernel(
    blocks, core_ref, one_keep, one_send, own_ref, got_ref, weight_ref, gx_in, x_ref, middle_ref,
    mod_ref, query_sum, keep_ref, send_ref, stay_ref, odd_ref, even_ref, notes_ref, total,
    grads,
):
    piece = stay_ref.shape[1]
    rows, width = x_ref.shape
    half = keep_ref.shape[0]
    block = rows // blocks
    step = pl.program_id(0)
    turned = lambda ref: ref[...].reshape(half, rows)
    grads[...] = (own_ref[...].astype(F32) + got_ref[...].astype(F32)).astype(BF16)
    keep_ref[...] = contract(turned(one_keep), grads[...], 1, 0).astype(BF16)
    send_ref[...] = contract(turned(one_send), grads[...], 1, 0).astype(BF16)

    @pl.when(step == 0)
    def _():
        total[...] = gx_in[...] + contract(grads[...], weight_ref[...], 1, 1)

    @pl.when(step == 1)
    def _():
        notes = []
        for s in range(blocks):
            part = slice(s * block, (s + 1) * block)
            grad = total[part] + contract(grads[part], weight_ref[...], 1, 1)
            normed, inverse = norm_parts(x_ref[part].astype(F32))
            notes.append(jnp.sum(grad, 0, keepdims=True))
            notes.append(jnp.sum(grad * normed, 0, keepdims=True))
            back = norm_back(grad, normed, inverse, mod_row(mod_ref, s, 1, width))
            low = (middle_ref[part] + back).astype(BF16)
            for k in range(block // piece):
                leaving(k, s, low[k * piece : (k + 1) * piece], stay_ref, odd_ref, even_ref)
        notes.append(query_sum[...])
        notes.append(jnp.sum(grads[...].astype(F32), 0, keepdims=True))
        notes.append(jnp.zeros((NOTES - 2 * blocks - 2, width), F32))
        notes_ref[...] = jnp.concatenate(notes, 0).astype(BF16)


def leave(
    core, one_turned, own, got, weight, gx, x, grad_middle, mod, query_sum, blocks, piece, after=()
):
    rows, width = x.shape
    half = width // 2
    const = lambda shape: pl.BlockSpec(shape, lambda i, c: (0,) * len(shape))
    once = lambda shape: pl.BlockSpec(
        shape, lambda i, c: (0,) * len(shape), pipeline_mode=pl.Buffered(1)
    )
    shapes = leaving_shapes(blocks, piece, width)
    return launch(
        functools.partial(leave_kernel, blocks),
        [like(BF16, half, 2 * width), like(BF16, half, 2 * width)] + shapes,
        prefetch=1,
        grid=(2,),
        in_specs=turned_specs(one_turned)
        + [
            pl.BlockSpec((rows, width), lambda i, c: (0, i)),
            pl.BlockSpec((rows, width), lambda i, c: (0, i)),
            pl.BlockSpec((width, width), lambda i, c: (0, 1 + i)),
            once((rows, width)),
            once((rows, width)),
            once((rows, width)),
            once((8, 2 * width)),
            once((1, width)),
        ],
        out_specs=[
            pl.BlockSpec((half, width), lambda i, c: (0, i)),
            pl.BlockSpec((half, width), lambda i, c: (0, i)),
        ]
        + [const(s.shape) for s in shapes],
        scratch=[pltpu.VMEM((rows, width), F32), pltpu.VMEM((rows, width), BF16)],
        after=after,
        micros=500,
        name="leave",
    )(core, one_turned, one_turned, own, got, weight, gx, x, grad_middle, mod, query_sum)


def head_columns(ref, start, head_width):
    part = ref[:, start : start + head_width]
    return jnp.concatenate(
        [part, jnp.zeros((part.shape[0], LANES - head_width), part.dtype)], axis=1
    )


def kept_heads(list_ref, blocks, heads, index, one, together):
    count = list_ref[blocks * heads + index]

    def body(i, carry):
        one([list_ref[index * heads + i * together + u] for u in range(together)])
        return carry

    lax.fori_loop(0, (count + together - 1) // together, body, 0)


def masked_heads(keep_ref, blocks, heads, block, blank):
    for index in range(blocks):

        def body(h, carry):
            @pl.when(keep_ref[index * heads + h] == 0)
            def _():
                blank(h, pl.ds(index * block, block))

            return carry

        lax.fori_loop(0, heads, body, 0)


def attend_kernel(
    heads, head_width, blocks, long_ref, keep_ref, list_ref, q_ref, own_ref, other_ref, out_ref,
    lse_ref, qh, kh, vh, oh,
):
    rows, width = q_ref.shape
    block = rows // blocks
    factor = head_width**-0.5 * LOG2E
    is_long = long_ref[0] == 1
    for h in range(heads):
        start = h * head_width
        qh[h] = head_columns(q_ref, start, head_width)
        kh[h, :rows] = head_columns(own_ref, start, head_width)
        vh[h, :rows] = head_columns(own_ref, width + start, head_width)

    @pl.when(is_long)
    def _():
        for h in range(heads):
            start = h * head_width
            kh[h, rows:] = head_columns(other_ref, start, head_width)
            vh[h, rows:] = head_columns(other_ref, width + start, head_width)

    def blank(h, part):
        oh[h, part, :] = jnp.zeros((block, LANES), BF16)

    masked_heads(keep_ref, blocks, heads, block, blank)

    def loop(index, together, first, count, key_first, key_count):
        def one(group):
            part, keys_part = pl.ds(first, count), pl.ds(key_first, key_count)
            scores = [contract(kh[h, keys_part, :], qh[h, part, :], 1, 1) for h in group]
            tops = [jnp.max(x, 0, keepdims=True) for x in scores]
            exponents = [jnp.exp2((x - top) * factor) for x, top in zip(scores, tops)]
            totals = [jnp.sum(x, 0, keepdims=True) for x in exponents]
            for h, exponent, top, total in zip(group, exponents, tops, totals):
                mixed = contract(vh[h, keys_part, :], exponent.astype(BF16), 0, 0) * (1.0 / total)
                oh[h, part, :] = mixed.T.astype(BF16)
                lse_ref[pl.ds(h, 1), part] = top * factor + jnp.log2(total)

        kept_heads(list_ref, blocks, heads, index, one, together)

    @pl.when(is_long)
    def _():
        loop(0, LONG_HEADS, 0, rows, 0, 2 * rows)

    @pl.when(jnp.logical_not(is_long))
    def _():
        for index in range(blocks):
            loop(index, SHORT_HEADS, index * block, block, index * block, block)

    for h in range(heads):
        out_ref[:, h * head_width : (h + 1) * head_width] = oh[h, :, :head_width]


def attend(queries, own, other, long_flag, keep, kept, blocks):
    rows, width = queries.shape
    heads = keep.shape[0] // blocks
    head_width = width // heads
    vmem = pl.BlockSpec(memory_space=pltpu.VMEM)
    smem = pl.BlockSpec(memory_space=pltpu.SMEM)
    return pl.pallas_call(
        functools.partial(attend_kernel, heads, head_width, blocks),
        in_specs=[smem, smem, smem, vmem, vmem, vmem],
        out_specs=[vmem, vmem],
        out_shape=[
            jax.ShapeDtypeStruct((rows, width), BF16),
            jax.ShapeDtypeStruct((heads, rows), F32),
        ],
        scratch_shapes=[
            pltpu.VMEM((heads, rows, LANES), BF16),
            pltpu.VMEM((heads, 2 * rows, LANES), BF16),
            pltpu.VMEM((heads, 2 * rows, LANES), BF16),
            pltpu.VMEM((heads, rows, LANES), BF16),
        ],
        compiler_params=pltpu.CompilerParams(vmem_limit_bytes=56 * 1024 * 1024),
        cost_estimate=pl.CostEstimate(
            flops=100 * rows * rows * width,
            bytes_accessed=12 * rows * width,
            transcendentals=2 * rows * rows * heads,
        ),
        name="attend",
    )(long_flag, keep, kept, queries, own, other)


def attend_back_kernel(
    heads, head_width, blocks, long_ref, keep_ref, list_ref, q_ref, own_ref, other_ref, go_ref,
    lse_ref, delta_ref, gq_ref, gown_ref, gother_ref, qh, kh, vh, gh, gqh, gkh, gvh,
):
    rows, width = q_ref.shape
    block = rows // blocks
    scale = head_width**-0.5
    factor = scale * LOG2E
    is_long = long_ref[0] == 1
    for h in range(heads):
        start = h * head_width
        qh[h] = head_columns(q_ref, start, head_width)
        gh[h] = head_columns(go_ref, start, head_width)
        kh[h, :rows] = head_columns(own_ref, start, head_width)
        vh[h, :rows] = head_columns(own_ref, width + start, head_width)

    @pl.when(is_long)
    def _():
        for h in range(heads):
            start = h * head_width
            kh[h, rows:] = head_columns(other_ref, start, head_width)
            vh[h, rows:] = head_columns(other_ref, width + start, head_width)

    def blank(h, part):
        for ref in (gqh, gkh, gvh):
            ref[h, part, :] = jnp.zeros((block, LANES), BF16)

    masked_heads(keep_ref, blocks, heads, block, blank)

    def loop(index, together, first, count, key_first, key_count):
        def one(group):
            part, keys_part = pl.ds(first, count), pl.ds(key_first, key_count)
            scores = [contract(kh[h, keys_part, :], qh[h, part, :], 1, 1) for h in group]
            grads = [contract(vh[h, keys_part, :], gh[h, part, :], 1, 1) for h in group]
            probs = [
                jnp.exp2(x * factor - lse_ref[pl.ds(h, 1), part]) for h, x in zip(group, scores)
            ]
            slopes = [
                (p * (g - delta_ref[pl.ds(h, 1), part])).astype(BF16)
                for h, p, g in zip(group, probs, grads)
            ]
            for h, p, slope in zip(group, probs, slopes):
                gvh[h, keys_part, :] = contract(p.astype(BF16), gh[h, part, :], 1, 0).astype(BF16)
                gkh[h, keys_part, :] = (contract(slope, qh[h, part, :], 1, 0) * scale).astype(BF16)
                gqh[h, part, :] = ((contract(kh[h, keys_part, :], slope, 0, 0) * scale).T).astype(BF16)

        kept_heads(list_ref, blocks, heads, index, one, together)

    @pl.when(is_long)
    def _():
        def blank_other(h, part):
            for ref in (gkh, gvh):
                ref[h, pl.ds(rows + part.start, block), :] = jnp.zeros((block, LANES), BF16)

        masked_heads(keep_ref, blocks, heads, block, blank_other)
        loop(0, LONG_BACK, 0, rows, 0, 2 * rows)

    @pl.when(jnp.logical_not(is_long))
    def _():
        for index in range(blocks):
            loop(index, SHORT_HEADS, index * block, block, index * block, block)
        gother_ref[...] = jnp.zeros_like(gother_ref)

    for h in range(heads):
        start = h * head_width
        gq_ref[:, start : start + head_width] = gqh[h, :, :head_width]
        gown_ref[:, start : start + head_width] = gkh[h, :rows, :head_width]
        gown_ref[:, width + start : width + start + head_width] = gvh[h, :rows, :head_width]

    @pl.when(is_long)
    def _():
        for h in range(heads):
            start = h * head_width
            gother_ref[:, start : start + head_width] = gkh[h, rows:, :head_width]
            gother_ref[:, width + start : width + start + head_width] = gvh[h, rows:, :head_width]


def attend_back(
    queries, own, other, grad_out, lse, delta, long_flag, keep, kept, blocks, after=()
):
    rows, width = queries.shape
    heads = keep.shape[0] // blocks
    head_width = width // heads
    short = pltpu.VMEM((heads, rows, LANES), BF16)
    full = pltpu.VMEM((heads, 2 * rows, LANES), BF16)
    return launch(
        functools.partial(attend_back_kernel, heads, head_width, blocks),
        [like(BF16, rows, width), like(BF16, rows, 2 * width), like(BF16, rows, 2 * width)],
        in_specs=smem_specs(3) + vmem_specs(6),
        out_specs=vmem_specs(3),
        scratch=[short, full, full, short, short, full, full],
        after=after,
        vmem=60,
        micros=500,
        name="attend_back",
    )(long_flag, keep, kept, queries, own, other, grad_out, lse, delta)


def feed_kernel(
    blocks, sub, group, first, resume, core_ref, keep_ref, x_ref, g_ref, xk_ref, xs_ref, bias_ref,
    wi_ref, wo_ref, *refs,
):
    act, gbefore = refs[-2:]
    out_ref, gx_ref, act_ref, wik_ref, wis_ref, gbias_ref = refs[-8:-2]
    rows, _ = x_ref.shape
    block = rows // blocks
    chunk = wi_ref.shape[1]
    half = wik_ref.shape[0]
    step = pl.program_id(0)
    groups = keep_ref.shape[0] // blocks
    turned = lambda ref: ref[...].reshape(half, rows)
    for lo in range(0, chunk, sub):
        cols = slice(lo, lo + sub)
        column_sum = jnp.zeros((1, sub), F32)
        for index in range(blocks):
            part = slice(index * block, (index + 1) * block)
            before = contract(x_ref[part], wi_ref[:, cols], 1, 0) + bias_ref[:, cols]
            grad_act = contract(g_ref[part], wo_ref[cols, :], 1, 1)
            base = index * groups + ((first + step) * chunk + lo) // group
            keep = jnp.concatenate(
                [
                    jnp.full((1, group), keep_ref[base + m].astype(F32))
                    for m in range(sub // group)
                ],
                axis=1,
            )
            square = before * before
            bend = jnp.tanh(GELU_A * before * (1.0 + GELU_B * square))
            gate = 0.5 * (1.0 + bend)
            slope = gate + (0.5 * GELU_A) * before * (1.0 - bend * bend) * (
                1.0 + (3.0 * GELU_B) * square
            )
            act[part, cols] = (before * gate * keep).astype(BF16)
            grad = (grad_act * keep * slope).astype(BF16)
            gbefore[part, cols] = grad
            column_sum += jnp.sum(grad.astype(F32), 0, keepdims=True)
        gbias_ref[:, cols] = column_sum
    out = contract(act[...], wo_ref[...], 1, 0)
    gx = contract(gbefore[...], wi_ref[...], 1, 1)

    @pl.when(step == 0)
    def _():
        if resume:
            out_ref[...] = refs[0][...] + out
            gx_ref[...] = refs[1][...] + gx
        else:
            out_ref[...] = out
            gx_ref[...] = gx

    @pl.when(step != 0)
    def _():
        out_ref[...] += out
        gx_ref[...] += gx

    act_ref[...] = act[...]
    wik_ref[...] = contract(turned(xk_ref), gbefore[...], 1, 0).astype(BF16)
    wis_ref[...] = contract(turned(xs_ref), gbefore[...], 1, 0).astype(BF16)


def feed(core, keep, x, grad, turned, bias, wi, wo, blocks, chunk, sub, first, count, before=()):
    rows, width = x.shape
    hidden = wi.shape[1]
    half = width // 2
    group = hidden * blocks // keep.shape[0]
    single = pl.Buffered(1)
    once = lambda shape: pl.BlockSpec(shape, lambda i, *c: (0, 0), pipeline_mode=single)
    tpairs, _, tshare, _ = turned.shape
    spec = lambda lead: pl.BlockSpec((tpairs, None, tshare, rows), lead, pipeline_mode=single)
    return launch(
        functools.partial(feed_kernel, blocks, sub, group, first, bool(before)),
        [
            like(F32, rows, width),
            like(F32, rows, width),
            like(BF16, rows, count * chunk),
            like(BF16, half, count * chunk),
            like(BF16, half, count * chunk),
            like(F32, 1, count * chunk),
        ],
        prefetch=2,
        grid=(count,),
        in_specs=[
            once((rows, width)),
            once((rows, width)),
            spec(lambda i, c, k: (0, c[0], 0, 0)),
            spec(lambda i, c, k: (0, 1 - c[0], 0, 0)),
            pl.BlockSpec((1, chunk), lambda i, *c: (0, first + i)),
            pl.BlockSpec((width, chunk), lambda i, *c: (0, first + i)),
            pl.BlockSpec((chunk, width), lambda i, *c: (first + i, 0)),
        ]
        + [once((rows, width))] * len(before),
        out_specs=[
            pl.BlockSpec((rows, width), lambda i, *c: (0, 0)),
            pl.BlockSpec((rows, width), lambda i, *c: (0, 0)),
            pl.BlockSpec((rows, chunk), lambda i, *c: (0, i)),
            pl.BlockSpec((half, chunk), lambda i, *c: (0, i)),
            pl.BlockSpec((half, chunk), lambda i, *c: (0, i)),
            pl.BlockSpec((1, chunk), lambda i, *c: (0, i)),
        ],
        scratch=[pltpu.VMEM((rows, chunk), BF16), pltpu.VMEM((rows, chunk), BF16)],
        vmem=FEED_VMEM,
        micros=0,
        name="feed",
    )(core, keep, x, grad, turned, turned, bias, wi, wo, *before)


def outer_kernel(share, starts, core_ref, *refs):
    acts = refs[: len(starts)]
    g_ref = refs[len(starts)]
    keep_ref, send_ref = refs[-2:]
    core = core_ref[0]
    step = pl.program_id(0)
    for act_ref, (lo, hi) in zip(acts, starts):

        @pl.when((step >= lo) & (step < hi))
        def _():
            grad = contract(act_ref[...], g_ref[...], 0, 0).astype(BF16)
            for pair in range(keep_ref.shape[0]):
                even = grad[2 * pair * share : (2 * pair + 1) * share]
                odd = grad[(2 * pair + 1) * share : (2 * pair + 2) * share]

                @pl.when(core == 0)
                def _():
                    keep_ref[pair] = even
                    send_ref[pair] = odd

                @pl.when(core != 0)
                def _():
                    keep_ref[pair] = odd
                    send_ref[pair] = even


def outer_part(core, acts, grad, share, chunk, after=()):
    rows, width = grad.shape
    pairs = chunk // (2 * share)
    specs, starts, at = [], [], 0
    for act in acts:
        count = act.shape[1] // chunk
        starts.append((at, at + count))
        specs.append(
            pl.BlockSpec(
                (rows, chunk), lambda i, lo=at, n=count: (0, jnp.clip(i - lo, 0, n - 1))
            )
        )
        at += count
    return launch(
        functools.partial(outer_kernel, share, starts),
        [like(BF16, at * pairs, share, width)] * 2,
        grid=(at,),
        in_specs=smem_specs(1) + specs + [pl.BlockSpec((rows, width), lambda i: (0, 0))],
        out_specs=[pl.BlockSpec((pairs, share, width), lambda i: (i, 0, 0))] * 2,
        after=after,
        micros=0,
        name="outer_part",
    )(core, *acts, grad)


def split_bit(array, dim, bit):
    keep = lax.dynamic_index_in_dim(array, bit, dim, keepdims=False)
    send = lax.dynamic_index_in_dim(array, 1 - bit, dim, keepdims=False)
    return keep, send


def split_kernel(units, place_ref, *refs):
    outs = refs[-4:]
    at = 0
    for member, count in enumerate(units):
        ins = refs[8 * member : 8 * member + 8]
        for m, out in enumerate(outs):
            left, right = ins[2 * m], ins[2 * m + 1]
            total = (left[0].astype(F32) + right[0].astype(F32)).astype(BF16)
            if count == 1 and len(total.shape) == 2:
                out[0, at] = total
            else:
                out[0, at : at + count] = total
        at += count


def split_call(
    place, arrays, blocks, spots, units, tail, count, low_bit, high_bit, after, name, micros=0
):
    low = lambda p: (p[2] >> low_bit) & 1
    high = lambda p: (p[2] >> high_bit) & 1
    leads = [
        lambda j, p: j * 2 + low(p),
        lambda j, p: j * 2 + 1 - low(p),
        lambda j, p: high(p) * count + j,
        lambda j, p: (1 - high(p)) * count + j,
    ]
    specs = []
    for block, spot in zip(blocks, spots):
        for m, lead in enumerate(leads):
            index = lambda j, p, lead=lead, spot=spot[m // 2]: (lead(j, p),) + spot
            specs += [pl.BlockSpec((1,) + block, index)] * 2
    shape = (sum(units),) + tail
    return launch(
        functools.partial(split_kernel, units),
        [like(BF16, count, *shape)] * 4,
        prefetch=1,
        grid=(count,),
        in_specs=specs,
        out_specs=[pl.BlockSpec((1,) + shape, lambda j, p: (j, 0, 0, 0))] * 4,
        after=after,
        micros=micros,
        name=name,
    )(place, *arrays)


def cross_kernel(kinds, share, place_ref, *refs):
    keep_ref, send_ref = refs[-2:]
    bit = place_ref[1] & 1

    def write(out_ref, low):
        rows = [[], []]
        for n, members in enumerate(kinds):
            am, ag, bm, bg = refs[4 * n : 4 * n + 4]
            at = 0
            for by_rows in members:
                if by_rows:
                    for high, (m, g) in enumerate(((am, ag), (bm, bg))):
                        rows[high].append(m[0, at + low].astype(F32) + g[0, at + low].astype(F32))
                    at += 2
                else:
                    for m, g in ((am, ag), (bm, bg)):
                        total = m[0, at].astype(F32) + g[0, at].astype(F32)
                        for high in range(2):
                            first = (2 * high + low) * share
                            rows[high].append(total[first : first + share])
                    at += 1
        for high in range(2):
            count = sum(part.shape[0] for part in rows[high])
            if out_ref.shape[1] > count:
                blank = jnp.zeros((out_ref.shape[1] - count, out_ref.shape[2]), F32)
                rows[high].append(blank)
            out_ref[high] = jnp.concatenate(rows[high], 0).astype(BF16)

    @pl.when(bit == 0)
    def _():
        write(keep_ref, 0)
        write(send_ref, 1)

    @pl.when(bit == 1)
    def _():
        write(keep_ref, 1)
        write(send_ref, 0)


def last_kernel(place_ref, mine_ref, got_ref, *refs):
    keep_ref, send_ref = refs[-2:]
    bit = place_ref[1] >> 1
    add = lambda i: (mine_ref[i].astype(F32) + got_ref[i].astype(F32)).astype(BF16)
    keep_ref[...] = add(bit)
    send_ref[...] = add(1 - bit)


def total_kernel(mine_ref, got_ref, out_ref):
    out_ref[...] = mine_ref[...].astype(F32) + got_ref[...].astype(F32)


def small_call(body, place, arrays, shape, after, name, micros=0):
    return launch(
        body,
        [shape, shape],
        in_specs=smem_specs(1) + vmem_specs(len(arrays)),
        out_specs=vmem_specs(2),
        after=after,
        vmem=24,
        micros=micros,
        name=name,
    )(place, *arrays)


class Package:
    def __init__(self, place, *members):
        self.place = place
        self.keeps = [keep for keep, _ in members]
        self.flight = [swap(send, "bucket", 1) for _, send in members]
        self.kinds = [keep.ndim == 4 for keep in self.keeps]

    def first(self, *after):
        pairs = self.keeps[0].shape[0]
        self.bits = pairs.bit_length() - 1
        self.count = pairs // 2
        self.turn = 0
        arrays, blocks, spots, units = [], [], [], []
        for keep, got, by_rows in zip(self.keeps, self.flight, self.kinds):
            arrays += [keep, got] * 4
            if by_rows:
                blocks.append((2,) + keep.shape[2:])
                spots.append([(0, 0, 0), (1, 0, 0)])
                units.append(2)
                tail = keep.shape[2:]
            else:
                tail = (keep.shape[1], keep.shape[2] // 2)
                blocks.append(tail)
                spots.append([(0, 0), (0, 1)])
                units.append(1)
        self.unit_count, self.tail = sum(units), tail
        return self.depart(arrays, blocks, spots, units, after, "sum_first")

    def depart(self, arrays, blocks, spots, units, after, name, micros=0):
        low_bit, high_bit = 1 + self.turn, self.bits - self.turn
        (a_keep, a_send, b_keep, b_send), self.done = split_call(
            self.place, arrays, blocks, spots, units, self.tail, self.count, low_bit, high_bit,
            after, name, micros,
        )
        self.mine = [a_keep, b_keep]
        self.flight = [swap(a_send, "bucket", 1 << low_bit), swap(b_send, "bucket", 1 << high_bit)]
        self.turn += 1
        self.count //= 2
        return self.done

    def second(self, *after, micros=0):
        while self.turn < self.bits:
            (am, bm), (ag, bg) = self.mine, self.flight
            spots = [[(0, 0, 0), (0, 0, 0)]]
            block = (self.unit_count,) + self.tail
            arrays = [am, ag, am, ag, bm, bg, bm, bg]
            self.depart(
                arrays, [block], spots, [self.unit_count], after, "sum_second", micros
            )
        return self.done


class Cross:
    def __init__(self, packages, *after, micros=0):
        self.place = packages[0].place
        self.kinds = [p.kinds for p in packages]
        unit, width = packages[0].tail
        self.tiles = sum(4 if by_rows else 2 for kinds in self.kinds for by_rows in kinds)
        self.tail = (unit // 4, width)
        arrays = []
        for p in packages:
            arrays += [p.mine[0], p.flight[0], p.mine[1], p.flight[1]]
        self.rows = -(-self.tiles * self.tail[0] // 16) * 16
        shape = like(BF16, 2, self.rows, width)
        (self.mine, send), self.done = small_call(
            functools.partial(cross_kernel, self.kinds, self.tail[0]), self.place, arrays, shape, after, "cross",
            micros,
        )
        self.flight = swap(send, "seq", 1)

    def last(self, *after):
        shape = like(BF16, self.rows, self.tail[1])
        (self.mine, send), self.done = small_call(
            last_kernel, self.place, [self.mine, self.flight], shape, after, "last"
        )
        self.flight = swap(send, "seq", 2)
        return self.done

    def total(self, *after):
        return launch(
            total_kernel,
            [like(F32, *self.mine.shape)],
            in_specs=vmem_specs(2),
            out_specs=vmem_specs(1),
            after=after,
            vmem=24,
            name="total",
        )(self.mine, self.flight)

    def results(self, total):
        out, at = [], 0
        share = self.tail[0]
        for kinds in self.kinds:
            for by_rows in kinds:
                if by_rows:
                    out.append(total[at : at + 4 * share])
                    at += 4 * share
                else:
                    sides = [total[at : at + share], total[at + share : at + 2 * share]]
                    out.append(jnp.concatenate(sides, 1))
                    at += 2 * share
        return out


def notes_kernel(blocks, early_ref, late_ref, early_cond, late_cond, out_ref, early_sum, late_sum):
    width = early_ref.shape[1]
    for part in range(6):
        if part < 2:
            ref, cond, count, which = late_ref, late_cond, 2, part
        else:
            ref, cond, count, which = early_ref, early_cond, 4, part - 2
        inside = lax.broadcasted_iota(jnp.int32, cond.shape, 0) % ref_pitch(ref, early_ref, late_ref)
        mine = (inside % count == which) & (inside < count * blocks)
        picked = jnp.where(mine, cond[...].astype(F32), 0.0).astype(BF16)
        out_ref[:, part * width : (part + 1) * width] = contract(picked, ref[...], 0, 0)
    for ref, total in ((early_ref, early_sum), (late_ref, late_sum)):
        pitch = ref_pitch(ref, early_ref, late_ref)
        shape = (NOTES, ref.shape[0])
        kind = lax.broadcasted_iota(jnp.int32, shape, 0)
        row = lax.broadcasted_iota(jnp.int32, shape, 1) % pitch
        total[...] = contract(jnp.where(kind == row, 1.0, 0.0).astype(BF16), ref[...], 1, 0)


def ref_pitch(ref, early_ref, late_ref):
    return NOTES if ref is early_ref else NOTES * late_ref.shape[0] // early_ref.shape[0]


def notes_part(early, late, early_cond, late_cond, blocks):
    width = early.shape[1]
    return launch(
        functools.partial(notes_kernel, blocks),
        [
            like(F32, early_cond.shape[1], 6 * width),
            like(F32, NOTES, width),
            like(F32, NOTES, width),
        ],
        in_specs=vmem_specs(4),
        out_specs=vmem_specs(3),
        vmem=32,
        name="notes_part",
    )(early, late, early_cond, late_cond)


def on_device(
    tokens,
    segment,
    keep_route,
    condition,
    group_bucket,
    head_mask,
    channel_mask,
    ada_weight,
    ada_bias,
    qkv_weight,
    query_bias,
    value_bias,
    proj_weight,
    proj_bias,
    inner_weight,
    inner_bias,
    outer_weight,
    outer_bias,
    cotangent,
):
    rows, width = tokens.shape
    slots = condition.shape[0]
    hidden = inner_weight.shape[1]
    group_count = lax.axis_size("bucket")
    seq_count = lax.axis_size("seq")
    bucket = lax.axis_index("bucket")
    seq = lax.axis_index("seq")
    core = bucket % 2
    piece = rows // slots
    block = piece * seq_count
    blocks = rows // block
    place = jnp.stack([core, seq, bucket]).astype(jnp.int32)
    row_share = width // group_count
    aligned = row_share % 16 == 0

    def turned(array):
        split = array.reshape(group_count // 2, 2, row_share, rows)
        if aligned:
            return split
        keep, send = split_bit(split, 1, core)
        return jnp.stack([keep, send]).reshape(1, 2, width // 2, rows)

    turned_core = place[:1] if aligned else jnp.zeros((1,), jnp.int32)

    seg_other = swap(segment, "bucket", 1)
    bucket_other = swap(group_bucket, "bucket", 1)
    tokens_own = tokens.reshape(slots, piece, width)
    tokens_other = swap(tokens_own, "bucket", 1)
    cond_other = swap(condition, "bucket", 1)
    route_columns = jnp.broadcast_to(keep_route.astype(BF16)[:, None], (rows, LANES))
    payload = jnp.concatenate([cotangent, route_columns], 1).reshape(slots, piece, width + LANES)

    (
        send_which, send_index, back_which, back_index, cond_which, cond_row, flags, keep_heads,
        keep_channels, kept,
    ) = make_plan(
        place, segment, seg_other, group_bucket, bucket_other, head_mask, channel_mask, slots,
        piece, seq_count, blocks,
    )

    def bring(pieces):
        return [pieces[0]] + [swap(pieces[k], "seq", k) for k in range(1, seq_count)]

    x_sent, x_mark = send_blocks(tokens_own, tokens_other, send_which, send_index, seq_count, blocks)
    x_parts = bring(x_sent)
    payload = hold(payload, x_mark)
    payload_other = swap(payload, "bucket", 1)
    mod, cond_act = modulate(
        cond_which, cond_row, condition, cond_other, ada_weight, ada_bias, blocks, width,
        (payload_other,),
    )
    payload_sent, _ = send_blocks(
        payload, payload_other, send_which, send_index, seq_count, blocks, (x_parts[3],)
    )
    payload_parts = bring(payload_sent)
    pair_bias = jnp.concatenate([jnp.zeros_like(value_bias), value_bias])[None, :]
    x, normed_one, one_turned, own_kv = enter(x_parts, mod, qkv_weight, pair_bias, blocks)
    other_kv = swap(own_kv, "bucket", 1)
    queries = linear(normed_one, qkv_weight, query_bias, width, width // 3)
    attended, lse = attend(queries, own_kv, other_kv, flags, keep_heads, kept, blocks)
    branch_one, middle, normed_two, two_turned, att_turned, grad_branch_two, grad_outer_bias = (
        middle_part(payload_parts, attended, proj_weight, proj_bias, x, mod, blocks)
    )

    share = hidden // group_count
    by_rows = (group_count // 2, row_share, -1)
    chunk = 2 * width // 3
    feed_args = (
        turned_core, keep_channels, normed_two, grad_branch_two, turned(two_turned),
        inner_bias[None, :], inner_weight, outer_weight, blocks, chunk, FEED_SUB,
    )
    (branch_two, grad_two, act_a, wi_keep, wi_send, hidden_a), _ = feed(*feed_args, 0, 3)
    inner = Package(place, (wi_keep.reshape(by_rows), wi_send.reshape(by_rows)))
    (branch_two, grad_two, act_b, wi_keep, wi_send, hidden_b), mark = feed(
        *feed_args, 3, 3, (branch_two, grad_two)
    )
    mark = inner.first(mark)
    (wo_keep, wo_send), mark = outer_part(
        place[:1], [act_a, act_b], grad_branch_two, share, width, (mark,)
    )
    by_units = (group_count // 2, 4, share // 4, width)
    rest = Package(
        place,
        (wi_keep.reshape(by_rows), wi_send.reshape(by_rows)),
        (wo_keep.reshape(by_units), wo_send.reshape(by_units)),
    )
    (out_stay, out_odd, out_even, early, grad_middle, grad_branch_one, grad_attended, delta), mark = (
        turn_part(
            payload_parts, keep_heads, branch_two, grad_two, middle, branch_one, attended, mod,
            outer_bias, proj_weight, cond_act, (grad_outer_bias, hidden_a, hidden_b), blocks,
            (mark,),
        )
    )
    mark = inner.second(mark)
    mark = rest.first(mark)
    out_near = swap(out_odd, "seq", 1)
    early_all = lax.all_gather(early, ("bucket", "seq"), axis=0, tiled=True)

    (grad_queries, grad_own, grad_other), mark = attend_back(
        queries, own_kv, other_kv, grad_attended, lse, delta, flags, keep_heads, kept, blocks,
        (mark,),
    )
    grad_got = swap(grad_other, "bucket", 1)
    out_relay, mark = relay(out_even, out_near, (mark,))
    out_far = swap(out_relay, "seq", 2)
    inner_cross = Cross([inner], mark)
    (pq_keep, pq_send, grad_one_part, query_sum), mark = query_back(
        turned_core, turned(att_turned), turned(one_turned), grad_branch_one, grad_queries,
        qkv_weight, (inner_cross.done,),
    )
    mark = rest.second(mark, micros=500)
    mark = inner_cross.last(mark)
    out_own, mark = collect(out_stay, out_near, out_far, (mark,))
    out_other = swap(out_own, "bucket", 1)
    (kv_keep, kv_send, x_stay, x_odd, x_even, late), mark = leave(
        turned_core, turned(one_turned), grad_own, grad_got, qkv_weight, grad_one_part, x,
        grad_middle, mod, query_sum, blocks, piece, (mark,),
    )
    projections = Package(
        place,
        (pq_keep.reshape(by_rows), pq_send.reshape(by_rows)),
        (kv_keep.reshape(by_rows), kv_send.reshape(by_rows)),
    )
    x_near = swap(x_odd, "seq", 1)
    late_all = lax.all_gather(late, ("bucket", "seq"), axis=0, tiled=True)

    (inner_sum,), mark = inner_cross.total(mark)
    rest_cross = Cross([rest], mark, micros=500)
    mark = projections.first(rest_cross.done)
    x_relay, mark = relay(x_even, x_near, (mark,), 500)
    x_far = swap(x_relay, "seq", 2)
    mark = rest_cross.last(mark)
    block_out, mark = pick_blocks(
        out_own, out_other, back_which, back_index, BF16, (mark,), 500
    )
    mark = projections.second(mark)
    x_own, mark = collect(x_stay, x_near, x_far, (mark,))
    x_other = swap(x_own, "bucket", 1)
    projections_cross = Cross([projections], mark)
    (rest_sum,), mark = rest_cross.total(projections_cross.done)
    grad_tokens, mark = pick_blocks(x_own, x_other, back_which, back_index, F32, (mark,))
    mark = projections_cross.last(mark)
    (projections_sum,), mark = projections_cross.total(mark)
    block_out = block_out.reshape(rows, width)
    grad_tokens = grad_tokens.reshape(rows, width)
    (inner_a,) = inner_cross.results(inner_sum)
    inner_b, grad_outer_weight = rest_cross.results(rest_sum)
    grad_inner_weight = jnp.concatenate([inner_a, inner_b], 1)
    proj_query, key_value = projections_cross.results(projections_sum)
    grad_proj_weight = proj_query[:, :width]
    grad_qkv_weight = jnp.concatenate([proj_query[:, width:], key_value], 1)

    early_all = hold(early_all, projections_cross.done)
    late_all = hold(late_all, projections_cross.done)
    spot = bucket * seq_count + seq
    device_count = group_count * seq_count
    columns = width // device_count
    cond_mine = lax.dynamic_slice_in_dim(early_all, spot * columns, columns, 1)
    cond_mine = cond_mine.reshape(device_count, NOTES, columns)[:, NOTES - blocks :]

    def at_rows(parts, pitch):
        spread = jnp.broadcast_to(
            cond_mine[:, :, None, :], (device_count, blocks, parts, columns)
        ).reshape(device_count, blocks * parts, columns)
        rest = jnp.zeros((device_count, pitch - blocks * parts, columns), BF16)
        return jnp.concatenate([spread, rest], 1).reshape(device_count * pitch, columns)

    (grad_ada_weight, early_sum, late_sum), _ = notes_part(
        early_all, late_all, at_rows(4, NOTES), at_rows(2, NOTES), blocks
    )

    def own_part(array):
        array = array.reshape(-1)
        size = array.shape[0] // device_count
        return lax.dynamic_slice_in_dim(array, spot * size, size, 0)

    ada_rows = jnp.concatenate(
        [
            sum(late_sum[2 * s : 2 * s + 2] for s in range(blocks)),
            sum(early_sum[4 * s : 4 * s + 4] for s in range(blocks)),
        ],
        0,
    )
    at = 4 * blocks
    return (
        block_out,
        grad_tokens,
        grad_ada_weight,
        own_part(ada_rows),
        grad_qkv_weight,
        own_part(late_sum[2 * blocks]),
        own_part(late_sum[2 * blocks + 1]),
        grad_proj_weight,
        own_part(early_sum[at]),
        grad_inner_weight,
        own_part(early_sum[at + 2 : at + 6]),
        grad_outer_weight,
        own_part(early_sum[at + 1]),
    )


def solution(mesh):
    split = P(("bucket", "seq"))
    split_rows = P(("bucket", "seq"), None)
    return jax.shard_map(
        on_device,
        mesh=mesh,
        in_specs=(split_rows, split, split, P("bucket", None), P("bucket"))
        + (P(),) * 13
        + (split_rows,),
        out_specs=(
            split_rows,
            split_rows,
            split_rows,
            split,
            split_rows,
            split,
            split,
            split_rows,
            split,
            split_rows,
            split,
            split_rows,
            split,
        ),
        check_vma=False,
    )
```
